512 devices in a mesh: batch: 32 (over y, x, core), feat: 16 (over z).
Axes of the slice: x: 4, y: 4, z: 16, core: 2. Of those that a mesh axis runs over, the one named last changes fastest.
Arguments:
- embeds: bfloat16 [2048, 2, 8192], P('batch'), may hold values from -64 to 64
- weight: bfloat16 [8192, 8192], P('batch', 'feat'), may hold values from -0.0625 to 0.0625
Outputs:
- loss_value: float32 [], replicated
- grad_weight: float32 [8192, 8192], P('batch', 'feat')
The draws below stay inside these ranges and needn't reach their ends.
All inputs are finite; a program needn't handle non-finite values.
Results may differ from the reference program's by a relative error of at most 0.00485.
Values may be sent and summed in bfloat16 or wider, within the bound.
No kernel may reach another device: no remote copies, remote signals or barrier semaphores. Data moves between devices by JAX's collectives and lax.ppermute only.
A program may use at most 64 MiB of HBM per device.

```python
import jax
import jax.numpy as jnp
from jax import lax

D_IN = 8192
D_OUT = 8192
ROWS = 2048


def draw_embeds(key, part):
    key = jax.random.fold_in(key, 7)
    keys = jax.random.split(key, 4)
    position = jnp.arange(ROWS, dtype=jnp.float32).reshape(ROWS, 1) / max(ROWS - 1, 1)
    shared = jax.random.truncated_normal(keys[0], -4.0, 4.0, (ROWS, D_IN), jnp.float32)
    jitter = jax.random.truncated_normal(keys[1], -4.0, 4.0, (ROWS, D_IN), jnp.float32)
    row_scale = (1.0 + 2.0 * position) * jnp.exp(jax.random.uniform(keys[2], (ROWS, 1), jnp.float32, -0.3, 0.3))
    offset = 0.7 * jax.random.truncated_normal(keys[3], -3.0, 3.0, (D_IN,), jnp.float32)
    first_view = row_scale * (shared + offset)
    second_view = row_scale * (0.8 * shared + 0.6 * jitter + offset)
    return jnp.stack([first_view, second_view], axis=1).astype(jnp.bfloat16)


def steps_of(rng, extent, pieces, low, high):
    loudness = 1.0
    for dim, blocks in pieces:
        steps = jax.random.uniform(jax.random.fold_in(jax.random.fold_in(rng, 6), dim), (blocks,), jnp.float32, low / len(pieces), high / len(pieces))
        loudness = loudness * jnp.repeat(jnp.exp(steps), extent[dim] // blocks).reshape((-1,) + (1,) * (len(extent) - 1 - dim))
    return loudness


def normal_values(rng, shape, scale, bound, cuts=(), kind=jnp.bfloat16):
    gain = steps_of(rng, shape, cuts, -0.22, 0.18) if cuts else 1.0
    entries = jax.random.normal(rng, shape, jnp.float32) * scale * gain
    return jnp.minimum(jnp.maximum(entries, -bound), bound).astype(kind)


def setup_inputs(seed: int = 0) -> dict:
    key_of = jax.random.split(jax.random.key(seed), 3)
    embeds = draw_embeds(jax.random.fold_in(key_of[2], 71), 0)
    weight = normal_values(key_of[1], (D_IN, D_OUT), D_IN ** -0.5, 0.0625, ((0, 32), (1, 16)))
    return {"embeds": embeds, "weight": weight}


off_weight = 0.0051
loss_scale = 8.0
epsilon = 1e-05

def split_product(gram, view):
    high = gram.astype(jnp.bfloat16)
    low = (gram - high.astype(jnp.float32)).astype(jnp.bfloat16)
    return jnp.dot(high, view, preferred_element_type=jnp.float32) + jnp.dot(low, view, preferred_element_type=jnp.float32)

def reference(embeds, weight):
    flattened = embeds.reshape(ROWS * 2, D_IN)
    projected = jnp.dot(flattened, weight, preferred_element_type=jnp.float32).reshape(ROWS, 2, D_OUT)
    row_mean = lax.optimization_barrier(jnp.sum(projected, axis=0)) / ROWS
    centered = projected - row_mean
    variance = lax.optimization_barrier(jnp.sum(centered * centered, axis=0)) / ROWS
    spread = jnp.sqrt(variance + epsilon)
    standard = centered / spread
    normed = standard.astype(jnp.bfloat16)
    view_a = normed[:, 0]
    view_b = normed[:, 1]
    gram_a = jnp.dot(view_a, view_a.T, preferred_element_type=jnp.float32)
    gram_b = jnp.dot(view_b, view_b.T, preferred_element_type=jnp.float32)
    float_a = view_a.astype(jnp.float32)
    float_b = view_b.astype(jnp.float32)
    diagonal = lax.optimization_barrier(jnp.sum(float_a * float_b, axis=0)) / ROWS
    frobenius = jnp.sum(gram_a * gram_b) / (ROWS * ROWS)
    loss_value = (jnp.sum((1.0 - diagonal) ** 2 - off_weight * diagonal * diagonal) + off_weight * frobenius) / D_OUT
    weight_diag = 2.0 * ((1.0 - off_weight) * diagonal - 1.0)
    scale_off = 2.0 * off_weight / (ROWS * ROWS)
    grad_a = loss_scale * (scale_off * split_product(gram_b, view_a) + weight_diag * float_b / ROWS)
    grad_b = loss_scale * (scale_off * split_product(gram_a, view_b) + weight_diag * float_a / ROWS)
    grad_normed = jnp.stack([grad_a, grad_b], axis=1)
    grad_mean = lax.optimization_barrier(jnp.sum(grad_normed, axis=0)) / ROWS
    grad_cross = lax.optimization_barrier(jnp.sum(grad_normed * standard, axis=0)) / ROWS
    grad_proj = ((grad_normed - grad_mean - standard * grad_cross) / spread).astype(jnp.bfloat16)
    grad_flat = grad_proj.reshape(ROWS * 2, D_OUT)
    grad_weight = lax.dot_general(flattened, grad_flat, (((0,), (0,)), ((), ())), preferred_element_type=jnp.float32)
    return (loss_value, grad_weight)
```

```python
import jax
import jax.numpy as jnp
from jax import lax
from jax.sharding import Mesh, PartitionSpec as P

D_OUT = 8192

off_weight = 0.0051
loss_scale = 8.0
epsilon = 1e-05

F32 = jnp.float32
BF16 = jnp.bfloat16
PLANE = ("y", "x")
PAD = 16


def exchange(blocks, axes):
    return lax.all_to_all(blocks, axes, split_axis=0, concat_axis=0, tiled=True)


def gather(block, axes):
    n = lax.axis_size(axes)
    blocks = jnp.broadcast_to(block[None], (n,) + block.shape)
    return exchange(blocks, axes)


def pieces(value):
    high = lax.reduce_precision(value, 8, 7)
    rest = value - high
    middle = lax.reduce_precision(rest, 8, 7)
    low = rest - middle
    return [high.astype(BF16), middle.astype(BF16), low.astype(BF16)]


def pad_rows(rows, width):
    rows = [r.reshape(1, width) for r in rows]
    return jnp.concatenate(rows + [jnp.zeros((PAD - len(rows), width), BF16)], axis=0)


def scalar_rows(values, width):
    rows = []
    for value in values:
        rows += [jnp.broadcast_to(p, (width,)) for p in pieces(value)]
    return pad_rows(rows, width)


def split_product(gram_t, view):
    high = gram_t.astype(BF16)
    low = (gram_t - high.astype(F32)).astype(BF16)
    rows = (((0,), (0,)), ((), ()))
    return lax.dot_general(high, view, rows, preferred_element_type=F32) + lax.dot_general(
        low, view, rows, preferred_element_type=F32
    )


def body(embeds, weight):
    n_chip = lax.axis_size(PLANE)
    n_feat = lax.axis_size("feat")
    n_batch = 2 * n_chip
    local_rows, _, d_in = embeds.shape
    chip_rows = 2 * local_rows
    n_rows = local_rows * n_batch
    depth, width_out = weight.shape
    half = width_out // 2
    core = lax.axis_index("core")
    chip = lax.axis_index(PLANE)
    first = core == 0

    def in_core_order(own, other, axis):
        return jnp.concatenate([jnp.where(first, own, other), jnp.where(first, other, own)], axis=axis)

    def swap_core(a):
        return lax.ppermute(a, "core", [(0, 1), (1, 0)])

    with jax.named_scope("weight_gather"):
        halves = weight.reshape(depth, 2, half).transpose(1, 0, 2)
        chip_weight = exchange(halves, "core").reshape(2 * depth, half)
        all_weight = gather(chip_weight, PLANE).reshape(d_in, half)
    with jax.named_scope("embeds_order"):
        by_view = embeds.transpose(1, 0, 2).reshape(2 * local_rows, d_in)
        other_view = swap_core(by_view)
    with jax.named_scope("embeds_exchange"):
        exchanged = lax.all_to_all(
            by_view.reshape(2 * local_rows, n_batch, depth).transpose(1, 0, 2),
            ("y", "x", "core"), split_axis=0, concat_axis=0, tiled=True,
        ).reshape(n_batch, 2, local_rows, depth)
        embeds_a = exchanged[:, 0].reshape(n_rows, depth)
        embeds_b = exchanged[:, 1].reshape(n_rows, depth)

    with jax.named_scope("project"):
        own = jnp.dot(by_view, all_weight, preferred_element_type=F32)
        other = jnp.dot(other_view, all_weight, preferred_element_type=F32)
        own = jnp.concatenate([own[:local_rows], own[local_rows:]], axis=1)
        other = jnp.concatenate([other[:local_rows], other[local_rows:]], axis=1)
        projected = in_core_order(own, other, 0)
    with jax.named_scope("project_gather"):
        chip_mean = jnp.sum(projected, axis=0) / chip_rows
        block = jnp.concatenate(
            [(projected - chip_mean).astype(BF16), pad_rows(pieces(chip_mean), width_out)], axis=0
        )
        got = gather(block, PLANE)
    with jax.named_scope("standardize"):
        chip_means = jnp.sum(got[:, chip_rows : chip_rows + 3].astype(F32), axis=1)
        row_mean = jnp.sum(chip_means, axis=0) / n_chip
        centered = got[:, :chip_rows].astype(F32) + (chip_means - row_mean)[:, None, :]
        centered = centered.reshape(n_rows, width_out)
        variance = jnp.sum(centered * centered, axis=0) / n_rows
        spread = jnp.sqrt(variance + epsilon)
        standard = centered / spread
        normed = standard.astype(BF16)
        view_a, view_b = normed[:, :half], normed[:, half:]
        float_a, float_b = view_a.astype(F32), view_b.astype(F32)
        diagonal = jnp.sum(float_a * float_b, axis=0) / n_rows
        diag_local = jnp.sum((1.0 - diagonal) ** 2 - off_weight * diagonal * diagonal)

    with jax.named_scope("gram"):
        mine = lax.dynamic_slice_in_dim(normed, chip * chip_rows, chip_rows, axis=0)
        contract = (((1,), (1,)), ((), ()))
        part_a = lax.dot_general(view_a, mine[:, :half], contract, preferred_element_type=F32)
        part_b = lax.dot_general(view_b, mine[:, half:], contract, preferred_element_type=F32)
        parts = jnp.stack([part_a.astype(BF16), part_b.astype(BF16)])
    with jax.named_scope("gram_core"):
        parts = jnp.sum(exchange(parts, "core").astype(F32), axis=0)
    with jax.named_scope("gram_reduce"):
        parts = parts.astype(BF16).reshape(n_feat, n_rows // n_feat, chip_rows)
        extra = jnp.broadcast_to(scalar_rows([diag_local], chip_rows)[None], (n_feat, PAD, chip_rows))
        got_z = exchange(jnp.concatenate([parts, extra], axis=1), "feat")
        summed = jnp.sum(got_z.astype(F32), axis=0)
        gram_block = summed[: n_rows // n_feat].astype(BF16)
        diag_core = jnp.sum(summed[n_rows // n_feat : n_rows // n_feat + 3, 0])
    with jax.named_scope("gram_gather"):
        gram_t = gather(gram_block, "feat").reshape(n_rows, chip_rows)
        other_t, other_diag = swap_core(gram_t), swap_core(diag_core)
        gram_a = jnp.where(first, gram_t, other_t).astype(F32)
        gram_b = jnp.where(first, other_t, gram_t).astype(F32)
        diag_total = diag_core + other_diag
    with jax.named_scope("back"):
        off_local = jnp.sum(gram_a * gram_b)
        back_a = split_product(gram_b, view_a)
        back_b = split_product(gram_a, view_b)
        back = jnp.concatenate([back_a, back_b], axis=1).astype(BF16)
        block = jnp.concatenate([back, scalar_rows([off_local], width_out)], axis=0)
    with jax.named_scope("back_gather"):
        got = gather(block, PLANE)
    with jax.named_scope("grad"):
        off_total = jnp.sum(got[:, chip_rows : chip_rows + 3, 0].astype(F32)) / (n_rows * n_rows)
        loss_value = (off_weight * off_total + diag_total) / D_OUT
        back = got[:, :chip_rows].astype(F32).reshape(n_rows, width_out)
        weight_diag = 2.0 * ((1.0 - off_weight) * diagonal - 1.0)
        weight_diag = jnp.concatenate([weight_diag, weight_diag])
        scale_off = 2.0 * off_weight / (n_rows * n_rows)
        crossed = jnp.concatenate([float_b, float_a], axis=1)
        grad_normed = loss_scale * (scale_off * back + weight_diag * crossed / n_rows)
        grad_mean = jnp.sum(grad_normed, axis=0) / n_rows
        grad_cross = jnp.sum(grad_normed * standard, axis=0) / n_rows
        grad_proj = ((grad_normed - grad_mean - standard * grad_cross) / spread).astype(BF16)
    with jax.named_scope("grad_swap"):
        other_proj = swap_core(grad_proj)
    with jax.named_scope("weight_grad"):
        def half_grad(g):
            rows = (((0,), (0,)), ((), ()))
            return lax.dot_general(embeds_a, g[:, :half], rows, preferred_element_type=F32) + lax.dot_general(
                embeds_b, g[:, half:], rows, preferred_element_type=F32
            )
        grad_weight = in_core_order(half_grad(grad_proj), half_grad(other_proj), 1)
    return (loss_value, grad_weight)


def solution(mesh):
    n_batch, n_feat = mesh.devices.shape
    grid = Mesh(mesh.devices.reshape(4, n_batch // 8, 2, n_feat), ("y", "x", "core", "feat"))
    batch = ("y", "x", "core")
    return jax.shard_map(
        body,
        mesh=grid,
        in_specs=(P(batch, None, None), P(batch, "feat")),
        out_specs=(P(), P(batch, "feat")),
        check_vma=False,
    )
```

```python
import jax
import jax.numpy as jnp
from jax import lax
from jax.sharding import Mesh, PartitionSpec as P

D_OUT = 8192

off_weight = 0.0051
loss_scale = 8.0
epsilon = 1e-05

F32 = jnp.float32
BF16 = jnp.bfloat16
PLANE = ("y", "x")
PAD = 16


def exchange(blocks, axes):
    return lax.all_to_all(blocks, axes, split_axis=0, concat_axis=0, tiled=True)


def gather(block, axes):
    n = lax.axis_size(axes)
    blocks = jnp.broadcast_to(block[None], (n,) + block.shape)
    return exchange(blocks, axes)


def pieces(value):
    high = lax.reduce_precision(value, 8, 7)
    rest = value - high
    middle = lax.reduce_precision(rest, 8, 7)
    low = rest - middle
    return [high.astype(BF16), middle.astype(BF16), low.astype(BF16)]


def pad_rows(rows, width):
    rows = [r.reshape(1, width) for r in rows]
    return jnp.concatenate(rows + [jnp.zeros((PAD - len(rows), width), BF16)], axis=0)


def split_product(gram_t, view):
    high = gram_t.astype(BF16)
    low = (gram_t - high.astype(F32)).astype(BF16)
    rows = (((0,), (0,)), ((), ()))
    return lax.dot_general(high, view, rows, preferred_element_type=F32) + lax.dot_general(
        low, view, rows, preferred_element_type=F32
    )


def body(embeds, weight):
    n_chip = lax.axis_size(PLANE)
    n_feat = lax.axis_size("feat")
    n_batch = 2 * n_chip
    local_rows, _, d_in = embeds.shape
    chip_rows = 2 * local_rows
    n_rows = local_rows * n_batch
    depth, width_out = weight.shape
    half = width_out // 2
    core = lax.axis_index("core")
    chip = lax.axis_index(PLANE)
    first = core == 0

    def in_core_order(own, other, axis):
        return jnp.concatenate([jnp.where(first, own, other), jnp.where(first, other, own)], axis=axis)

    def swap_core(a):
        return lax.ppermute(a, "core", [(0, 1), (1, 0)])

    with jax.named_scope("embeds_order"):
        by_view = embeds.transpose(1, 0, 2).reshape(2 * local_rows, d_in)
        share = 2 * local_rows // n_feat
        z_rows = lax.dynamic_slice_in_dim(by_view, lax.axis_index("feat") * share, share, axis=0)
        z_rows = z_rows.reshape(share, n_chip, 2 * depth).transpose(1, 0, 2)
    with jax.named_scope("weight_gather"):
        halves = weight.reshape(depth, 2, half).transpose(1, 0, 2)
        chip_weight = exchange(halves, "core").reshape(2 * depth, half)
        blocks = jnp.broadcast_to(chip_weight[None], (n_chip,) + chip_weight.shape)
        blocks, by_view, z_rows = lax.optimization_barrier((blocks, by_view, z_rows))
        other_view = swap_core(by_view)
        all_weight = exchange(blocks, PLANE).reshape(d_in, half)
    with jax.named_scope("project"):
        all_weight, by_view = lax.optimization_barrier((all_weight, by_view))
        own = jnp.dot(by_view, all_weight, preferred_element_type=F32)
        other = jnp.dot(other_view, all_weight, preferred_element_type=F32)
        own = jnp.concatenate([own[:local_rows], own[local_rows:]], axis=1)
        other = jnp.concatenate([other[:local_rows], other[local_rows:]], axis=1)
        projected = in_core_order(own, other, 0)
    with jax.named_scope("project_gather"):
        chip_mean = jnp.sum(projected, axis=0) / chip_rows
        block = jnp.concatenate(
            [
                (projected - chip_mean).astype(BF16),
                jnp.stack(pieces(chip_mean)),
                jnp.zeros((PAD - share - 3, width_out), BF16),
            ],
            axis=0,
        )
        blocks = jnp.broadcast_to(block[None], (n_chip,) + block.shape)
        got = exchange(jnp.concatenate([blocks, z_rows], axis=1), PLANE)
    with jax.named_scope("embeds_gather"):
        z_got = got[:, chip_rows + PAD - share :].reshape(n_chip, share, 2, depth)
        kept = jnp.where(first, z_got[:, :, 0], z_got[:, :, 1])
        sent = swap_core(jnp.where(first, z_got[:, :, 1], z_got[:, :, 0]))
        rows = jnp.stack([jnp.where(first, kept, sent), jnp.where(first, sent, kept)], axis=1)
        exchanged = lax.all_gather(rows, "feat", axis=0, tiled=False)
        exchanged = exchanged.reshape(2, n_feat // 2, n_batch, share, depth).transpose(0, 2, 1, 3, 4)
        embeds_a = exchanged[0].reshape(n_rows, depth)
        embeds_b = exchanged[1].reshape(n_rows, depth)
    with jax.named_scope("standardize"):
        chip_means = jnp.sum(got[:, chip_rows : chip_rows + 3].astype(F32), axis=1)
        row_mean = jnp.sum(chip_means, axis=0) / n_chip
        centered = got[:, :chip_rows].astype(F32) + (chip_means - row_mean)[:, None, :]
        centered = centered.reshape(n_rows, width_out)
        variance = jnp.sum(centered * centered, axis=0) / n_rows
        spread = jnp.sqrt(variance + epsilon)
        standard = centered / spread
        normed = standard.astype(BF16)
        view_a, view_b = normed[:, :half], normed[:, half:]
        float_a, float_b = view_a.astype(F32), view_b.astype(F32)
        diagonal = jnp.sum(float_a * float_b, axis=0) / n_rows
        diag_terms = (1.0 - diagonal) ** 2 - off_weight * diagonal * diagonal
        diag_local = diag_terms[:chip_rows] + diag_terms[chip_rows:]

    with jax.named_scope("gram"):
        mine = lax.dynamic_slice_in_dim(normed, chip * chip_rows, chip_rows, axis=0)
        contract = (((1,), (1,)), ((), ()))
        part_a = lax.dot_general(view_a, mine[:, :half], contract, preferred_element_type=F32)
        part_b = lax.dot_general(view_b, mine[:, half:], contract, preferred_element_type=F32)
        parts = jnp.stack([part_a.astype(BF16), part_b.astype(BF16)])
        extra = pad_rows(pieces(diag_local), chip_rows)
        parts, extra, diagonal, spread = lax.optimization_barrier((parts, extra, diagonal, spread))
    with jax.named_scope("gram_core"):
        parts = jnp.sum(exchange(parts, "core").astype(F32), axis=0)
    with jax.named_scope("gram_reduce"):
        parts = parts.astype(BF16).reshape(n_feat, n_rows // n_feat, chip_rows)
        extra = jnp.broadcast_to(extra[None], (n_feat, PAD, chip_rows))
        got_z = exchange(jnp.concatenate([parts, extra], axis=1), "feat")
        summed = jnp.sum(got_z.astype(F32), axis=0)
        gram_block = summed[: n_rows // n_feat].astype(BF16)
        diag_core = jnp.sum(summed[n_rows // n_feat : n_rows // n_feat + 3], axis=0)
        gram_block, diag_core = lax.optimization_barrier((gram_block, diag_core))
    with jax.named_scope("gram_gather"):
        gram_t = gather(gram_block, "feat").reshape(n_rows, chip_rows)
        other_t = swap_core(gram_t)
        gram_a = jnp.where(first, gram_t, other_t).astype(F32)
        gram_b = jnp.where(first, other_t, gram_t).astype(F32)
    with jax.named_scope("back"):
        off_local = jnp.sum(gram_a * gram_b, axis=0)
        back_a = split_product(gram_b, view_a)
        back_b = split_product(gram_a, view_b)
        back = jnp.concatenate([back_a, back_b], axis=1).astype(BF16)
        terms = jnp.concatenate([off_local, jnp.zeros((width_out - chip_rows,), F32)])
        block = jnp.concatenate([back, pad_rows(pieces(terms), width_out)], axis=0)
        other_diag = swap_core(diag_core)
    with jax.named_scope("back_gather"):
        got = gather(block, PLANE)
    with jax.named_scope("grad"):
        off_total = jnp.sum(got[:, chip_rows : chip_rows + 3, :chip_rows].astype(F32)) / (n_rows * n_rows)
        diag_total = jnp.sum(diag_core + other_diag)
        loss_value = (off_weight * off_total + diag_total) / D_OUT
        back = got[:, :chip_rows].astype(F32).reshape(n_rows, width_out)
        weight_diag = 2.0 * ((1.0 - off_weight) * diagonal - 1.0)
        weight_diag = jnp.concatenate([weight_diag, weight_diag])
        scale_off = 2.0 * off_weight / (n_rows * n_rows)
        crossed = jnp.concatenate([float_b, float_a], axis=1)
        grad_normed = loss_scale * (scale_off * back + weight_diag * crossed / n_rows)
        grad_mean = jnp.sum(grad_normed, axis=0) / n_rows
        grad_cross = jnp.sum(grad_normed * standard, axis=0) / n_rows
        grad_proj = ((grad_normed - grad_mean - standard * grad_cross) / spread).astype(BF16)
    with jax.named_scope("grad_swap"):
        other_proj = swap_core(grad_proj)
    with jax.named_scope("weight_grad"):
        def half_grad(g):
            rows = (((0,), (0,)), ((), ()))
            return lax.dot_general(embeds_a, g[:, :half], rows, preferred_element_type=F32) + lax.dot_general(
                embeds_b, g[:, half:], rows, preferred_element_type=F32
            )
        grad_weight = in_core_order(half_grad(grad_proj), half_grad(other_proj), 1)
    return (loss_value, grad_weight)


def solution(mesh):
    n_batch, n_feat = mesh.devices.shape
    grid = Mesh(mesh.devices.reshape(4, n_batch // 8, 2, n_feat), ("y", "x", "core", "feat"))
    batch = ("y", "x", "core")
    return jax.shard_map(
        body,
        mesh=grid,
        in_specs=(P(batch, None, None), P(batch, "feat")),
        out_specs=(P(), P(batch, "feat")),
        check_vma=False,
    )
```

```python
import jax
import jax.numpy as jnp
from jax import lax
from jax.sharding import Mesh, PartitionSpec as P

D_OUT = 8192

off_weight = 0.0051
loss_scale = 8.0
epsilon = 1e-05

F32 = jnp.float32
BF16 = jnp.bfloat16
PLANE = ("y", "x")
BATCH = ("y", "x", "core")
PAD = 16


def exchange(blocks, axes):
    return lax.all_to_all(blocks, axes, split_axis=0, concat_axis=0, tiled=True)


def gather(block, axes):
    n = lax.axis_size(axes)
    blocks = jnp.broadcast_to(block[None], (n,) + block.shape)
    return exchange(blocks, axes)


def pieces(value):
    high = lax.reduce_precision(value, 8, 7)
    rest = value - high
    middle = lax.reduce_precision(rest, 8, 7)
    low = rest - middle
    return [high.astype(BF16), middle.astype(BF16), low.astype(BF16)]


def pad_rows(rows, width):
    rows = [r.reshape(1, width) for r in rows]
    return jnp.concatenate(rows + [jnp.zeros((PAD - len(rows), width), BF16)], axis=0)


def split_product(gram_t, view):
    high = gram_t.astype(BF16)
    low = (gram_t - high.astype(F32)).astype(BF16)
    rows = (((0,), (0,)), ((), ()))
    return lax.dot_general(high, view, rows, preferred_element_type=F32) + lax.dot_general(
        low, view, rows, preferred_element_type=F32
    )


def body(embeds, weight):
    n_chip = lax.axis_size(PLANE)
    n_feat = lax.axis_size("feat")
    n_batch = 2 * n_chip
    local_rows, _, d_in = embeds.shape
    chip_rows = 2 * local_rows
    n_rows = local_rows * n_batch
    depth, width_out = weight.shape
    half = width_out // 2
    core = lax.axis_index("core")
    chip = lax.axis_index(PLANE)
    first = core == 0

    def in_core_order(own, other, axis):
        return jnp.concatenate([jnp.where(first, own, other), jnp.where(first, other, own)], axis=axis)

    def swap_core(a):
        return lax.ppermute(a, "core", [(0, 1), (1, 0)])

    with jax.named_scope("embeds_exchange"):
        share = 2 * local_rows // n_feat
        per_view = n_feat // 2
        z = lax.axis_index("feat")
        z_rows = lax.dynamic_slice(embeds, ((z % per_view) * share, z // per_view, 0), (share, 1, d_in))
        z_rows = z_rows.reshape(share, n_batch, depth).transpose(1, 0, 2)
        z_rows = exchange(z_rows, BATCH)
        weight, z_rows = lax.optimization_barrier((weight, z_rows))
        embeds_k = lax.all_gather(z_rows, "feat", axis=0, tiled=False)
        embeds_k = embeds_k.reshape(2, per_view, n_batch, share, depth).transpose(0, 2, 1, 3, 4)
        embeds_k = embeds_k.reshape(2, n_rows, depth)
    with jax.named_scope("weight_gather"):
        core_weight = gather(weight, PLANE).reshape(n_chip * depth, width_out)
    with jax.named_scope("embeds_order"):
        by_core = embeds.reshape(local_rows, 2, n_chip, 2, depth).transpose(3, 1, 0, 2, 4)
        by_core = by_core.reshape(2, 2 * local_rows, n_chip * depth)
        own_rows = lax.dynamic_index_in_dim(by_core, core, 0, keepdims=False)
        other_rows = swap_core(lax.dynamic_index_in_dim(by_core, 1 - core, 0, keepdims=False))
    with jax.named_scope("project"):
        own = jnp.dot(own_rows, core_weight, preferred_element_type=F32)
        other = jnp.dot(other_rows, core_weight, preferred_element_type=F32)
        def by_half(p):
            a, b = p[:local_rows], p[local_rows:]
            low = jnp.concatenate([a[:, :half], b[:, :half]], axis=1)
            high = jnp.concatenate([a[:, half:], b[:, half:]], axis=1)
            return jnp.where(first, low, high), jnp.where(first, high, low)

        own_kept, own_sent = by_half(own)
        other_kept, other_sent = by_half(other)
        got_other, got_own = jnp.split(swap_core(jnp.concatenate([own_sent, other_sent])), 2)
        projected = in_core_order(own_kept + got_own, other_kept + got_other, 0)
    with jax.named_scope("project_gather"):
        chip_mean = jnp.sum(projected, axis=0) / chip_rows
        block = jnp.concatenate(
            [(projected - chip_mean).astype(BF16), pad_rows(pieces(chip_mean), width_out)], axis=0
        )
        block, embeds_k = lax.optimization_barrier((block, embeds_k))
        got = gather(block, PLANE)
        embeds_a, embeds_b = embeds_k[0], embeds_k[1]
    with jax.named_scope("standardize"):
        chip_means = jnp.sum(got[:, chip_rows : chip_rows + 3].astype(F32), axis=1)
        row_mean = jnp.sum(chip_means, axis=0) / n_chip
        centered = got[:, :chip_rows].astype(F32) + (chip_means - row_mean)[:, None, :]
        centered = centered.reshape(n_rows, width_out)
        variance = jnp.sum(centered * centered, axis=0) / n_rows
        spread = jnp.sqrt(variance + epsilon)
        standard = centered / spread
        normed = standard.astype(BF16)
        view_a, view_b = normed[:, :half], normed[:, half:]
        float_a, float_b = view_a.astype(F32), view_b.astype(F32)
        diagonal = jnp.sum(float_a * float_b, axis=0) / n_rows
        diag_terms = (1.0 - diagonal) ** 2 - off_weight * diagonal * diagonal
        diag_local = diag_terms[:chip_rows] + diag_terms[chip_rows:]

    with jax.named_scope("gram"):
        mine = lax.dynamic_slice_in_dim(normed, chip * chip_rows, chip_rows, axis=0)
        contract = (((1,), (1,)), ((), ()))
        part_a = lax.dot_general(view_a, mine[:, :half], contract, preferred_element_type=F32)
        part_b = lax.dot_general(view_b, mine[:, half:], contract, preferred_element_type=F32)
        parts = jnp.stack([part_a.astype(BF16), part_b.astype(BF16)])
        extra = pad_rows(pieces(diag_local), chip_rows)
        parts, extra, diagonal, spread = lax.optimization_barrier((parts, extra, diagonal, spread))
    with jax.named_scope("gram_core"):
        parts = jnp.sum(exchange(parts, "core").astype(F32), axis=0)
    with jax.named_scope("gram_reduce"):
        parts = parts.astype(BF16).reshape(n_feat, n_rows // n_feat, chip_rows)
        extra = jnp.broadcast_to(extra[None], (n_feat, PAD, chip_rows))
        got_z = exchange(jnp.concatenate([parts, extra], axis=1), "feat")
        summed = jnp.sum(got_z.astype(F32), axis=0)
        gram_block = summed[: n_rows // n_feat].astype(BF16)
        diag_core = jnp.sum(summed[n_rows // n_feat : n_rows // n_feat + 3], axis=0)
        gram_block, diag_core = lax.optimization_barrier((gram_block, diag_core))
    with jax.named_scope("gram_gather"):
        gram_t = gather(gram_block, "feat").reshape(n_rows, chip_rows)
        other_t = swap_core(gram_t)
        gram_a = jnp.where(first, gram_t, other_t).astype(F32)
        gram_b = jnp.where(first, other_t, gram_t).astype(F32)
    with jax.named_scope("back"):
        off_local = jnp.sum(gram_a * gram_b, axis=0)
        back_a = split_product(gram_b, view_a)
        back_b = split_product(gram_a, view_b)
        back = jnp.concatenate([back_a, back_b], axis=1).astype(BF16)
        terms = jnp.concatenate([off_local, jnp.zeros((width_out - chip_rows,), F32)])
        block = jnp.concatenate([back, pad_rows(pieces(terms), width_out)], axis=0)
        other_diag = swap_core(diag_core)
    with jax.named_scope("back_gather"):
        got = gather(block, PLANE)
    with jax.named_scope("grad"):
        off_total = jnp.sum(got[:, chip_rows : chip_rows + 3, :chip_rows].astype(F32)) / (n_rows * n_rows)
        diag_total = jnp.sum(diag_core + other_diag)
        loss_value = (off_weight * off_total + diag_total) / D_OUT
        back = got[:, :chip_rows].astype(F32).reshape(n_rows, width_out)
        weight_diag = 2.0 * ((1.0 - off_weight) * diagonal - 1.0)
        weight_diag = jnp.concatenate([weight_diag, weight_diag])
        scale_off = 2.0 * off_weight / (n_rows * n_rows)
        crossed = jnp.concatenate([float_b, float_a], axis=1)
        grad_normed = loss_scale * (scale_off * back + weight_diag * crossed / n_rows)
        grad_mean = jnp.sum(grad_normed, axis=0) / n_rows
        grad_cross = jnp.sum(grad_normed * standard, axis=0) / n_rows
        grad_proj = ((grad_normed - grad_mean - standard * grad_cross) / spread).astype(BF16)
    with jax.named_scope("grad_swap"):
        other_proj = swap_core(grad_proj)
    with jax.named_scope("weight_grad"):
        def half_grad(g):
            rows = (((0,), (0,)), ((), ()))
            return lax.dot_general(embeds_a, g[:, :half], rows, preferred_element_type=F32) + lax.dot_general(
                embeds_b, g[:, half:], rows, preferred_element_type=F32
            )
        grad_weight = in_core_order(half_grad(grad_proj), half_grad(other_proj), 1)
    return (loss_value, grad_weight)


def solution(mesh):
    n_batch, n_feat = mesh.devices.shape
    grid = Mesh(mesh.devices.reshape(4, n_batch // 8, 2, n_feat), ("y", "x", "core", "feat"))
    return jax.shard_map(
        body,
        mesh=grid,
        in_specs=(P(BATCH, None, None), P(BATCH, "feat")),
        out_specs=(P(), P(BATCH, "feat")),
        check_vma=False,
    )
```

```python
import functools

import jax
import jax.numpy as jnp
from jax import lax
from jax.experimental import pallas as pl
from jax.experimental.pallas import tpu as pltpu
from jax.sharding import Mesh, PartitionSpec as P

D_OUT = 8192

off_weight = 0.0051
loss_scale = 8.0
epsilon = 1e-05

F32 = jnp.float32
BF16 = jnp.bfloat16
PLANE = ("y", "x")
BATCH = ("y", "x", "core")
PAD = 16


def exchange(blocks, axes):
    return lax.all_to_all(blocks, axes, split_axis=0, concat_axis=0, tiled=True)


def gather(block, axes):
    n = lax.axis_size(axes)
    blocks = jnp.broadcast_to(block[None], (n,) + block.shape)
    return exchange(blocks, axes)


def pieces(value):
    high = lax.reduce_precision(value, 8, 7)
    rest = value - high
    middle = lax.reduce_precision(rest, 8, 7)
    low = rest - middle
    return [high.astype(BF16), middle.astype(BF16), low.astype(BF16)]


def pad_rows(rows, width):
    rows = [r.reshape(1, width) for r in rows]
    return jnp.concatenate(rows + [jnp.zeros((PAD - len(rows), width), BF16)], axis=0)


def split_product(gram_t, view):
    high = gram_t.astype(BF16)
    low = (gram_t - high.astype(F32)).astype(BF16)
    rows = (((0,), (0,)), ((), ()))
    return lax.dot_general(high, view, rows, preferred_element_type=F32) + lax.dot_general(
        low, view, rows, preferred_element_type=F32
    )


def ring_groups():
    index = lambda y, x, c: (y * 4 + x) * 2 + c
    along_x = lambda c: [[index(y, x, c) for x in range(4)] for y in range(4)]
    along_y = lambda c: [[index(y, x, c) for y in range(4)] for x in range(4)]
    return along_x(0) + along_y(1), along_y(0) + along_x(1)


def ring_gather(block, groups):
    blocks = jnp.broadcast_to(block[None], (4,) + block.shape)
    return lax.all_to_all(blocks, BATCH, split_axis=0, concat_axis=0, tiled=True, axis_index_groups=groups)


def grad_kernel(n_rows, chip_rows, scale, back_ref, got_ref, shift_ref, inv_ref, cross_ref, out_ref, grad_ref, std_ref):
    n_chip, _, width = got_ref.shape
    half = width // 2
    inv, factor = inv_ref[...], cross_ref[...]

    def fold(a):
        return jnp.sum(a.reshape(chip_rows // 8, 8, width), axis=0)

    def first(p, sums):
        centered = got_ref[p, :chip_rows].astype(F32) + shift_ref[pl.ds(p, 1), :]
        standard = centered * inv
        normed = standard.astype(BF16).astype(F32)
        crossed = jnp.concatenate([normed[:, half:], normed[:, :half]], axis=1)
        grad = scale * back_ref[p, :chip_rows].astype(F32) + factor * crossed
        rows = pl.ds(pl.multiple_of(p * chip_rows, chip_rows), chip_rows)
        grad_ref[rows, :] = grad
        std_ref[rows, :] = standard
        return sums[0] + fold(grad), sums[1] + fold(grad * standard)

    zero = jnp.zeros((8, width), F32)
    total, cross = lax.fori_loop(0, n_chip, first, (zero, zero))
    grad_mean = jnp.sum(total, axis=0, keepdims=True) / n_rows
    grad_cross = jnp.sum(cross, axis=0, keepdims=True) / n_rows

    def second(p, carry):
        rows = pl.ds(pl.multiple_of(p * chip_rows, chip_rows), chip_rows)
        out_ref[rows, :] = ((grad_ref[rows, :] - grad_mean - std_ref[rows, :] * grad_cross) * inv).astype(BF16)
        return carry

    lax.fori_loop(0, n_chip, second, 0)


def body(embeds, weight):
    n_chip = lax.axis_size(PLANE)
    n_feat = lax.axis_size("feat")
    n_batch = 2 * n_chip
    local_rows, _, d_in = embeds.shape
    chip_rows = 2 * local_rows
    n_rows = local_rows * n_batch
    depth, width_out = weight.shape
    half = width_out // 2
    core = lax.axis_index("core")
    chip = lax.axis_index(PLANE)
    first = core == 0

    def in_core_order(own, other, axis):
        return jnp.concatenate([jnp.where(first, own, other), jnp.where(first, other, own)], axis=axis)

    def swap_core(a):
        return lax.ppermute(a, "core", [(0, 1), (1, 0)])

    with jax.named_scope("embeds_exchange"):
        share = 2 * local_rows // n_feat
        per_view = n_feat // 2
        z = lax.axis_index("feat")
        z_rows = lax.dynamic_slice(embeds, ((z % per_view) * share, z // per_view, 0), (share, 1, d_in))
        z_rows = z_rows.reshape(share, n_batch, depth).transpose(1, 0, 2)
        z_rows = exchange(z_rows, BATCH)
        weight, z_rows = lax.optimization_barrier((weight, z_rows))
        embeds_k = lax.all_gather(z_rows, "feat", axis=0, tiled=False)
    with jax.named_scope("weight_gather"):
        first_groups, second_groups = ring_groups()
        row_weight = ring_gather(weight, first_groups)
        core_weight = ring_gather(row_weight, second_groups).reshape(n_chip * depth, width_out)
    with jax.named_scope("embeds_order"):
        by_core = embeds.reshape(local_rows, 2, 4, n_chip // 4, 2, depth)
        rows_zero = by_core[:, :, :, :, 0].transpose(1, 0, 2, 3, 4).reshape(2 * local_rows, n_chip * depth)
        rows_one = by_core[:, :, :, :, 1].transpose(1, 0, 3, 2, 4).reshape(2 * local_rows, n_chip * depth)
        own_rows = jnp.where(first, rows_zero, rows_one)
        other_rows = swap_core(jnp.where(first, rows_one, rows_zero))
    with jax.named_scope("project"):
        own = jnp.dot(own_rows, core_weight, preferred_element_type=F32)
        other = jnp.dot(other_rows, core_weight, preferred_element_type=F32)
        def by_half(p):
            a, b = p[:local_rows], p[local_rows:]
            low = jnp.concatenate([a[:, :half], b[:, :half]], axis=1)
            high = jnp.concatenate([a[:, half:], b[:, half:]], axis=1)
            return jnp.where(first, low, high), jnp.where(first, high, low)

        own_kept, own_sent = by_half(own)
        other_kept, other_sent = by_half(other)
        got_other, got_own = jnp.split(swap_core(jnp.concatenate([own_sent, other_sent])), 2)
        projected = in_core_order(own_kept + got_own, other_kept + got_other, 0)
    with jax.named_scope("project_gather"):
        chip_mean = jnp.sum(projected, axis=0) / chip_rows
        block = jnp.concatenate(
            [(projected - chip_mean).astype(BF16), pad_rows(pieces(chip_mean), width_out)], axis=0
        )
        block, embeds_k = lax.optimization_barrier((block, embeds_k))
        got = gather(block, PLANE)
        embeds_k = embeds_k.reshape(2, per_view, n_batch, share, depth).transpose(0, 2, 1, 3, 4)
        embeds_k = embeds_k.reshape(2, n_rows, depth)
        embeds_a, embeds_b = embeds_k[0], embeds_k[1]
    with jax.named_scope("standardize"):
        chip_means = jnp.sum(got[:, chip_rows : chip_rows + 3].astype(F32), axis=1)
        row_mean = jnp.sum(chip_means, axis=0) / n_chip
        shift = chip_means - row_mean
        centered = got[:, :chip_rows].astype(F32) + shift[:, None, :]
        centered = centered.reshape(n_rows, width_out)
        variance = jnp.sum(centered * centered, axis=0) / n_rows
        spread = jnp.sqrt(variance + epsilon)
        inverse = 1.0 / spread
        normed = (centered * inverse).astype(BF16)
        view_a, view_b = normed[:, :half], normed[:, half:]
        float_a, float_b = view_a.astype(F32), view_b.astype(F32)
        diagonal = jnp.sum(float_a * float_b, axis=0) / n_rows
        diag_terms = (1.0 - diagonal) ** 2 - off_weight * diagonal * diagonal
        diag_local = diag_terms[:chip_rows] + diag_terms[chip_rows:]

    with jax.named_scope("gram"):
        mine = lax.dynamic_slice_in_dim(normed, chip * chip_rows, chip_rows, axis=0)
        contract = (((1,), (1,)), ((), ()))
        part_a = lax.dot_general(view_a, mine[:, :half], contract, preferred_element_type=F32)
        part_b = lax.dot_general(view_b, mine[:, half:], contract, preferred_element_type=F32)
        parts = jnp.stack([part_a.astype(BF16), part_b.astype(BF16)])
        extra = pad_rows(pieces(diag_local), chip_rows)
        weight_diag = 2.0 * ((1.0 - off_weight) * diagonal - 1.0)
        factor = loss_scale / n_rows * jnp.concatenate([weight_diag, weight_diag])
        parts, extra, factor, inverse = lax.optimization_barrier((parts, extra, factor, inverse))
    with jax.named_scope("gram_core"):
        parts = jnp.sum(exchange(parts, "core").astype(F32), axis=0)
    with jax.named_scope("gram_reduce"):
        parts = parts.astype(BF16).reshape(n_feat, n_rows // n_feat, chip_rows)
        extra = jnp.broadcast_to(extra[None], (n_feat, PAD, chip_rows))
        got_z = exchange(jnp.concatenate([parts, extra], axis=1), "feat")
        summed = jnp.sum(got_z.astype(F32), axis=0)
        gram_block = summed[: n_rows // n_feat].astype(BF16)
        diag_core = jnp.sum(summed[n_rows // n_feat : n_rows // n_feat + 3], axis=0)
        gram_block, diag_core = lax.optimization_barrier((gram_block, diag_core))
    with jax.named_scope("gram_gather"):
        gram_t = gather(gram_block, "feat").reshape(n_rows, chip_rows)
        other_t = swap_core(gram_t)
        gram_a = jnp.where(first, gram_t, other_t).astype(F32)
        gram_b = jnp.where(first, other_t, gram_t).astype(F32)
    with jax.named_scope("back"):
        off_local = jnp.sum(gram_a * gram_b, axis=0)
        back_a = split_product(gram_b, view_a)
        back_b = split_product(gram_a, view_b)
        back = jnp.concatenate([back_a, back_b], axis=1).astype(BF16)
        terms = jnp.concatenate([off_local, jnp.zeros((width_out - chip_rows,), F32)])
        block = jnp.concatenate([back, pad_rows(pieces(terms), width_out)], axis=0)
        block, diag_terms = lax.optimization_barrier((block, diag_core + swap_core(diag_core)))
    with jax.named_scope("back_gather"):
        got_back = gather(block, PLANE)
    with jax.named_scope("grad"):
        off_total = jnp.sum(got_back[:, chip_rows : chip_rows + 3, :chip_rows].astype(F32)) / (n_rows * n_rows)
        diag_total = jnp.sum(diag_terms)
        loss_value = (off_weight * off_total + diag_total) / D_OUT
        scale_off = 2.0 * off_weight / (n_rows * n_rows)
        vmem = pl.BlockSpec(memory_space=pltpu.VMEM)
        grad_proj = pl.pallas_call(
            functools.partial(grad_kernel, n_rows, chip_rows, loss_scale * scale_off),
            out_shape=jax.ShapeDtypeStruct((n_rows, width_out), BF16),
            in_specs=[vmem] * 5,
            out_specs=vmem,
            scratch_shapes=[pltpu.VMEM((n_rows, width_out), F32)] * 2,
            compiler_params=pltpu.CompilerParams(vmem_limit_bytes=32 * 1024 * 1024),
            cost_estimate=pl.CostEstimate(flops=20 * n_rows * width_out, bytes_accessed=8 * n_rows * width_out, transcendentals=0),
            name="grad",
        )(got_back, got, shift, inverse[None], factor[None])
    with jax.named_scope("grad_swap"):
        other_proj = swap_core(grad_proj)
    with jax.named_scope("weight_grad"):
        def half_grad(g):
            rows = (((0,), (0,)), ((), ()))
            return lax.dot_general(embeds_a, g[:, :half], rows, preferred_element_type=F32) + lax.dot_general(
                embeds_b, g[:, half:], rows, preferred_element_type=F32
            )
        grad_weight = in_core_order(half_grad(grad_proj), half_grad(other_proj), 1)
    return (loss_value, grad_weight)


def solution(mesh):
    n_batch, n_feat = mesh.devices.shape
    grid = Mesh(mesh.devices.reshape(4, n_batch // 8, 2, n_feat), ("y", "x", "core", "feat"))
    return jax.shard_map(
        body,
        mesh=grid,
        in_specs=(P(BATCH, None, None), P(BATCH, "feat")),
        out_specs=(P(), P(BATCH, "feat")),
        check_vma=False,
    )
```

```python
import functools

import jax
import jax.numpy as jnp
from jax import lax
from jax.experimental import pallas as pl
from jax.experimental.pallas import tpu as pltpu
from jax.sharding import Mesh, PartitionSpec as P

D_OUT = 8192

off_weight = 0.0051
loss_scale = 8.0
epsilon = 1e-05

F32 = jnp.float32
BF16 = jnp.bfloat16
PLANE = ("y", "x")
BATCH = ("y", "x", "core")
FEAT = ("z1", "z0")
PAD = 16


def exchange(blocks, axes):
    return lax.all_to_all(blocks, axes, split_axis=0, concat_axis=0, tiled=True)


def gather(block, axes):
    n = lax.axis_size(axes)
    blocks = jnp.broadcast_to(block[None], (n,) + block.shape)
    return exchange(blocks, axes)


def pieces(value):
    high = lax.reduce_precision(value, 8, 7)
    rest = value - high
    middle = lax.reduce_precision(rest, 8, 7)
    low = rest - middle
    return [high.astype(BF16), middle.astype(BF16), low.astype(BF16)]


def pad_rows(rows, width):
    rows = [r.reshape(1, width) for r in rows]
    return jnp.concatenate(rows + [jnp.zeros((PAD - len(rows), width), BF16)], axis=0)


def split_product(gram_t, view):
    high = gram_t.astype(BF16)
    low = (gram_t - high.astype(F32)).astype(BF16)
    rows = (((0,), (0,)), ((), ()))
    return lax.dot_general(high, view, rows, preferred_element_type=F32) + lax.dot_general(
        low, view, rows, preferred_element_type=F32
    )


def ring_groups():
    index = lambda y, x, c: (y * 4 + x) * 2 + c
    along_x = lambda c: [[index(y, x, c) for x in range(4)] for y in range(4)]
    along_y = lambda c: [[index(y, x, c) for y in range(4)] for x in range(4)]
    return along_x(0) + along_y(1), along_y(0) + along_x(1)


def ring_gather(block, groups):
    blocks = jnp.broadcast_to(block[None], (4,) + block.shape)
    return lax.all_to_all(blocks, BATCH, split_axis=0, concat_axis=0, tiled=True, axis_index_groups=groups)


def grad_kernel(n_rows, chip_rows, scale, back_ref, got_ref, shift_ref, inv_ref, cross_ref, out_ref, grad_ref, std_ref):
    n_chip, _, width = got_ref.shape
    half = width // 2
    inv, factor = inv_ref[...], cross_ref[...]

    def fold(a):
        return jnp.sum(a.reshape(chip_rows // 8, 8, width), axis=0)

    def first(p, sums):
        centered = got_ref[p, :chip_rows].astype(F32) + shift_ref[pl.ds(p, 1), :]
        standard = centered * inv
        normed = standard.astype(BF16).astype(F32)
        crossed = jnp.concatenate([normed[:, half:], normed[:, :half]], axis=1)
        grad = scale * back_ref[p, :chip_rows].astype(F32) + factor * crossed
        rows = pl.ds(pl.multiple_of(p * chip_rows, chip_rows), chip_rows)
        grad_ref[rows, :] = grad
        std_ref[rows, :] = standard
        return sums[0] + fold(grad), sums[1] + fold(grad * standard)

    zero = jnp.zeros((8, width), F32)
    total, cross = lax.fori_loop(0, n_chip, first, (zero, zero))
    grad_mean = jnp.sum(total, axis=0, keepdims=True) / n_rows
    grad_cross = jnp.sum(cross, axis=0, keepdims=True) / n_rows

    def second(p, carry):
        rows = pl.ds(pl.multiple_of(p * chip_rows, chip_rows), chip_rows)
        out_ref[rows, :] = ((grad_ref[rows, :] - grad_mean - std_ref[rows, :] * grad_cross) * inv).astype(BF16)
        return carry

    lax.fori_loop(0, n_chip, second, 0)


def body(embeds, weight):
    n_chip = lax.axis_size(PLANE)
    n_near, n_far = lax.axis_size("z0"), lax.axis_size("z1")
    n_feat = n_near * n_far
    n_batch = 2 * n_chip
    local_rows, _, d_in = embeds.shape
    chip_rows = 2 * local_rows
    n_rows = local_rows * n_batch
    depth, width_out = weight.shape
    half = width_out // 2
    core = lax.axis_index("core")
    chip = lax.axis_index(PLANE)
    first = core == 0

    def in_core_order(own, other, axis):
        return jnp.concatenate([jnp.where(first, own, other), jnp.where(first, other, own)], axis=axis)

    def swap_core(a):
        return lax.ppermute(a, "core", [(0, 1), (1, 0)])

    with jax.named_scope("embeds_exchange"):
        odd = lax.axis_index("z0") % 2
        one_view = lax.dynamic_index_in_dim(embeds, odd, 1, keepdims=False)
        one_view = one_view.reshape(local_rows, n_batch, depth).transpose(1, 0, 2)
        one_view = exchange(one_view, BATCH).reshape(n_rows, depth)
        weight, one_view = lax.optimization_barrier((weight, one_view))
        other_one = lax.ppermute(one_view, "z0", [(0, 1), (1, 0), (2, 3), (3, 2)])
    with jax.named_scope("weight_gather"):
        first_groups, second_groups = ring_groups()
        row_weight = ring_gather(weight, first_groups)
        core_weight = ring_gather(row_weight, second_groups).reshape(n_chip * depth, width_out)
    with jax.named_scope("embeds_order"):
        by_core = embeds.reshape(local_rows, 2, 4, n_chip // 4, 2, depth)
        rows_zero = by_core[:, :, :, :, 0].transpose(1, 0, 2, 3, 4).reshape(2 * local_rows, n_chip * depth)
        rows_one = by_core[:, :, :, :, 1].transpose(1, 0, 3, 2, 4).reshape(2 * local_rows, n_chip * depth)
        own_rows = jnp.where(first, rows_zero, rows_one)
        other_rows = swap_core(jnp.where(first, rows_one, rows_zero))
    with jax.named_scope("project"):
        own = jnp.dot(own_rows, core_weight, preferred_element_type=F32)
        other = jnp.dot(other_rows, core_weight, preferred_element_type=F32)
        def by_half(p):
            a, b = p[:local_rows], p[local_rows:]
            low = jnp.concatenate([a[:, :half], b[:, :half]], axis=1)
            high = jnp.concatenate([a[:, half:], b[:, half:]], axis=1)
            return jnp.where(first, low, high), jnp.where(first, high, low)

        own_kept, own_sent = by_half(own)
        other_kept, other_sent = by_half(other)
        got_other, got_own = jnp.split(swap_core(jnp.concatenate([own_sent, other_sent])), 2)
        projected = in_core_order(own_kept + got_own, other_kept + got_other, 0)
    with jax.named_scope("project_gather"):
        chip_mean = jnp.sum(projected, axis=0) / chip_rows
        block = jnp.concatenate(
            [(projected - chip_mean).astype(BF16), pad_rows(pieces(chip_mean), width_out)], axis=0
        )
        got = gather(block, PLANE)
    with jax.named_scope("standardize"):
        chip_means = jnp.sum(got[:, chip_rows : chip_rows + 3].astype(F32), axis=1)
        row_mean = jnp.sum(chip_means, axis=0) / n_chip
        shift = chip_means - row_mean
        centered = got[:, :chip_rows].astype(F32) + shift[:, None, :]
        centered = centered.reshape(n_rows, width_out)
        variance = jnp.sum(centered * centered, axis=0) / n_rows
        spread = jnp.sqrt(variance + epsilon)
        inverse = 1.0 / spread
        normed = (centered * inverse).astype(BF16)
        view_a, view_b = normed[:, :half], normed[:, half:]
        float_a, float_b = view_a.astype(F32), view_b.astype(F32)
        diagonal = jnp.sum(float_a * float_b, axis=0) / n_rows
        diag_terms = (1.0 - diagonal) ** 2 - off_weight * diagonal * diagonal
        diag_local = diag_terms[:chip_rows] + diag_terms[chip_rows:]

    with jax.named_scope("gram"):
        mine = lax.dynamic_slice_in_dim(normed, chip * chip_rows, chip_rows, axis=0)
        contract = (((1,), (1,)), ((), ()))
        part_a = lax.dot_general(view_a, mine[:, :half], contract, preferred_element_type=F32)
        part_b = lax.dot_general(view_b, mine[:, half:], contract, preferred_element_type=F32)
        parts = jnp.stack([part_a.astype(BF16), part_b.astype(BF16)])
        extra = pad_rows(pieces(diag_local), chip_rows)
        weight_diag = 2.0 * ((1.0 - off_weight) * diagonal - 1.0)
        factor = loss_scale / n_rows * jnp.concatenate([weight_diag, weight_diag])
        parts, extra, factor, inverse, other_one = lax.optimization_barrier((parts, extra, factor, inverse, other_one))
    with jax.named_scope("gram_core"):
        parts = jnp.sum(exchange(parts, "core").astype(F32), axis=0)
    with jax.named_scope("gram_reduce"):
        parts = parts.astype(BF16).reshape(n_near, n_rows // n_near, chip_rows)
        extra = jnp.broadcast_to(extra[None], (n_near, PAD, chip_rows))
        got_z = exchange(jnp.concatenate([parts, extra], axis=1), "z0")
        summed = jnp.sum(got_z.astype(F32), axis=0)
        extra = pad_rows(pieces(jnp.sum(summed[n_rows // n_near :], axis=0)), chip_rows)
        parts = summed[: n_rows // n_near].astype(BF16).reshape(n_far, n_rows // n_feat, chip_rows)
        extra = jnp.broadcast_to(extra[None], (n_far, PAD, chip_rows))
        got_z = exchange(jnp.concatenate([parts, extra], axis=1), "z1")
        summed = jnp.sum(got_z.astype(F32), axis=0)
        gram_block = summed[: n_rows // n_feat].astype(BF16)
        diag_core = jnp.sum(summed[n_rows // n_feat :], axis=0)
        gram_block, diag_core = lax.optimization_barrier((gram_block, diag_core))
    with jax.named_scope("gram_gather"):
        gram_t = gather(gather(gram_block, "z1"), "z0").reshape(n_rows, chip_rows)
        other_t = swap_core(gram_t)
        gram_a = jnp.where(first, gram_t, other_t).astype(F32)
        gram_b = jnp.where(first, other_t, gram_t).astype(F32)
    with jax.named_scope("back"):
        off_local = jnp.sum(gram_a * gram_b, axis=0)
        back_a = split_product(gram_b, view_a)
        back_b = split_product(gram_a, view_b)
        back = jnp.concatenate([back_a, back_b], axis=1).astype(BF16)
        terms = jnp.concatenate([off_local, jnp.zeros((width_out - chip_rows,), F32)])
        block = jnp.concatenate([back, pad_rows(pieces(terms), width_out)], axis=0)
        block, diag_terms = lax.optimization_barrier((block, diag_core + swap_core(diag_core)))
    with jax.named_scope("back_gather"):
        got_back = gather(block, PLANE)
    with jax.named_scope("grad"):
        off_total = jnp.sum(got_back[:, chip_rows : chip_rows + 3, :chip_rows].astype(F32)) / (n_rows * n_rows)
        diag_total = jnp.sum(diag_terms)
        loss_value = (off_weight * off_total + diag_total) / D_OUT
        scale_off = 2.0 * off_weight / (n_rows * n_rows)
        vmem = pl.BlockSpec(memory_space=pltpu.VMEM)
        grad_proj = pl.pallas_call(
            functools.partial(grad_kernel, n_rows, chip_rows, loss_scale * scale_off),
            out_shape=jax.ShapeDtypeStruct((n_rows, width_out), BF16),
            in_specs=[vmem] * 5,
            out_specs=vmem,
            scratch_shapes=[pltpu.VMEM((n_rows, width_out), F32)] * 2,
            compiler_params=pltpu.CompilerParams(vmem_limit_bytes=32 * 1024 * 1024),
            cost_estimate=pl.CostEstimate(flops=20 * n_rows * width_out, bytes_accessed=8 * n_rows * width_out, transcendentals=0),
            name="grad",
        )(got_back, got, shift, inverse[None], factor[None])
    with jax.named_scope("grad_swap"):
        other_proj = swap_core(grad_proj)
    with jax.named_scope("weight_grad"):
        embeds_a = jnp.where(odd == 0, one_view, other_one)
        embeds_b = jnp.where(odd == 0, other_one, one_view)
        def half_grad(g):
            rows = (((0,), (0,)), ((), ()))
            return lax.dot_general(embeds_a, g[:, :half], rows, preferred_element_type=F32) + lax.dot_general(
                embeds_b, g[:, half:], rows, preferred_element_type=F32
            )
        grad_weight = in_core_order(half_grad(grad_proj), half_grad(other_proj), 1)
    return (loss_value, grad_weight)


def solution(mesh):
    n_batch, n_feat = mesh.devices.shape
    grid = Mesh(mesh.devices.reshape(4, n_batch // 8, 2, n_feat // 4, 4), BATCH + FEAT)
    return jax.shard_map(
        body,
        mesh=grid,
        in_specs=(P(BATCH, None, None), P(BATCH, FEAT)),
        out_specs=(P(), P(BATCH, FEAT)),
        check_vma=False,
    )
```

```python
import functools

import jax
import jax.numpy as jnp
from jax import lax
from jax.experimental import pallas as pl
from jax.experimental.pallas import tpu as pltpu
from jax.sharding import Mesh, PartitionSpec as P

D_OUT = 8192

off_weight = 0.0051
loss_scale = 8.0
epsilon = 1e-05

F32 = jnp.float32
BF16 = jnp.bfloat16
PLANE = ("y", "x")
BATCH = ("y", "x", "core")
FEAT = ("z1", "z0")
PAD = 8


def exchange(blocks, axes):
    return lax.all_to_all(blocks, axes, split_axis=0, concat_axis=0, tiled=True)


def gather(block, axes):
    n = lax.axis_size(axes)
    blocks = jnp.broadcast_to(block[None], (n,) + block.shape)
    return exchange(blocks, axes)


def pieces(value):
    high = lax.reduce_precision(value, 8, 7)
    rest = value - high
    middle = lax.reduce_precision(rest, 8, 7)
    low = rest - middle
    return [high.astype(BF16), middle.astype(BF16), low.astype(BF16)]


def pad_rows(rows, width):
    rows = [r.reshape(1, width) for r in rows]
    return jnp.concatenate(rows + [jnp.zeros((PAD - len(rows), width), BF16)], axis=0)


def split_product(gram_t, view):
    high = gram_t.astype(BF16)
    low = (gram_t - high.astype(F32)).astype(BF16)
    rows = (((0,), (0,)), ((), ()))
    return lax.dot_general(high, view, rows, preferred_element_type=F32) + lax.dot_general(
        low, view, rows, preferred_element_type=F32
    )


def with_rows(main, rows):
    n = main.shape[0]
    index = lax.broadcasted_iota(jnp.int32, (n + PAD, 1), 0)
    main = jnp.pad(main, ((0, PAD), (0, 0)))
    for i, row in enumerate(rows):
        main = jnp.where(index == n + i, row[None, :], main)
    return main


def ring_groups():
    index = lambda y, x, c: (y * 4 + x) * 2 + c
    along_x = lambda c: [[index(y, x, c) for x in range(4)] for y in range(4)]
    along_y = lambda c: [[index(y, x, c) for y in range(4)] for x in range(4)]
    return along_x(0) + along_y(1), along_y(0) + along_x(1)


def ring_gather(block, groups):
    blocks = jnp.broadcast_to(block[None], (4,) + block.shape)
    return lax.all_to_all(blocks, BATCH, split_axis=0, concat_axis=0, tiled=True, axis_index_groups=groups)


def grad_kernel(n_rows, chip_rows, scale, back_ref, got_ref, shift_ref, inv_ref, cross_ref, out_ref, grad_ref, std_ref):
    n_chip, _, width = got_ref.shape
    half = width // 2
    inv, factor = inv_ref[...], cross_ref[...]

    def fold(a):
        return jnp.sum(a.reshape(chip_rows // 8, 8, width), axis=0)

    def first(p, sums):
        centered = got_ref[p, :chip_rows].astype(F32) + shift_ref[pl.ds(p, 1), :]
        standard = centered * inv
        normed = standard.astype(BF16).astype(F32)
        crossed = jnp.concatenate([normed[:, half:], normed[:, :half]], axis=1)
        grad = scale * back_ref[p, :chip_rows].astype(F32) + factor * crossed
        rows = pl.ds(pl.multiple_of(p * chip_rows, chip_rows), chip_rows)
        grad_ref[rows, :] = grad
        std_ref[rows, :] = standard
        return sums[0] + fold(grad), sums[1] + fold(grad * standard)

    zero = jnp.zeros((8, width), F32)
    total, cross = lax.fori_loop(0, n_chip, first, (zero, zero))
    grad_mean = jnp.sum(total, axis=0, keepdims=True) / n_rows
    grad_cross = jnp.sum(cross, axis=0, keepdims=True) / n_rows

    def second(p, carry):
        rows = pl.ds(pl.multiple_of(p * chip_rows, chip_rows), chip_rows)
        out_ref[rows, :] = ((grad_ref[rows, :] - grad_mean - std_ref[rows, :] * grad_cross) * inv).astype(BF16)
        return carry

    lax.fori_loop(0, n_chip, second, 0)


def project_kernel(place_ref, own_ref, other_ref, weight_ref, kept_ref, sent_ref):
    rows = jnp.concatenate([own_ref[...], other_ref[...]], axis=0)
    both = jnp.dot(rows, weight_ref[...], preferred_element_type=F32)
    n, half = both.shape[0] // 4, both.shape[1] // 2
    first = place_ref[0] == 0
    for owner in range(2):
        a = both[2 * owner * n : (2 * owner + 1) * n, :]
        b = both[(2 * owner + 1) * n : (2 * owner + 2) * n, :]
        low = jnp.concatenate([a[:, :half], b[:, :half]], axis=1)
        high = jnp.concatenate([a[:, half:], b[:, half:]], axis=1)
        kept_ref[owner * n : (owner + 1) * n, :] = jnp.where(first, low, high)
        sent_ref[owner * n : (owner + 1) * n, :] = jnp.where(first, high, low)


def half_grad(odd, one_ref, other_ref, grad_ref, store):
    half = grad_ref.shape[1] // 2

    def product(a_ref, b_ref):
        return jnp.dot(a_ref[...], grad_ref[:, :half], preferred_element_type=F32) + jnp.dot(
            b_ref[...], grad_ref[:, half:], preferred_element_type=F32
        )

    @pl.when(odd == 0)
    def _():
        store(product(one_ref, other_ref))

    @pl.when(odd != 0)
    def _():
        store(product(other_ref, one_ref))


def own_half_kernel(place_ref, one_ref, other_ref, grad_ref, out_ref):
    def store(value):
        out_ref[...] = value

    half_grad(place_ref[1], one_ref, other_ref, grad_ref, store)


def other_half_kernel(place_ref, one_ref, other_ref, grad_ref, mine_ref, out_ref):
    first = place_ref[0] == 0
    half = mine_ref.shape[1]

    def store(value):
        mine = mine_ref[...]
        out_ref[:, :half] = jnp.where(first, mine, value)
        out_ref[:, half:] = jnp.where(first, value, mine)

    half_grad(place_ref[1], one_ref, other_ref, grad_ref, store)


def body(embeds, weight):
    n_chip = lax.axis_size(PLANE)
    n_near, n_far = lax.axis_size("z0"), lax.axis_size("z1")
    n_feat = n_near * n_far
    n_batch = 2 * n_chip
    local_rows, _, d_in = embeds.shape
    chip_rows = 2 * local_rows
    n_rows = local_rows * n_batch
    depth, width_out = weight.shape
    half = width_out // 2
    core = lax.axis_index("core")
    chip = lax.axis_index(PLANE)
    first = core == 0

    def in_core_order(own, other, axis):
        return jnp.concatenate([jnp.where(first, own, other), jnp.where(first, other, own)], axis=axis)

    def swap_core(a):
        return lax.ppermute(a, "core", [(0, 1), (1, 0)])

    odd = lax.axis_index("z0") % 2
    place = jnp.stack([core, odd]).astype(jnp.int32)
    vmem = pl.BlockSpec(memory_space=pltpu.VMEM)
    smem = pl.BlockSpec(memory_space=pltpu.SMEM)
    params = pltpu.CompilerParams(vmem_limit_bytes=32 * 1024 * 1024)

    with jax.named_scope("embeds_exchange"):
        by_view = lax.optimization_barrier(embeds.transpose(1, 0, 2).reshape(2 * local_rows, d_in))
        one_view = lax.dynamic_slice_in_dim(by_view, odd * local_rows, local_rows, axis=0)
        one_view = one_view.reshape(local_rows, n_batch, depth).transpose(1, 0, 2)
        one_view = exchange(one_view, BATCH).reshape(n_rows, depth)
        weight, one_view = lax.optimization_barrier((weight, one_view))
        other_one = lax.ppermute(one_view, "z0", [(0, 1), (1, 0), (2, 3), (3, 2)])
    with jax.named_scope("weight_gather"):
        first_groups, second_groups = ring_groups()
        row_weight = ring_gather(weight, first_groups)
        core_weight = ring_gather(row_weight, second_groups).reshape(n_chip * depth, width_out)
    with jax.named_scope("embeds_order"):
        by_core = by_view.reshape(2 * local_rows, 4, n_chip // 4, 2, depth)
        rows_zero = by_core[:, :, :, 0].reshape(2 * local_rows, n_chip * depth)
        rows_one = by_core[:, :, :, 1].transpose(0, 2, 1, 3).reshape(2 * local_rows, n_chip * depth)
        own_rows = jnp.where(first, rows_zero, rows_one)
        other_rows = swap_core(jnp.where(first, rows_one, rows_zero))
    with jax.named_scope("project"):
        kept, sent = pl.pallas_call(
            project_kernel,
            out_shape=[jax.ShapeDtypeStruct((2 * local_rows, width_out), F32)] * 2,
            in_specs=[smem] + [vmem] * 3,
            out_specs=[vmem, vmem],
            compiler_params=params,
            name="project",
        )(place, own_rows, other_rows, core_weight)
        got_other, got_own = jnp.split(swap_core(sent), 2)
        own, other = jnp.split(kept, 2)
        projected = in_core_order(own + got_own, other + got_other, 0)
    with jax.named_scope("project_gather"):
        chip_mean = jnp.sum(projected, axis=0) / chip_rows
        block = with_rows((projected - chip_mean).astype(BF16), pieces(chip_mean))
        got = gather(block, PLANE)
        one_t, other_t = one_view.T, other_one.T
    with jax.named_scope("standardize"):
        chip_means = jnp.sum(got[:, chip_rows : chip_rows + 3].astype(F32), axis=1)
        row_mean = jnp.sum(chip_means, axis=0) / n_chip
        shift = chip_means - row_mean
        centered = got[:, :chip_rows].astype(F32) + shift[:, None, :]
        centered = centered.reshape(n_rows, width_out)
        variance = jnp.sum(centered * centered, axis=0) / n_rows
        spread = jnp.sqrt(variance + epsilon)
        inverse = 1.0 / spread
        normed = (centered * inverse).astype(BF16)
        view_a, view_b = normed[:, :half], normed[:, half:]
        float_a, float_b = view_a.astype(F32), view_b.astype(F32)
        diagonal = jnp.sum(float_a * float_b, axis=0) / n_rows
        diag_terms = (1.0 - diagonal) ** 2 - off_weight * diagonal * diagonal
        diag_local = diag_terms[:chip_rows] + diag_terms[chip_rows:]

    with jax.named_scope("gram"):
        mine = lax.dynamic_slice_in_dim(normed, chip * chip_rows, chip_rows, axis=0)
        contract = (((1,), (1,)), ((), ()))
        part_a = lax.dot_general(view_a, mine[:, :half], contract, preferred_element_type=F32)
        part_b = lax.dot_general(view_b, mine[:, half:], contract, preferred_element_type=F32)
        parts = jnp.stack([part_a.astype(BF16), part_b.astype(BF16)])
        weight_diag = 2.0 * ((1.0 - off_weight) * diagonal - 1.0)
        factor = loss_scale / n_rows * jnp.concatenate([weight_diag, weight_diag])
        parts, diag_local, factor, inverse, one_t, other_t = lax.optimization_barrier(
            (parts, diag_local, factor, inverse, one_t, other_t)
        )
    with jax.named_scope("gram_core"):
        extra = pad_rows(pieces(diag_local + swap_core(diag_local)), chip_rows)
        parts = jnp.sum(exchange(parts, "core").astype(F32), axis=0)
    with jax.named_scope("gram_reduce"):
        parts = parts.astype(BF16).reshape(n_near, n_rows // n_near, chip_rows)
        extra = jnp.broadcast_to(extra[None], (n_near, PAD, chip_rows))
        got_z = exchange(jnp.concatenate([parts, extra], axis=1), "z0")
        summed = jnp.sum(got_z.astype(F32), axis=0)
        extra = pad_rows(pieces(jnp.sum(summed[n_rows // n_near :], axis=0)), chip_rows)
        parts = summed[: n_rows // n_near].astype(BF16).reshape(n_far, n_rows // n_feat, chip_rows)
        extra = jnp.broadcast_to(extra[None], (n_far, PAD, chip_rows))
        got_z = exchange(jnp.concatenate([parts, extra], axis=1), "z1")
        summed = jnp.sum(got_z.astype(F32), axis=0)
        gram_block = summed[: n_rows // n_feat].astype(BF16)
        diag_terms = jnp.sum(summed[n_rows // n_feat :], axis=0)
        gram_block, diag_terms = lax.optimization_barrier((gram_block, diag_terms))
    with jax.named_scope("gram_gather"):
        gram_t = gather(gather(gram_block, "z1"), "z0").reshape(n_rows, chip_rows)
        other_gram = swap_core(gram_t)
        gram_a = jnp.where(first, gram_t, other_gram).astype(F32)
        gram_b = jnp.where(first, other_gram, gram_t).astype(F32)
    with jax.named_scope("back"):
        off_local = jnp.sum(gram_a * gram_b, axis=0)
        back_a = split_product(gram_b, view_a)
        back_b = split_product(gram_a, view_b)
        back = jnp.concatenate([back_a, back_b], axis=1).astype(BF16)
        terms = jnp.concatenate([off_local, jnp.zeros((width_out - chip_rows,), F32)])
        block = with_rows(back, pieces(terms))
    with jax.named_scope("back_gather"):
        got_back = gather(block, PLANE)
    with jax.named_scope("grad"):
        off_total = jnp.sum(got_back[:, chip_rows : chip_rows + 3, :chip_rows].astype(F32)) / (n_rows * n_rows)
        diag_total = jnp.sum(diag_terms)
        loss_value = (off_weight * off_total + diag_total) / D_OUT
        scale_off = 2.0 * off_weight / (n_rows * n_rows)
        grad_proj = pl.pallas_call(
            functools.partial(grad_kernel, n_rows, chip_rows, loss_scale * scale_off),
            out_shape=jax.ShapeDtypeStruct((n_rows, width_out), BF16),
            in_specs=[vmem] * 5,
            out_specs=vmem,
            scratch_shapes=[pltpu.VMEM((n_rows, width_out), F32)] * 2,
            compiler_params=params,
            cost_estimate=pl.CostEstimate(flops=20 * n_rows * width_out, bytes_accessed=8 * n_rows * width_out, transcendentals=0),
            name="grad",
        )(got_back, got, shift, inverse[None], factor[None])
    with jax.named_scope("grad_swap"):
        other_proj = swap_core(grad_proj)
    with jax.named_scope("weight_grad"):
        mine = pl.pallas_call(
            own_half_kernel,
            out_shape=jax.ShapeDtypeStruct((depth, half), F32),
            in_specs=[smem] + [vmem] * 3,
            out_specs=vmem,
            compiler_params=params,
            name="own_half",
        )(place, one_t, other_t, grad_proj)
        grad_weight = pl.pallas_call(
            other_half_kernel,
            out_shape=jax.ShapeDtypeStruct((depth, width_out), F32),
            in_specs=[smem] + [vmem] * 4,
            out_specs=vmem,
            compiler_params=params,
            name="other_half",
        )(place, one_t, other_t, other_proj, mine)
    return (loss_value, grad_weight)


def solution(mesh):
    n_batch, n_feat = mesh.devices.shape
    grid = Mesh(mesh.devices.reshape(4, n_batch // 8, 2, n_feat // 4, 4), BATCH + FEAT)
    return jax.shard_map(
        body,
        mesh=grid,
        in_specs=(P(BATCH, None, None), P(BATCH, FEAT)),
        out_specs=(P(), P(BATCH, FEAT)),
        check_vma=False,
    )
```

```python
import functools

import jax
import jax.numpy as jnp
from jax import lax
from jax.experimental import pallas as pl
from jax.experimental.pallas import tpu as pltpu
from jax.sharding import Mesh, PartitionSpec as P

D_OUT = 8192

off_weight = 0.0051
loss_scale = 8.0
epsilon = 1e-05

F32 = jnp.float32
BF16 = jnp.bfloat16
PLANE = ("y", "x")
BATCH = ("y", "x", "core")
FEAT = ("z1", "z0")
PAD = 8


def exchange(blocks, axes):
    return lax.all_to_all(blocks, axes, split_axis=0, concat_axis=0, tiled=True)


def gather(block, axes):
    n = lax.axis_size(axes)
    blocks = jnp.broadcast_to(block[None], (n,) + block.shape)
    return exchange(blocks, axes)


def pieces(value):
    high = lax.reduce_precision(value, 8, 7)
    rest = value - high
    middle = lax.reduce_precision(rest, 8, 7)
    low = rest - middle
    return [high.astype(BF16), middle.astype(BF16), low.astype(BF16)]


def pad_rows(rows, width):
    rows = [r.reshape(1, width) for r in rows]
    return jnp.concatenate(rows + [jnp.zeros((PAD - len(rows), width), BF16)], axis=0)


def split_product(gram_t, view):
    high = gram_t.astype(BF16)
    low = (gram_t - high.astype(F32)).astype(BF16)
    rows = (((0,), (0,)), ((), ()))
    return lax.dot_general(high, view, rows, preferred_element_type=F32) + lax.dot_general(
        low, view, rows, preferred_element_type=F32
    )


def with_rows(main, rows):
    n = main.shape[0]
    index = lax.broadcasted_iota(jnp.int32, (n + PAD, 1), 0)
    main = jnp.pad(main, ((0, PAD), (0, 0)))
    for i, row in enumerate(rows):
        main = jnp.where(index == n + i, row[None, :], main)
    return main


def ring_groups():
    index = lambda y, x, c: (y * 4 + x) * 2 + c
    along_x = lambda c: [[index(y, x, c) for x in range(4)] for y in range(4)]
    along_y = lambda c: [[index(y, x, c) for y in range(4)] for x in range(4)]
    return along_x(0) + along_y(1), along_y(0) + along_x(1)


def ring_gather(block, groups):
    blocks = jnp.broadcast_to(block[None], (4,) + block.shape)
    return lax.all_to_all(blocks, BATCH, split_axis=0, concat_axis=0, tiled=True, axis_index_groups=groups)


def grad_kernel(n_rows, chip_rows, scale, back_ref, got_ref, shift_ref, inv_ref, cross_ref, diag_ref, out_ref, loss_ref, grad_ref, std_ref):
    n_chip, _, width = got_ref.shape
    half = width // 2
    inv, factor = inv_ref[...], cross_ref[...]

    def fold(a):
        return jnp.sum(a.reshape(chip_rows // 8, 8, width), axis=0)

    def first(p, sums):
        centered = got_ref[p, :chip_rows].astype(F32) + shift_ref[pl.ds(p, 1), :]
        standard = centered * inv
        normed = standard.astype(BF16).astype(F32)
        crossed = jnp.concatenate([normed[:, half:], normed[:, :half]], axis=1)
        grad = scale * back_ref[p, :chip_rows].astype(F32) + factor * crossed
        rows = pl.ds(pl.multiple_of(p * chip_rows, chip_rows), chip_rows)
        grad_ref[rows, :] = grad
        std_ref[rows, :] = standard
        return sums[0] + fold(grad), sums[1] + fold(grad * standard)

    off_terms = jnp.zeros((1, chip_rows), F32)
    for p in range(n_chip):
        spare = back_ref[p, chip_rows:, :chip_rows].astype(F32)
        off_terms = off_terms + jnp.sum(spare, axis=0, keepdims=True)
    loss_ref[0] = jnp.sum(off_weight / (n_rows * n_rows) * off_terms + diag_ref[...]) / D_OUT

    zero = jnp.zeros((8, width), F32)
    total, cross = lax.fori_loop(0, n_chip, first, (zero, zero))
    grad_mean = jnp.sum(total, axis=0, keepdims=True) / n_rows
    grad_cross = jnp.sum(cross, axis=0, keepdims=True) / n_rows

    def second(p, carry):
        rows = pl.ds(pl.multiple_of(p * chip_rows, chip_rows), chip_rows)
        out_ref[rows, :] = ((grad_ref[rows, :] - grad_mean - std_ref[rows, :] * grad_cross) * inv).astype(BF16)
        return carry

    lax.fori_loop(0, n_chip, second, 0)


def order_kernel(place_ref, rows_ref, own_ref, sent_ref):
    depth = rows_ref.shape[1] // 32

    def pick(core, out_ref):
        for j in range(16):
            chip = j if core == 0 else (j % 4) * 4 + j // 4
            source = (2 * chip + core) * depth
            out_ref[:, j * depth : (j + 1) * depth] = rows_ref[:, source : source + depth]

    @pl.when(place_ref[0] == 0)
    def _():
        pick(0, own_ref)
        pick(1, sent_ref)

    @pl.when(place_ref[0] != 0)
    def _():
        pick(1, own_ref)
        pick(0, sent_ref)


def project_kernel(place_ref, own_ref, other_ref, weight_ref, kept_ref, sent_ref):
    rows = jnp.concatenate([own_ref[...], other_ref[...]], axis=0)
    both = jnp.dot(rows, weight_ref[...], preferred_element_type=F32)
    n, half = both.shape[0] // 4, both.shape[1] // 2
    first = place_ref[0] == 0
    for owner in range(2):
        a = both[2 * owner * n : (2 * owner + 1) * n, :]
        b = both[(2 * owner + 1) * n : (2 * owner + 2) * n, :]
        low = jnp.concatenate([a[:, :half], b[:, :half]], axis=1)
        high = jnp.concatenate([a[:, half:], b[:, half:]], axis=1)
        kept_ref[owner * n : (owner + 1) * n, :] = jnp.where(first, low, high)
        sent_ref[owner * n : (owner + 1) * n, :] = jnp.where(first, high, low)


def half_grad(odd, one_ref, other_ref, grad_ref, store):
    half = grad_ref.shape[1] // 2

    def product(a_ref, b_ref):
        return jnp.dot(a_ref[...], grad_ref[:, :half], preferred_element_type=F32) + jnp.dot(
            b_ref[...], grad_ref[:, half:], preferred_element_type=F32
        )

    @pl.when(odd == 0)
    def _():
        store(product(one_ref, other_ref))

    @pl.when(odd != 0)
    def _():
        store(product(other_ref, one_ref))


def own_half_kernel(place_ref, one_ref, other_ref, grad_ref, out_ref):
    def store(value):
        out_ref[...] = value

    half_grad(place_ref[1], one_ref, other_ref, grad_ref, store)


def other_half_kernel(place_ref, one_ref, other_ref, grad_ref, mine_ref, out_ref):
    first = place_ref[0] == 0
    half = mine_ref.shape[1]

    def store(value):
        mine = mine_ref[...]
        out_ref[:, :half] = jnp.where(first, mine, value)
        out_ref[:, half:] = jnp.where(first, value, mine)

    half_grad(place_ref[1], one_ref, other_ref, grad_ref, store)


def body(embeds, weight):
    n_chip = lax.axis_size(PLANE)
    n_near, n_far = lax.axis_size("z0"), lax.axis_size("z1")
    n_feat = n_near * n_far
    n_batch = 2 * n_chip
    local_rows, _, d_in = embeds.shape
    chip_rows = 2 * local_rows
    n_rows = local_rows * n_batch
    depth, width_out = weight.shape
    half = width_out // 2
    core = lax.axis_index("core")
    chip = lax.axis_index(PLANE)
    first = core == 0

    def in_core_order(own, other, axis):
        return jnp.concatenate([jnp.where(first, own, other), jnp.where(first, other, own)], axis=axis)

    def swap_core(a):
        return lax.ppermute(a, "core", [(0, 1), (1, 0)])

    odd = lax.axis_index("z0") % 2
    place = jnp.stack([core, odd]).astype(jnp.int32)
    vmem = pl.BlockSpec(memory_space=pltpu.VMEM)
    smem = pl.BlockSpec(memory_space=pltpu.SMEM)
    params = pltpu.CompilerParams(vmem_limit_bytes=32 * 1024 * 1024)

    with jax.named_scope("embeds_exchange"):
        by_view = lax.optimization_barrier(embeds.transpose(1, 0, 2).reshape(2 * local_rows, d_in))
        upper = lax.axis_index("z0") // 2
        part = local_rows // 2
        quarter = lax.dynamic_slice_in_dim(by_view, (2 * odd + upper) * part, part, axis=0)
        quarter = quarter.reshape(part, n_batch, depth).transpose(1, 0, 2)
        quarter = exchange(quarter, BATCH)
    with jax.named_scope("embeds_order"):
        own_rows, sent_rows = pl.pallas_call(
            order_kernel,
            out_shape=[jax.ShapeDtypeStruct((2 * local_rows, n_chip * depth), BF16)] * 2,
            in_specs=[smem, vmem],
            out_specs=[vmem, vmem],
            compiler_params=params,
            name="order",
        )(place, by_view)
        other_rows = swap_core(sent_rows)
    with jax.named_scope("weight_gather"):
        weight, quarter, own_rows, other_rows = lax.optimization_barrier((weight, quarter, own_rows, other_rows))
        first_groups, second_groups = ring_groups()
        row_weight = ring_gather(weight, first_groups)
        core_weight = ring_gather(row_weight, second_groups).reshape(n_chip * depth, width_out)
    with jax.named_scope("project"):
        kept, sent = pl.pallas_call(
            project_kernel,
            out_shape=[jax.ShapeDtypeStruct((2 * local_rows, width_out), F32)] * 2,
            in_specs=[smem] + [vmem] * 3,
            out_specs=[vmem, vmem],
            compiler_params=params,
            name="project",
        )(place, own_rows, other_rows, core_weight)
        got_other, got_own = jnp.split(swap_core(sent), 2)
        own, other = jnp.split(kept, 2)
        projected = in_core_order(own + got_own, other + got_other, 0)
    with jax.named_scope("project_gather"):
        chip_mean = jnp.sum(projected, axis=0) / chip_rows
        block = with_rows((projected - chip_mean).astype(BF16), pieces(chip_mean))
        block, quarter = lax.optimization_barrier((block, quarter))
        other_quarter = lax.ppermute(quarter, "z0", [(0, 2), (2, 0), (1, 3), (3, 1)])
        got = gather(block, PLANE)
    with jax.named_scope("standardize"):
        chip_means = jnp.sum(got[:, chip_rows : chip_rows + 3].astype(F32), axis=1)
        row_mean = jnp.sum(chip_means, axis=0) / n_chip
        shift = chip_means - row_mean
        centered = got[:, :chip_rows].astype(F32) + shift[:, None, :]
        centered = centered.reshape(n_rows, width_out)
        variance = jnp.sum(centered * centered, axis=0) / n_rows
        spread = jnp.sqrt(variance + epsilon)
        inverse = 1.0 / spread
        normed = (centered * inverse).astype(BF16)
        view_a, view_b = normed[:, :half], normed[:, half:]
        float_a, float_b = view_a.astype(F32), view_b.astype(F32)
        diagonal = jnp.sum(float_a * float_b, axis=0) / n_rows
        diag_terms = (1.0 - diagonal) ** 2 - off_weight * diagonal * diagonal
        diag_local = diag_terms[:chip_rows] + diag_terms[chip_rows:]

    with jax.named_scope("gram"):
        mine = lax.dynamic_slice_in_dim(normed, chip * chip_rows, chip_rows, axis=0)
        contract = (((1,), (1,)), ((), ()))
        part_a = lax.dot_general(view_a, mine[:, :half], contract, preferred_element_type=F32)
        part_b = lax.dot_general(view_b, mine[:, half:], contract, preferred_element_type=F32)
        parts = jnp.stack([part_a.astype(BF16), part_b.astype(BF16)])
        weight_diag = 2.0 * ((1.0 - off_weight) * diagonal - 1.0)
        factor = loss_scale / n_rows * jnp.concatenate([weight_diag, weight_diag])
        parts, diag_local, factor, inverse, other_quarter = lax.optimization_barrier(
            (parts, diag_local, factor, inverse, other_quarter)
        )
    with jax.named_scope("gram_core"):
        extra = pad_rows(pieces(diag_local + swap_core(diag_local)), chip_rows)
        parts = jnp.sum(exchange(parts, "core").astype(F32), axis=0)
    with jax.named_scope("gram_reduce"):
        parts = parts.astype(BF16).reshape(n_near, n_rows // n_near, chip_rows)
        extra = jnp.broadcast_to(extra[None], (n_near, PAD, chip_rows))
        got_z = exchange(jnp.concatenate([parts, extra], axis=1), "z0")
        summed = jnp.sum(got_z.astype(F32), axis=0)
        extra = pad_rows(pieces(jnp.sum(summed[n_rows // n_near :], axis=0)), chip_rows)
        parts = summed[: n_rows // n_near].astype(BF16).reshape(n_far, n_rows // n_feat, chip_rows)
        extra = jnp.broadcast_to(extra[None], (n_far, PAD, chip_rows))
        got_z = exchange(jnp.concatenate([parts, extra], axis=1), "z1")
        summed = jnp.sum(got_z.astype(F32), axis=0)
        gram_block = summed[: n_rows // n_feat].astype(BF16)
        diag_terms = jnp.sum(summed[n_rows // n_feat :], axis=0)
        gram_block, diag_terms = lax.optimization_barrier((gram_block, diag_terms))
    with jax.named_scope("gram_gather"):
        gram_t = gather(gather(gram_block, "z1"), "z0").reshape(n_rows, chip_rows)
        other_gram = swap_core(gram_t)
        gram_a = jnp.where(first, gram_t, other_gram).astype(F32)
        gram_b = jnp.where(first, other_gram, gram_t).astype(F32)
    with jax.named_scope("back"):
        off_local = jnp.sum(gram_a * gram_b, axis=0)
        back_a = split_product(gram_b, view_a)
        back_b = split_product(gram_a, view_b)
        back = jnp.concatenate([back_a, back_b], axis=1).astype(BF16)
        terms = jnp.concatenate([off_local, jnp.zeros((width_out - chip_rows,), F32)])
        block = with_rows(back, pieces(terms))
    with jax.named_scope("back_gather"):
        block, quarter, other_quarter = lax.optimization_barrier((block, quarter, other_quarter))
        low = jnp.where(upper == 0, quarter, other_quarter)
        high = jnp.where(upper == 0, other_quarter, quarter)
        one_t = jnp.concatenate([low, high], axis=1).reshape(n_rows, depth).T
        other_t = lax.ppermute(one_t, "z0", [(0, 1), (1, 0), (2, 3), (3, 2)])
        got_back = gather(block, PLANE)
        got_back, one_t, other_t = lax.optimization_barrier((got_back, one_t, other_t))
    with jax.named_scope("grad"):
        scale_off = 2.0 * off_weight / (n_rows * n_rows)
        grad_proj, loss = pl.pallas_call(
            functools.partial(grad_kernel, n_rows, chip_rows, loss_scale * scale_off),
            out_shape=[jax.ShapeDtypeStruct((n_rows, width_out), BF16), jax.ShapeDtypeStruct((1,), F32)],
            in_specs=[vmem] * 6,
            out_specs=[vmem, smem],
            scratch_shapes=[pltpu.VMEM((n_rows, width_out), F32)] * 2,
            compiler_params=params,
            cost_estimate=pl.CostEstimate(flops=20 * n_rows * width_out, bytes_accessed=8 * n_rows * width_out, transcendentals=0),
            name="grad",
        )(got_back, got, shift, inverse[None], factor[None], diag_terms[None])
        loss_value = loss[0]
    with jax.named_scope("grad_swap"):
        other_proj = swap_core(grad_proj)
    with jax.named_scope("weight_grad"):
        mine = pl.pallas_call(
            own_half_kernel,
            out_shape=jax.ShapeDtypeStruct((depth, half), F32),
            in_specs=[smem] + [vmem] * 3,
            out_specs=vmem,
            compiler_params=params,
            name="own_half",
        )(place, one_t, other_t, grad_proj)
        grad_weight = pl.pallas_call(
            other_half_kernel,
            out_shape=jax.ShapeDtypeStruct((depth, width_out), F32),
            in_specs=[smem] + [vmem] * 4,
            out_specs=vmem,
            compiler_params=params,
            name="other_half",
        )(place, one_t, other_t, other_proj, mine)
    return (loss_value, grad_weight)


def solution(mesh):
    n_batch, n_feat = mesh.devices.shape
    grid = Mesh(mesh.devices.reshape(4, n_batch // 8, 2, n_feat // 4, 4), BATCH + FEAT)
    return jax.shard_map(
        body,
        mesh=grid,
        in_specs=(P(BATCH, None, None), P(BATCH, FEAT)),
        out_specs=(P(), P(BATCH, FEAT)),
        check_vma=False,
    )
```

```python
import functools

import jax
import jax.numpy as jnp
from jax import lax
from jax.experimental import pallas as pl
from jax.experimental.pallas import tpu as pltpu
from jax.sharding import Mesh, PartitionSpec as P

D_OUT = 8192

off_weight = 0.0051
loss_scale = 8.0
epsilon = 1e-05

F32 = jnp.float32
BF16 = jnp.bfloat16
PLANE = ("y", "x")
BATCH = ("y", "x", "core")
FEAT = ("z1", "z0")
PAD = 8


def exchange(blocks, axes):
    return lax.all_to_all(blocks, axes, split_axis=0, concat_axis=0, tiled=True)


def gather(block, axes):
    n = lax.axis_size(axes)
    blocks = jnp.broadcast_to(block[None], (n,) + block.shape)
    return exchange(blocks, axes)


def pieces(value):
    high = lax.reduce_precision(value, 8, 7)
    rest = value - high
    middle = lax.reduce_precision(rest, 8, 7)
    low = rest - middle
    return [high.astype(BF16), middle.astype(BF16), low.astype(BF16)]


def pad_rows(rows, width):
    rows = [r.reshape(1, width) for r in rows]
    return jnp.concatenate(rows + [jnp.zeros((PAD - len(rows), width), BF16)], axis=0)


def split_product(gram_t, view):
    high = gram_t.astype(BF16)
    low = (gram_t - high.astype(F32)).astype(BF16)
    rows = (((0,), (0,)), ((), ()))
    return lax.dot_general(high, view, rows, preferred_element_type=F32) + lax.dot_general(
        low, view, rows, preferred_element_type=F32
    )


def with_rows(main, rows):
    n = main.shape[0]
    index = lax.broadcasted_iota(jnp.int32, (n + PAD, 1), 0)
    main = jnp.pad(main, ((0, PAD), (0, 0)))
    for i, row in enumerate(rows):
        main = jnp.where(index == n + i, row[None, :], main)
    return main


def ring_groups():
    index = lambda y, x, c: (y * 4 + x) * 2 + c
    along_x = lambda c: [[index(y, x, c) for x in range(4)] for y in range(4)]
    along_y = lambda c: [[index(y, x, c) for y in range(4)] for x in range(4)]
    return along_x(0) + along_y(1), along_y(0) + along_x(1)


def ring_gather(block, groups):
    blocks = jnp.broadcast_to(block[None], (4,) + block.shape)
    return lax.all_to_all(blocks, BATCH, split_axis=0, concat_axis=0, tiled=True, axis_index_groups=groups)


def grad_kernel(n_rows, chip_rows, scale, back_ref, got_ref, shift_ref, inv_ref, cross_ref, diag_ref, out_ref, grad_ref, std_ref):
    n_chip, _, width = got_ref.shape
    half = width // 2
    inv, factor = inv_ref[...], cross_ref[...]

    def fold(a):
        return jnp.sum(a.reshape(chip_rows // 8, 8, width), axis=0)

    def first(p, sums):
        centered = got_ref[p, :chip_rows].astype(F32) + shift_ref[pl.ds(p, 1), :]
        standard = centered * inv
        normed = standard.astype(BF16).astype(F32)
        crossed = jnp.concatenate([normed[:, half:], normed[:, :half]], axis=1)
        grad = scale * back_ref[p, :chip_rows].astype(F32) + factor * crossed
        rows = pl.ds(pl.multiple_of(p * chip_rows, chip_rows), chip_rows)
        grad_ref[rows, :] = grad
        std_ref[rows, :] = standard
        return sums[0] + fold(grad), sums[1] + fold(grad * standard)

    diag = diag_ref[...]
    high = diag.astype(BF16).astype(F32)
    middle = (diag - high).astype(BF16).astype(F32)
    row = lax.broadcasted_iota(jnp.int32, (16, chip_rows), 0)
    terms = jnp.where(row == 0, high, jnp.where(row == 1, middle, jnp.where(row == 2, diag - high - middle, 0.0)))
    out_ref[n_rows:, :] = jnp.concatenate([terms, jnp.zeros((16, width - chip_rows), F32)], axis=1).astype(BF16)

    zero = jnp.zeros((8, width), F32)
    total, cross = lax.fori_loop(0, n_chip, first, (zero, zero))
    grad_mean = jnp.sum(total, axis=0, keepdims=True) / n_rows
    grad_cross = jnp.sum(cross, axis=0, keepdims=True) / n_rows

    def second(p, carry):
        rows = pl.ds(pl.multiple_of(p * chip_rows, chip_rows), chip_rows)
        out_ref[rows, :] = ((grad_ref[rows, :] - grad_mean - std_ref[rows, :] * grad_cross) * inv).astype(BF16)
        return carry

    lax.fori_loop(0, n_chip, second, 0)


def order_kernel(place_ref, rows_ref, own_ref, sent_ref):
    depth = rows_ref.shape[1] // 32

    def pick(core, out_ref):
        for j in range(16):
            chip = j if core == 0 else (j % 4) * 4 + j // 4
            source = (2 * chip + core) * depth
            out_ref[:, j * depth : (j + 1) * depth] = rows_ref[:, source : source + depth]

    @pl.when(place_ref[0] == 0)
    def _():
        pick(0, own_ref)
        pick(1, sent_ref)

    @pl.when(place_ref[0] != 0)
    def _():
        pick(1, own_ref)
        pick(0, sent_ref)


def project_kernel(place_ref, own_ref, other_ref, weight_ref, kept_ref, sent_ref):
    rows = jnp.concatenate([own_ref[...], other_ref[...]], axis=0)
    both = jnp.dot(rows, weight_ref[...], preferred_element_type=F32)
    n, half = both.shape[0] // 4, both.shape[1] // 2
    first = place_ref[0] == 0
    for owner in range(2):
        a = both[2 * owner * n : (2 * owner + 1) * n, :]
        b = both[(2 * owner + 1) * n : (2 * owner + 2) * n, :]
        low = jnp.concatenate([a[:, :half], b[:, :half]], axis=1)
        high = jnp.concatenate([a[:, half:], b[:, half:]], axis=1)
        kept_ref[owner * n : (owner + 1) * n, :] = jnp.where(first, low, high)
        sent_ref[owner * n : (owner + 1) * n, :] = jnp.where(first, high, low)


def half_grad(odd, one_ref, other_ref, grad_ref, store):
    rows, half = one_ref.shape[1], grad_ref.shape[1] // 2

    def product(a_ref, b_ref):
        return jnp.dot(a_ref[...], grad_ref[:rows, :half], preferred_element_type=F32) + jnp.dot(
            b_ref[...], grad_ref[:rows, half:], preferred_element_type=F32
        )

    @pl.when(odd == 0)
    def _():
        store(product(one_ref, other_ref))

    @pl.when(odd != 0)
    def _():
        store(product(other_ref, one_ref))


def own_half_kernel(place_ref, one_ref, other_ref, grad_ref, out_ref):
    def store(value):
        out_ref[...] = value

    half_grad(place_ref[1], one_ref, other_ref, grad_ref, store)


def other_half_kernel(off_factor, place_ref, one_ref, other_ref, grad_ref, mine_ref, off_ref, diag_ref, out_ref, loss_ref):
    first = place_ref[0] == 0
    rows, terms = one_ref.shape[1], diag_ref.shape[1]
    other_diag = jnp.sum(grad_ref[rows:, :terms].astype(F32), axis=0, keepdims=True)
    loss_ref[0] = jnp.sum(off_factor * off_ref[...] + diag_ref[...] + other_diag) / D_OUT
    half = mine_ref.shape[1]

    def store(value):
        mine = mine_ref[...]
        out_ref[:, :half] = jnp.where(first, mine, value)
        out_ref[:, half:] = jnp.where(first, value, mine)

    half_grad(place_ref[1], one_ref, other_ref, grad_ref, store)


def body(embeds, weight):
    n_chip = lax.axis_size(PLANE)
    n_near, n_far = lax.axis_size("z0"), lax.axis_size("z1")
    n_feat = n_near * n_far
    n_batch = 2 * n_chip
    local_rows, _, d_in = embeds.shape
    chip_rows = 2 * local_rows
    n_rows = local_rows * n_batch
    depth, width_out = weight.shape
    half = width_out // 2
    core = lax.axis_index("core")
    chip = lax.axis_index(PLANE)
    first = core == 0

    def in_core_order(own, other, axis):
        return jnp.concatenate([jnp.where(first, own, other), jnp.where(first, other, own)], axis=axis)

    def swap_core(a):
        return lax.ppermute(a, "core", [(0, 1), (1, 0)])

    odd = lax.axis_index("z0") % 2
    place = jnp.stack([core, odd]).astype(jnp.int32)
    vmem = pl.BlockSpec(memory_space=pltpu.VMEM)
    smem = pl.BlockSpec(memory_space=pltpu.SMEM)
    params = pltpu.CompilerParams(vmem_limit_bytes=32 * 1024 * 1024)

    with jax.named_scope("embeds_exchange"):
        by_view = lax.optimization_barrier(embeds.transpose(1, 0, 2).reshape(2 * local_rows, d_in))
        one_view = lax.dynamic_slice_in_dim(by_view, odd * local_rows, local_rows, axis=0)
        one_view = one_view.reshape(local_rows, n_batch, depth).transpose(1, 0, 2)
        one_view = exchange(one_view, BATCH).reshape(n_rows, depth)
    with jax.named_scope("embeds_order"):
        own_rows, sent_rows = pl.pallas_call(
            order_kernel,
            out_shape=[jax.ShapeDtypeStruct((2 * local_rows, n_chip * depth), BF16)] * 2,
            in_specs=[smem, vmem],
            out_specs=[vmem, vmem],
            compiler_params=params,
            name="order",
        )(place, by_view)
        other_rows = swap_core(sent_rows)
    with jax.named_scope("weight_gather"):
        weight, one_view, own_rows, other_rows = lax.optimization_barrier((weight, one_view, own_rows, other_rows))
        first_groups, second_groups = ring_groups()
        row_weight = ring_gather(weight, first_groups)
        core_weight = ring_gather(row_weight, second_groups).reshape(n_chip * depth, width_out)
    with jax.named_scope("project"):
        kept, sent = pl.pallas_call(
            project_kernel,
            out_shape=[jax.ShapeDtypeStruct((2 * local_rows, width_out), F32)] * 2,
            in_specs=[smem] + [vmem] * 3,
            out_specs=[vmem, vmem],
            compiler_params=params,
            name="project",
        )(place, own_rows, other_rows, core_weight)
        got_other, got_own = jnp.split(swap_core(sent), 2)
        own, other = jnp.split(kept, 2)
        projected = in_core_order(own + got_own, other + got_other, 0)
    with jax.named_scope("project_gather"):
        chip_mean = jnp.sum(projected, axis=0) / chip_rows
        block = with_rows((projected - chip_mean).astype(BF16), pieces(chip_mean))
        block, one_view = lax.optimization_barrier((block, one_view))
        one_t = one_view.T
        other_t = lax.ppermute(one_t, "z0", [(0, 1), (1, 0), (2, 3), (3, 2)])
        got = gather(block, PLANE)
    with jax.named_scope("standardize"):
        chip_means = jnp.sum(got[:, chip_rows : chip_rows + 3].astype(F32), axis=1)
        row_mean = jnp.sum(chip_means, axis=0) / n_chip
        shift = chip_means - row_mean
        centered = got[:, :chip_rows].astype(F32) + shift[:, None, :]
        centered = centered.reshape(n_rows, width_out)
        variance = jnp.sum(centered * centered, axis=0) / n_rows
        spread = jnp.sqrt(variance + epsilon)
        inverse = 1.0 / spread
        normed = (centered * inverse).astype(BF16)
        view_a, view_b = normed[:, :half], normed[:, half:]
        float_a, float_b = view_a.astype(F32), view_b.astype(F32)
        diagonal = jnp.sum(float_a * float_b, axis=0) / n_rows
        diag_terms = (1.0 - diagonal) ** 2 - off_weight * diagonal * diagonal
        diag_local = diag_terms[:chip_rows] + diag_terms[chip_rows:]

    with jax.named_scope("gram"):
        def partial(view):
            mine = lax.dynamic_slice_in_dim(view, chip * chip_rows, chip_rows, axis=0)
            return lax.dot_general(view, mine, (((1,), (1,)), ((), ())), preferred_element_type=F32)

        sent = partial(jnp.where(first, view_b, view_a)).astype(BF16)
        kept = partial(jnp.where(first, view_a, view_b))
        weight_diag = 2.0 * ((1.0 - off_weight) * diagonal - 1.0)
        factor = loss_scale / n_rows * jnp.concatenate([weight_diag, weight_diag])
        sent, kept, diag_local, factor, inverse, one_t, other_t = lax.optimization_barrier(
            (sent, kept, diag_local, factor, inverse, one_t, other_t)
        )
    with jax.named_scope("gram_core"):
        extra = pad_rows(pieces(diag_local), chip_rows)
        parts = kept + swap_core(sent).astype(F32)
    with jax.named_scope("gram_reduce"):
        parts = parts.astype(BF16).reshape(n_near, n_rows // n_near, chip_rows)
        extra = jnp.broadcast_to(extra[None], (n_near, PAD, chip_rows))
        got_z = exchange(jnp.concatenate([parts, extra], axis=1), "z0")
        summed = jnp.sum(got_z.astype(F32), axis=0)
        extra = pad_rows(pieces(jnp.sum(summed[n_rows // n_near :], axis=0)), chip_rows)
        parts = summed[: n_rows // n_near].astype(BF16).reshape(n_far, n_rows // n_feat, chip_rows)
        extra = jnp.broadcast_to(extra[None], (n_far, PAD, chip_rows))
        got_z = exchange(jnp.concatenate([parts, extra], axis=1), "z1")
        summed = jnp.sum(got_z.astype(F32), axis=0)
        gram_block = summed[: n_rows // n_feat].astype(BF16)
        diag_terms = jnp.sum(summed[n_rows // n_feat :], axis=0)
        gram_block, diag_terms = lax.optimization_barrier((gram_block, diag_terms))
    with jax.named_scope("gram_gather"):
        gram_t = gather(gather(gram_block, "z1"), "z0").reshape(n_rows, chip_rows)
        other_gram = swap_core(gram_t)
        gram_a = jnp.where(first, gram_t, other_gram).astype(F32)
        gram_b = jnp.where(first, other_gram, gram_t).astype(F32)
    with jax.named_scope("back"):
        off_local = jnp.sum(gram_a * gram_b, axis=0)
        back_a = split_product(gram_b, view_a)
        back_b = split_product(gram_a, view_b)
        back = jnp.concatenate([back_a, back_b], axis=1).astype(BF16)
        terms = jnp.concatenate([off_local, jnp.zeros((width_out - chip_rows,), F32)])
        block = with_rows(back, pieces(terms))
    with jax.named_scope("back_gather"):
        got_back = gather(block, PLANE)
    with jax.named_scope("grad"):
        scale_off = 2.0 * off_weight / (n_rows * n_rows)
        off_terms = jnp.sum(got_back[:, chip_rows:, :chip_rows].astype(F32), axis=(0, 1))[None]
        grad_proj = pl.pallas_call(
            functools.partial(grad_kernel, n_rows, chip_rows, loss_scale * scale_off),
            out_shape=jax.ShapeDtypeStruct((n_rows + 16, width_out), BF16),
            in_specs=[vmem] * 6,
            out_specs=vmem,
            scratch_shapes=[pltpu.VMEM((n_rows, width_out), F32)] * 2,
            compiler_params=params,
            cost_estimate=pl.CostEstimate(flops=20 * n_rows * width_out, bytes_accessed=8 * n_rows * width_out, transcendentals=0),
            name="grad",
        )(got_back, got, shift, inverse[None], factor[None], diag_terms[None])
    with jax.named_scope("grad_swap"):
        other_proj = swap_core(grad_proj)
    with jax.named_scope("weight_grad"):
        mine = pl.pallas_call(
            own_half_kernel,
            out_shape=jax.ShapeDtypeStruct((depth, half), F32),
            in_specs=[smem] + [vmem] * 3,
            out_specs=vmem,
            compiler_params=params,
            name="own_half",
        )(place, one_t, other_t, grad_proj)
        grad_weight, loss = pl.pallas_call(
            functools.partial(other_half_kernel, off_weight / (n_rows * n_rows)),
            out_shape=[jax.ShapeDtypeStruct((depth, width_out), F32), jax.ShapeDtypeStruct((1,), F32)],
            in_specs=[smem] + [vmem] * 6,
            out_specs=[vmem, smem],
            compiler_params=params,
            name="other_half",
        )(place, one_t, other_t, other_proj, mine, off_terms, diag_terms[None])
    return (loss[0], grad_weight)


def solution(mesh):
    n_batch, n_feat = mesh.devices.shape
    grid = Mesh(mesh.devices.reshape(4, n_batch // 8, 2, n_feat // 4, 4), BATCH + FEAT)
    return jax.shard_map(
        body,
        mesh=grid,
        in_specs=(P(BATCH, None, None), P(BATCH, FEAT)),
        out_specs=(P(), P(BATCH, FEAT)),
        check_vma=False,
    )
```

```python
import functools

import jax
import jax.numpy as jnp
from jax import lax
from jax.experimental import pallas as pl
from jax.experimental.pallas import tpu as pltpu
from jax.sharding import Mesh, PartitionSpec as P

D_OUT = 8192

off_weight = 0.0051
loss_scale = 8.0
epsilon = 1e-05

F32 = jnp.float32
BF16 = jnp.bfloat16
PLANE = ("y", "x")
BATCH = ("y", "x", "core")
FEAT = ("z1", "z0")
PAD = 8


def exchange(blocks, axes):
    return lax.all_to_all(blocks, axes, split_axis=0, concat_axis=0, tiled=True)


def gather(block, axes):
    n = lax.axis_size(axes)
    blocks = jnp.broadcast_to(block[None], (n,) + block.shape)
    return exchange(blocks, axes)


def pieces(value):
    high = lax.reduce_precision(value, 8, 7)
    rest = value - high
    middle = lax.reduce_precision(rest, 8, 7)
    low = rest - middle
    return [high.astype(BF16), middle.astype(BF16), low.astype(BF16)]


def pad_rows(rows, width):
    rows = [r.reshape(1, width) for r in rows]
    return jnp.concatenate(rows + [jnp.zeros((PAD - len(rows), width), BF16)], axis=0)


def split_product(gram_t, view):
    high = gram_t.astype(BF16)
    low = (gram_t - high.astype(F32)).astype(BF16)
    rows = (((0,), (0,)), ((), ()))
    return lax.dot_general(high, view, rows, preferred_element_type=F32) + lax.dot_general(
        low, view, rows, preferred_element_type=F32
    )


def with_rows(main, rows):
    n = main.shape[0]
    index = lax.broadcasted_iota(jnp.int32, (n + PAD, 1), 0)
    main = jnp.pad(main, ((0, PAD), (0, 0)))
    for i, row in enumerate(rows):
        main = jnp.where(index == n + i, row[None, :], main)
    return main


def ring_groups():
    index = lambda y, x, c: (y * 4 + x) * 2 + c
    along_x = lambda c: [[index(y, x, c) for x in range(4)] for y in range(4)]
    along_y = lambda c: [[index(y, x, c) for y in range(4)] for x in range(4)]
    return along_x(0) + along_y(1), along_y(0) + along_x(1)


def ring_gather(block, groups):
    blocks = jnp.broadcast_to(block[None], (4,) + block.shape)
    return lax.all_to_all(blocks, BATCH, split_axis=0, concat_axis=0, tiled=True, axis_index_groups=groups)


def grad_kernel(n_rows, chip_rows, scale, back_ref, got_ref, shift_ref, inv_ref, cross_ref, diag_ref, out_ref, grad_ref, std_ref):
    n_chip, _, width = got_ref.shape
    half = width // 2
    inv, factor = inv_ref[...], cross_ref[...]

    def fold(a):
        return jnp.sum(a.reshape(chip_rows // 8, 8, width), axis=0)

    def first(p, sums):
        centered = got_ref[p, :chip_rows].astype(F32) + shift_ref[pl.ds(p, 1), :]
        standard = centered * inv
        normed = standard.astype(BF16).astype(F32)
        crossed = jnp.concatenate([normed[:, half:], normed[:, :half]], axis=1)
        grad = scale * back_ref[p, :chip_rows].astype(F32) + factor * crossed
        rows = pl.ds(pl.multiple_of(p * chip_rows, chip_rows), chip_rows)
        grad_ref[rows, :] = grad
        std_ref[rows, :] = standard
        return sums[0] + fold(grad), sums[1] + fold(grad * standard)

    diag = diag_ref[...]
    high = diag.astype(BF16).astype(F32)
    middle = (diag - high).astype(BF16).astype(F32)
    row = lax.broadcasted_iota(jnp.int32, (16, chip_rows), 0)
    terms = jnp.where(row == 0, high, jnp.where(row == 1, middle, jnp.where(row == 2, diag - high - middle, 0.0)))
    out_ref[n_rows:, :] = jnp.concatenate([terms, jnp.zeros((16, width - chip_rows), F32)], axis=1).astype(BF16)

    zero = jnp.zeros((8, width), F32)
    total, cross = lax.fori_loop(0, n_chip, first, (zero, zero))
    grad_mean = jnp.sum(total, axis=0, keepdims=True) / n_rows
    grad_cross = jnp.sum(cross, axis=0, keepdims=True) / n_rows

    def second(p, carry):
        rows = pl.ds(pl.multiple_of(p * chip_rows, chip_rows), chip_rows)
        out_ref[rows, :] = ((grad_ref[rows, :] - grad_mean - std_ref[rows, :] * grad_cross) * inv).astype(BF16)
        return carry

    lax.fori_loop(0, n_chip, second, 0)


def order_kernel(place_ref, rows_ref, own_ref, sent_ref):
    depth = rows_ref.shape[1] // 32

    def pick(core, out_ref):
        for j in range(16):
            chip = j if core == 0 else (j % 4) * 4 + j // 4
            source = (2 * chip + core) * depth
            out_ref[:, j * depth : (j + 1) * depth] = rows_ref[:, source : source + depth]

    @pl.when(place_ref[0] == 0)
    def _():
        pick(0, own_ref)
        pick(1, sent_ref)

    @pl.when(place_ref[0] != 0)
    def _():
        pick(1, own_ref)
        pick(0, sent_ref)


def project_kernel(place_ref, own_ref, other_ref, weight_ref, kept_ref, sent_ref):
    rows = jnp.concatenate([own_ref[...], other_ref[...]], axis=0)
    both = jnp.dot(rows, weight_ref[...], preferred_element_type=F32)
    n, half = both.shape[0] // 4, both.shape[1] // 2
    first = place_ref[0] == 0
    for owner in range(2):
        a = both[2 * owner * n : (2 * owner + 1) * n, :]
        b = both[(2 * owner + 1) * n : (2 * owner + 2) * n, :]
        low = jnp.concatenate([a[:, :half], b[:, :half]], axis=1)
        high = jnp.concatenate([a[:, half:], b[:, half:]], axis=1)
        kept_ref[owner * n : (owner + 1) * n, :] = jnp.where(first, low, high)
        sent_ref[owner * n : (owner + 1) * n, :] = jnp.where(first, high, low)


def half_grad(odd, one_ref, other_ref, grad_ref, store):
    rows, half = one_ref.shape[1], grad_ref.shape[1] // 2

    def product(a_ref, b_ref):
        return jnp.dot(a_ref[...], grad_ref[:rows, :half], preferred_element_type=F32) + jnp.dot(
            b_ref[...], grad_ref[:rows, half:], preferred_element_type=F32
        )

    @pl.when(odd == 0)
    def _():
        store(product(one_ref, other_ref))

    @pl.when(odd != 0)
    def _():
        store(product(other_ref, one_ref))


def own_half_kernel(place_ref, one_ref, other_ref, grad_ref, out_ref):
    def store(value):
        out_ref[...] = value

    half_grad(place_ref[1], one_ref, other_ref, grad_ref, store)


def other_half_kernel(off_factor, place_ref, one_ref, other_ref, grad_ref, mine_ref, off_ref, diag_ref, out_ref, loss_ref):
    first = place_ref[0] == 0
    rows, terms = one_ref.shape[1], diag_ref.shape[1]
    other_diag = jnp.sum(grad_ref[rows:, :terms].astype(F32), axis=0, keepdims=True)
    loss_ref[0] = jnp.sum(off_factor * off_ref[...] + diag_ref[...] + other_diag) / D_OUT
    half = mine_ref.shape[1]

    def store(value):
        mine = mine_ref[...]
        out_ref[:, :half] = jnp.where(first, mine, value)
        out_ref[:, half:] = jnp.where(first, value, mine)

    half_grad(place_ref[1], one_ref, other_ref, grad_ref, store)


def body(embeds, weight):
    n_chip = lax.axis_size(PLANE)
    n_near, n_far = lax.axis_size("z0"), lax.axis_size("z1")
    n_feat = n_near * n_far
    n_batch = 2 * n_chip
    local_rows, _, d_in = embeds.shape
    chip_rows = 2 * local_rows
    n_rows = local_rows * n_batch
    depth, width_out = weight.shape
    half = width_out // 2
    core = lax.axis_index("core")
    chip = lax.axis_index(PLANE)
    first = core == 0

    def in_core_order(own, other, axis):
        return jnp.concatenate([jnp.where(first, own, other), jnp.where(first, other, own)], axis=axis)

    def swap_core(a):
        return lax.ppermute(a, "core", [(0, 1), (1, 0)])

    odd = lax.axis_index("z0") % 2
    place = jnp.stack([core, odd]).astype(jnp.int32)
    vmem = pl.BlockSpec(memory_space=pltpu.VMEM)
    smem = pl.BlockSpec(memory_space=pltpu.SMEM)
    params = pltpu.CompilerParams(vmem_limit_bytes=32 * 1024 * 1024)

    with jax.named_scope("embeds_exchange"):
        by_view = lax.optimization_barrier(embeds.transpose(1, 0, 2).reshape(2 * local_rows, d_in))
        one_view = lax.dynamic_slice_in_dim(by_view, odd * local_rows, local_rows, axis=0)
        one_view = one_view.reshape(local_rows, n_batch, depth).transpose(1, 0, 2)
    with jax.named_scope("embeds_order"):
        own_rows, sent_rows = pl.pallas_call(
            order_kernel,
            out_shape=[jax.ShapeDtypeStruct((2 * local_rows, n_chip * depth), BF16)] * 2,
            in_specs=[smem, vmem],
            out_specs=[vmem, vmem],
            compiler_params=params,
            name="order",
        )(place, by_view)
    with jax.named_scope("weight_gather"):
        first_groups, second_groups = ring_groups()
        row_weight = ring_gather(weight, first_groups)
        row_weight, one_view, own_rows, sent_rows = lax.optimization_barrier((row_weight, one_view, own_rows, sent_rows))
        core_weight = ring_gather(row_weight, second_groups).reshape(n_chip * depth, width_out)
        core_weight, one_view, sent_rows = lax.optimization_barrier((core_weight, one_view, sent_rows))
        one_view = exchange(one_view, BATCH).reshape(n_rows, depth)
        other_rows = swap_core(sent_rows)
    with jax.named_scope("project"):
        kept, sent = pl.pallas_call(
            project_kernel,
            out_shape=[jax.ShapeDtypeStruct((2 * local_rows, width_out), F32)] * 2,
            in_specs=[smem] + [vmem] * 3,
            out_specs=[vmem, vmem],
            compiler_params=params,
            name="project",
        )(place, own_rows, other_rows, core_weight)
        kept, sent, one_view = lax.optimization_barrier((kept, sent, one_view))
        got_other, got_own = jnp.split(swap_core(sent), 2)
        own, other = jnp.split(kept, 2)
        projected = in_core_order(own + got_own, other + got_other, 0)
    with jax.named_scope("project_gather"):
        chip_mean = jnp.sum(projected, axis=0) / chip_rows
        block = with_rows((projected - chip_mean).astype(BF16), pieces(chip_mean))
        block, one_view = lax.optimization_barrier((block, one_view))
        one_t = one_view.T
        other_t = lax.ppermute(one_t, "z0", [(0, 1), (1, 0), (2, 3), (3, 2)])
        got = gather(block, PLANE)
    with jax.named_scope("standardize"):
        chip_means = jnp.sum(got[:, chip_rows : chip_rows + 3].astype(F32), axis=1)
        row_mean = jnp.sum(chip_means, axis=0) / n_chip
        shift = chip_means - row_mean
        centered = got[:, :chip_rows].astype(F32) + shift[:, None, :]
        centered = centered.reshape(n_rows, width_out)
        variance = jnp.sum(centered * centered, axis=0) / n_rows
        spread = jnp.sqrt(variance + epsilon)
        inverse = 1.0 / spread
        normed = (centered * inverse).astype(BF16)
        view_a, view_b = normed[:, :half], normed[:, half:]
        float_a, float_b = view_a.astype(F32), view_b.astype(F32)
        diagonal = jnp.sum(float_a * float_b, axis=0) / n_rows
        diag_terms = (1.0 - diagonal) ** 2 - off_weight * diagonal * diagonal
        diag_local = diag_terms[:chip_rows] + diag_terms[chip_rows:]

    with jax.named_scope("gram"):
        def partial(view):
            mine = lax.dynamic_slice_in_dim(view, chip * chip_rows, chip_rows, axis=0)
            return lax.dot_general(view, mine, (((1,), (1,)), ((), ())), preferred_element_type=F32)

        sent = partial(jnp.where(first, view_b, view_a)).astype(BF16)
        kept = partial(jnp.where(first, view_a, view_b))
        weight_diag = 2.0 * ((1.0 - off_weight) * diagonal - 1.0)
        factor = loss_scale / n_rows * jnp.concatenate([weight_diag, weight_diag])
        sent, kept, diag_local, factor, inverse, one_t, other_t = lax.optimization_barrier(
            (sent, kept, diag_local, factor, inverse, one_t, other_t)
        )
    with jax.named_scope("gram_core"):
        extra = pad_rows(pieces(diag_local), chip_rows)
        parts = kept + swap_core(sent).astype(F32)
    with jax.named_scope("gram_reduce"):
        parts = parts.astype(BF16).reshape(n_near, n_rows // n_near, chip_rows)
        extra = jnp.broadcast_to(extra[None], (n_near, PAD, chip_rows))
        got_z = exchange(jnp.concatenate([parts, extra], axis=1), "z0")
        summed = jnp.sum(got_z.astype(F32), axis=0)
        extra = pad_rows(pieces(jnp.sum(summed[n_rows // n_near :], axis=0)), chip_rows)
        parts = summed[: n_rows // n_near].astype(BF16).reshape(n_far, n_rows // n_feat, chip_rows)
        extra = jnp.broadcast_to(extra[None], (n_far, PAD, chip_rows))
        got_z = exchange(jnp.concatenate([parts, extra], axis=1), "z1")
        summed = jnp.sum(got_z.astype(F32), axis=0)
        gram_block = summed[: n_rows // n_feat].astype(BF16)
        diag_terms = jnp.sum(summed[n_rows // n_feat :], axis=0)
        gram_block, diag_terms = lax.optimization_barrier((gram_block, diag_terms))
    with jax.named_scope("gram_gather"):
        gram_t = gather(gather(gram_block, "z1"), "z0").reshape(n_rows, chip_rows)
        other_gram = swap_core(gram_t)
        gram_a = jnp.where(first, gram_t, other_gram).astype(F32)
        gram_b = jnp.where(first, other_gram, gram_t).astype(F32)
    with jax.named_scope("back"):
        off_local = jnp.sum(gram_a * gram_b, axis=0)
        back_a = split_product(gram_b, view_a)
        back_b = split_product(gram_a, view_b)
        back = jnp.concatenate([back_a, back_b], axis=1).astype(BF16)
        terms = jnp.concatenate([off_local, jnp.zeros((width_out - chip_rows,), F32)])
        block = with_rows(back, pieces(terms))
    with jax.named_scope("back_gather"):
        got_back = gather(block, PLANE)
    with jax.named_scope("grad"):
        scale_off = 2.0 * off_weight / (n_rows * n_rows)
        off_terms = jnp.sum(got_back[:, chip_rows:, :chip_rows].astype(F32), axis=(0, 1))[None]
        grad_proj = pl.pallas_call(
            functools.partial(grad_kernel, n_rows, chip_rows, loss_scale * scale_off),
            out_shape=jax.ShapeDtypeStruct((n_rows + 16, width_out), BF16),
            in_specs=[vmem] * 6,
            out_specs=vmem,
            scratch_shapes=[pltpu.VMEM((n_rows, width_out), F32)] * 2,
            compiler_params=params,
            cost_estimate=pl.CostEstimate(flops=20 * n_rows * width_out, bytes_accessed=8 * n_rows * width_out, transcendentals=0),
            name="grad",
        )(got_back, got, shift, inverse[None], factor[None], diag_terms[None])
    with jax.named_scope("grad_swap"):
        other_proj = swap_core(grad_proj)
    with jax.named_scope("weight_grad"):
        mine = pl.pallas_call(
            own_half_kernel,
            out_shape=jax.ShapeDtypeStruct((depth, half), F32),
            in_specs=[smem] + [vmem] * 3,
            out_specs=vmem,
            compiler_params=params,
            name="own_half",
        )(place, one_t, other_t, grad_proj)
        grad_weight, loss = pl.pallas_call(
            functools.partial(other_half_kernel, off_weight / (n_rows * n_rows)),
            out_shape=[jax.ShapeDtypeStruct((depth, width_out), F32), jax.ShapeDtypeStruct((1,), F32)],
            in_specs=[smem] + [vmem] * 6,
            out_specs=[vmem, smem],
            compiler_params=params,
            name="other_half",
        )(place, one_t, other_t, other_proj, mine, off_terms, diag_terms[None])
    return (loss[0], grad_weight)


def solution(mesh):
    n_batch, n_feat = mesh.devices.shape
    grid = Mesh(mesh.devices.reshape(4, n_batch // 8, 2, n_feat // 4, 4), BATCH + FEAT)
    return jax.shard_map(
        body,
        mesh=grid,
        in_specs=(P(BATCH, None, None), P(BATCH, FEAT)),
        out_specs=(P(), P(BATCH, FEAT)),
        check_vma=False,
    )
```

```python
import functools

import jax
import jax.numpy as jnp
from jax import lax
from jax.experimental import pallas as pl
from jax.experimental.pallas import tpu as pltpu
from jax.sharding import Mesh, PartitionSpec as P

D_OUT = 8192

off_weight = 0.0051
loss_scale = 8.0
epsilon = 1e-05

F32 = jnp.float32
BF16 = jnp.bfloat16
PLANE = ("y", "x")
BATCH = ("y", "x", "core")
FEAT = ("z1", "z0")
PAD = 8


def exchange(blocks, axes):
    return lax.all_to_all(blocks, axes, split_axis=0, concat_axis=0, tiled=True)


def gather(block, axes):
    n = lax.axis_size(axes)
    blocks = jnp.broadcast_to(block[None], (n,) + block.shape)
    return exchange(blocks, axes)


def pieces(value):
    high = lax.reduce_precision(value, 8, 7)
    rest = value - high
    middle = lax.reduce_precision(rest, 8, 7)
    low = rest - middle
    return [high.astype(BF16), middle.astype(BF16), low.astype(BF16)]


def pad_rows(rows, width):
    rows = [r.reshape(1, width) for r in rows]
    return jnp.concatenate(rows + [jnp.zeros((PAD - len(rows), width), BF16)], axis=0)


def split_product(gram_t, view):
    high = gram_t.astype(BF16)
    low = (gram_t - high.astype(F32)).astype(BF16)
    rows = (((0,), (0,)), ((), ()))
    return lax.dot_general(high, view, rows, preferred_element_type=F32) + lax.dot_general(
        low, view, rows, preferred_element_type=F32
    )


def with_rows(main, rows):
    n = main.shape[0]
    index = lax.broadcasted_iota(jnp.int32, (n + PAD, 1), 0)
    main = jnp.pad(main, ((0, PAD), (0, 0)))
    for i, row in enumerate(rows):
        main = jnp.where(index == n + i, row[None, :], main)
    return main


def ring_groups():
    index = lambda y, x, c: (y * 4 + x) * 2 + c
    along_x = lambda c: [[index(y, x, c) for x in range(4)] for y in range(4)]
    along_y = lambda c: [[index(y, x, c) for y in range(4)] for x in range(4)]
    return along_x(0) + along_y(1), along_y(0) + along_x(1)


def ring_gather(block, groups):
    blocks = jnp.broadcast_to(block[None], (4,) + block.shape)
    return lax.all_to_all(blocks, BATCH, split_axis=0, concat_axis=0, tiled=True, axis_index_groups=groups)


def grad_kernel(n_rows, chip_rows, scale, back_ref, got_ref, shift_ref, inv_ref, cross_ref, diag_ref, out_ref, grad_ref, std_ref):
    n_chip, _, width = got_ref.shape
    half = width // 2
    inv, factor = inv_ref[...], cross_ref[...]

    def fold(a):
        return jnp.sum(a.reshape(chip_rows // 8, 8, width), axis=0)

    def first(p, sums):
        centered = got_ref[p, :chip_rows].astype(F32) + shift_ref[pl.ds(p, 1), :]
        standard = centered * inv
        normed = standard.astype(BF16).astype(F32)
        crossed = jnp.concatenate([normed[:, half:], normed[:, :half]], axis=1)
        grad = scale * back_ref[p, :chip_rows].astype(F32) + factor * crossed
        rows = pl.ds(pl.multiple_of(p * chip_rows, chip_rows), chip_rows)
        grad_ref[rows, :] = grad
        std_ref[rows, :] = standard
        return sums[0] + fold(grad), sums[1] + fold(grad * standard)

    diag = diag_ref[...]
    high = diag.astype(BF16).astype(F32)
    middle = (diag - high).astype(BF16).astype(F32)
    row = lax.broadcasted_iota(jnp.int32, (16, chip_rows), 0)
    terms = jnp.where(row == 0, high, jnp.where(row == 1, middle, jnp.where(row == 2, diag - high - middle, 0.0)))
    out_ref[n_rows:, :] = jnp.concatenate([terms, jnp.zeros((16, width - chip_rows), F32)], axis=1).astype(BF16)

    zero = jnp.zeros((8, width), F32)
    total, cross = lax.fori_loop(0, n_chip, first, (zero, zero))
    grad_mean = jnp.sum(total, axis=0, keepdims=True) / n_rows
    grad_cross = jnp.sum(cross, axis=0, keepdims=True) / n_rows

    def second(p, carry):
        rows = pl.ds(pl.multiple_of(p * chip_rows, chip_rows), chip_rows)
        out_ref[rows, :] = ((grad_ref[rows, :] - grad_mean - std_ref[rows, :] * grad_cross) * inv).astype(BF16)
        return carry

    lax.fori_loop(0, n_chip, second, 0)


def order_kernel(place_ref, rows_ref, own_ref, sent_ref, view_ref):
    n, width = rows_ref.shape
    depth = width // 32

    def blocks(view):
        for j in range(32):
            view_ref[j] = rows_ref[view * n // 2 : (view + 1) * n // 2, j * depth : (j + 1) * depth]

    @pl.when(place_ref[1] == 0)
    def _():
        blocks(0)

    @pl.when(place_ref[1] != 0)
    def _():
        blocks(1)

    def pick(core, out_ref):
        for j in range(16):
            chip = j if core == 0 else (j % 4) * 4 + j // 4
            source = (2 * chip + core) * depth
            out_ref[:, j * depth : (j + 1) * depth] = rows_ref[:, source : source + depth]

    @pl.when(place_ref[0] == 0)
    def _():
        pick(0, own_ref)
        pick(1, sent_ref)

    @pl.when(place_ref[0] != 0)
    def _():
        pick(1, own_ref)
        pick(0, sent_ref)


def project_kernel(place_ref, own_ref, other_ref, weight_ref, kept_ref, sent_ref):
    rows = jnp.concatenate([own_ref[...], other_ref[...]], axis=0)
    both = jnp.dot(rows, weight_ref[...], preferred_element_type=F32)
    n, half = both.shape[0] // 4, both.shape[1] // 2
    first = place_ref[0] == 0
    for owner in range(2):
        a = both[2 * owner * n : (2 * owner + 1) * n, :]
        b = both[(2 * owner + 1) * n : (2 * owner + 2) * n, :]
        low = jnp.concatenate([a[:, :half], b[:, :half]], axis=1)
        high = jnp.concatenate([a[:, half:], b[:, half:]], axis=1)
        kept_ref[owner * n : (owner + 1) * n, :] = jnp.where(first, low, high)
        sent_ref[owner * n : (owner + 1) * n, :] = jnp.where(first, high, low)


def half_grad(odd, one_ref, other_ref, grad_ref, store):
    rows, half = one_ref.shape[1], grad_ref.shape[1] // 2

    def product(a_ref, b_ref):
        return jnp.dot(a_ref[...], grad_ref[:rows, :half], preferred_element_type=F32) + jnp.dot(
            b_ref[...], grad_ref[:rows, half:], preferred_element_type=F32
        )

    @pl.when(odd == 0)
    def _():
        store(product(one_ref, other_ref))

    @pl.when(odd != 0)
    def _():
        store(product(other_ref, one_ref))


def own_half_kernel(place_ref, one_ref, other_ref, grad_ref, out_ref):
    def store(value):
        out_ref[...] = value

    half_grad(place_ref[1], one_ref, other_ref, grad_ref, store)


def other_half_kernel(off_factor, place_ref, one_ref, other_ref, grad_ref, mine_ref, off_ref, diag_ref, out_ref, loss_ref):
    first = place_ref[0] == 0
    rows, terms = one_ref.shape[1], diag_ref.shape[1]
    other_diag = jnp.sum(grad_ref[rows:, :terms].astype(F32), axis=0, keepdims=True)
    loss_ref[0] = jnp.sum(off_factor * off_ref[...] + diag_ref[...] + other_diag) / D_OUT
    half = mine_ref.shape[1]

    def store(value):
        mine = mine_ref[...]
        out_ref[:, :half] = jnp.where(first, mine, value)
        out_ref[:, half:] = jnp.where(first, value, mine)

    half_grad(place_ref[1], one_ref, other_ref, grad_ref, store)


def body(embeds, weight):
    n_chip = lax.axis_size(PLANE)
    n_near, n_far = lax.axis_size("z0"), lax.axis_size("z1")
    n_feat = n_near * n_far
    n_batch = 2 * n_chip
    local_rows, _, d_in = embeds.shape
    chip_rows = 2 * local_rows
    n_rows = local_rows * n_batch
    depth, width_out = weight.shape
    half = width_out // 2
    core = lax.axis_index("core")
    chip = lax.axis_index(PLANE)
    first = core == 0

    def in_core_order(own, other, axis):
        return jnp.concatenate([jnp.where(first, own, other), jnp.where(first, other, own)], axis=axis)

    def swap_core(a):
        return lax.ppermute(a, "core", [(0, 1), (1, 0)])

    odd = lax.axis_index("z0") % 2
    place = jnp.stack([core, odd]).astype(jnp.int32)
    vmem = pl.BlockSpec(memory_space=pltpu.VMEM)
    smem = pl.BlockSpec(memory_space=pltpu.SMEM)
    params = pltpu.CompilerParams(vmem_limit_bytes=32 * 1024 * 1024)

    with jax.named_scope("embeds_exchange"):
        by_view = lax.optimization_barrier(embeds.transpose(1, 0, 2).reshape(2 * local_rows, d_in))
    with jax.named_scope("embeds_order"):
        own_rows, sent_rows, one_view = pl.pallas_call(
            order_kernel,
            out_shape=[jax.ShapeDtypeStruct((2 * local_rows, n_chip * depth), BF16)] * 2
            + [jax.ShapeDtypeStruct((n_batch, local_rows, depth), BF16)],
            in_specs=[smem, vmem],
            out_specs=[vmem] * 3,
            compiler_params=params,
            name="order",
        )(place, by_view)
    with jax.named_scope("weight_gather"):
        first_groups, second_groups = ring_groups()
        row_weight = ring_gather(weight, first_groups)
        row_weight, one_view, own_rows, sent_rows = lax.optimization_barrier((row_weight, one_view, own_rows, sent_rows))
        core_weight = ring_gather(row_weight, second_groups).reshape(n_chip * depth, width_out)
        core_weight, one_view, sent_rows = lax.optimization_barrier((core_weight, one_view, sent_rows))
        one_view = exchange(one_view, BATCH).reshape(n_rows, depth)
        other_rows = swap_core(sent_rows)
    with jax.named_scope("project"):
        kept, sent = pl.pallas_call(
            project_kernel,
            out_shape=[jax.ShapeDtypeStruct((2 * local_rows, width_out), F32)] * 2,
            in_specs=[smem] + [vmem] * 3,
            out_specs=[vmem, vmem],
            compiler_params=params,
            name="project",
        )(place, own_rows, other_rows, core_weight)
        kept, sent, one_view = lax.optimization_barrier((kept, sent, one_view))
        got_other, got_own = jnp.split(swap_core(sent), 2)
        own, other = jnp.split(kept, 2)
        projected = in_core_order(own + got_own, other + got_other, 0)
    with jax.named_scope("project_gather"):
        chip_mean = jnp.sum(projected, axis=0) / chip_rows
        block = with_rows((projected - chip_mean).astype(BF16), pieces(chip_mean))
        block, one_view = lax.optimization_barrier((block, one_view))
        one_t = one_view.T
        other_t = lax.ppermute(one_t, "z0", [(0, 1), (1, 0), (2, 3), (3, 2)])
        got = gather(block, PLANE)
    with jax.named_scope("standardize"):
        chip_means = jnp.sum(got[:, chip_rows : chip_rows + 3].astype(F32), axis=1)
        row_mean = jnp.sum(chip_means, axis=0) / n_chip
        shift = chip_means - row_mean
        centered = got[:, :chip_rows].astype(F32) + shift[:, None, :]
        centered = centered.reshape(n_rows, width_out)
        variance = jnp.sum(centered * centered, axis=0) / n_rows
        spread = jnp.sqrt(variance + epsilon)
        inverse = 1.0 / spread
        normed = (centered * inverse).astype(BF16)
        view_a, view_b = normed[:, :half], normed[:, half:]
        float_a, float_b = view_a.astype(F32), view_b.astype(F32)
        diagonal = jnp.sum(float_a * float_b, axis=0) / n_rows
        diag_terms = (1.0 - diagonal) ** 2 - off_weight * diagonal * diagonal
        diag_local = diag_terms[:chip_rows] + diag_terms[chip_rows:]

    with jax.named_scope("gram"):
        def partial(view):
            mine = lax.dynamic_slice_in_dim(view, chip * chip_rows, chip_rows, axis=0)
            return lax.dot_general(view, mine, (((1,), (1,)), ((), ())), preferred_element_type=F32)

        sent = partial(jnp.where(first, view_b, view_a)).astype(BF16)
        kept = partial(jnp.where(first, view_a, view_b))
        weight_diag = 2.0 * ((1.0 - off_weight) * diagonal - 1.0)
        factor = loss_scale / n_rows * jnp.concatenate([weight_diag, weight_diag])
        sent, kept, diag_local, factor, inverse, one_t, other_t = lax.optimization_barrier(
            (sent, kept, diag_local, factor, inverse, one_t, other_t)
        )
    with jax.named_scope("gram_core"):
        extra = pad_rows(pieces(diag_local), chip_rows)
        parts = kept + swap_core(sent).astype(F32)
    with jax.named_scope("gram_reduce"):
        parts = parts.astype(BF16).reshape(n_near, n_rows // n_near, chip_rows)
        extra = jnp.broadcast_to(extra[None], (n_near, PAD, chip_rows))
        got_z = exchange(jnp.concatenate([parts, extra], axis=1), "z0")
        summed = jnp.sum(got_z.astype(F32), axis=0)
        extra = pad_rows(pieces(jnp.sum(summed[n_rows // n_near :], axis=0)), chip_rows)
        parts = summed[: n_rows // n_near].astype(BF16).reshape(n_far, n_rows // n_feat, chip_rows)
        extra = jnp.broadcast_to(extra[None], (n_far, PAD, chip_rows))
        got_z = exchange(jnp.concatenate([parts, extra], axis=1), "z1")
        summed = jnp.sum(got_z.astype(F32), axis=0)
        gram_block = summed[: n_rows // n_feat].astype(BF16)
        diag_terms = jnp.sum(summed[n_rows // n_feat :], axis=0)
        gram_block, diag_terms = lax.optimization_barrier((gram_block, diag_terms))
    with jax.named_scope("gram_gather"):
        gram_t = gather(gather(gram_block, "z1"), "z0").reshape(n_rows, chip_rows)
        other_gram = swap_core(gram_t)
    with jax.named_scope("back"):
        own_gram, other_gram = gram_t.astype(F32), other_gram.astype(F32)
        with_own = split_product(own_gram, jnp.where(first, view_b, view_a))
        with_other = split_product(other_gram, jnp.where(first, view_a, view_b))
        off_local = jnp.sum(own_gram * other_gram, axis=0)
        back = in_core_order(with_other, with_own, 1).astype(BF16)
        terms = jnp.concatenate([off_local, jnp.zeros((width_out - chip_rows,), F32)])
        block = with_rows(back, pieces(terms))
    with jax.named_scope("back_gather"):
        got_back = gather(block, PLANE)
    with jax.named_scope("grad"):
        scale_off = 2.0 * off_weight / (n_rows * n_rows)
        off_terms = jnp.sum(got_back[:, chip_rows:, :chip_rows].astype(F32), axis=(0, 1))[None]
        grad_proj = pl.pallas_call(
            functools.partial(grad_kernel, n_rows, chip_rows, loss_scale * scale_off),
            out_shape=jax.ShapeDtypeStruct((n_rows + 16, width_out), BF16),
            in_specs=[vmem] * 6,
            out_specs=vmem,
            scratch_shapes=[pltpu.VMEM((n_rows, width_out), F32)] * 2,
            compiler_params=params,
            cost_estimate=pl.CostEstimate(flops=20 * n_rows * width_out, bytes_accessed=8 * n_rows * width_out, transcendentals=0),
            name="grad",
        )(got_back, got, shift, inverse[None], factor[None], diag_terms[None])
    with jax.named_scope("grad_swap"):
        other_proj = swap_core(grad_proj)
    with jax.named_scope("weight_grad"):
        mine = pl.pallas_call(
            own_half_kernel,
            out_shape=jax.ShapeDtypeStruct((depth, half), F32),
            in_specs=[smem] + [vmem] * 3,
            out_specs=vmem,
            compiler_params=params,
            name="own_half",
        )(place, one_t, other_t, grad_proj)
        grad_weight, loss = pl.pallas_call(
            functools.partial(other_half_kernel, off_weight / (n_rows * n_rows)),
            out_shape=[jax.ShapeDtypeStruct((depth, width_out), F32), jax.ShapeDtypeStruct((1,), F32)],
            in_specs=[smem] + [vmem] * 6,
            out_specs=[vmem, smem],
            compiler_params=params,
            name="other_half",
        )(place, one_t, other_t, other_proj, mine, off_terms, diag_terms[None])
    return (loss[0], grad_weight)


def solution(mesh):
    n_batch, n_feat = mesh.devices.shape
    grid = Mesh(mesh.devices.reshape(4, n_batch // 8, 2, n_feat // 4, 4), BATCH + FEAT)
    return jax.shard_map(
        body,
        mesh=grid,
        in_specs=(P(BATCH, None, None), P(BATCH, FEAT)),
        out_specs=(P(), P(BATCH, FEAT)),
        check_vma=False,
    )
```

```python
import functools

import jax
import jax.numpy as jnp
from jax import lax
from jax.experimental import pallas as pl
from jax.experimental.pallas import tpu as pltpu
from jax.sharding import Mesh, PartitionSpec as P

D_OUT = 8192

off_weight = 0.0051
loss_scale = 8.0
epsilon = 1e-05

F32 = jnp.float32
BF16 = jnp.bfloat16
PLANE = ("y", "x")
BATCH = ("y", "x", "core")
FEAT = ("z1", "z0")
PAD = 8


def exchange(blocks, axes):
    return lax.all_to_all(blocks, axes, split_axis=0, concat_axis=0, tiled=True)


def gather(block, axes):
    n = lax.axis_size(axes)
    blocks = jnp.broadcast_to(block[None], (n,) + block.shape)
    return exchange(blocks, axes)


def pieces(value):
    high = lax.reduce_precision(value, 8, 7)
    rest = value - high
    middle = lax.reduce_precision(rest, 8, 7)
    low = rest - middle
    return [high.astype(BF16), middle.astype(BF16), low.astype(BF16)]


def pad_rows(rows, width):
    rows = [r.reshape(1, width) for r in rows]
    return jnp.concatenate(rows + [jnp.zeros((PAD - len(rows), width), BF16)], axis=0)


def split_product(gram_t, view):
    high = gram_t.astype(BF16)
    low = (gram_t - high.astype(F32)).astype(BF16)
    rows = (((0,), (0,)), ((), ()))
    return lax.dot_general(high, view, rows, preferred_element_type=F32) + lax.dot_general(
        low, view, rows, preferred_element_type=F32
    )


def with_rows(main, rows):
    n = main.shape[0]
    index = lax.broadcasted_iota(jnp.int32, (n + PAD, 1), 0)
    main = jnp.pad(main, ((0, PAD), (0, 0)))
    for i, row in enumerate(rows):
        main = jnp.where(index == n + i, row[None, :], main)
    return main


def ring_groups():
    index = lambda y, x, c: (y * 4 + x) * 2 + c
    along_x = lambda c: [[index(y, x, c) for x in range(4)] for y in range(4)]
    along_y = lambda c: [[index(y, x, c) for y in range(4)] for x in range(4)]
    return along_x(0) + along_y(1), along_y(0) + along_x(1)


def ring_gather(block, groups):
    blocks = jnp.broadcast_to(block[None], (4,) + block.shape)
    return lax.all_to_all(blocks, BATCH, split_axis=0, concat_axis=0, tiled=True, axis_index_groups=groups)


def grad_kernel(n_rows, chip_rows, scale, back_ref, got_ref, shift_ref, inv_ref, cross_ref, diag_ref, out_ref, grad_ref, std_ref):
    n_chip, _, width = got_ref.shape
    half = width // 2
    inv, factor = inv_ref[...], cross_ref[...]

    def fold(a):
        return jnp.sum(a.reshape(chip_rows // 8, 8, width), axis=0)

    def first(p, sums):
        centered = got_ref[p, :chip_rows].astype(F32) + shift_ref[pl.ds(p, 1), :]
        standard = centered * inv
        normed = standard.astype(BF16).astype(F32)
        crossed = jnp.concatenate([normed[:, half:], normed[:, :half]], axis=1)
        grad = scale * back_ref[p, :chip_rows].astype(F32) + factor * crossed
        rows = pl.ds(pl.multiple_of(p * chip_rows, chip_rows), chip_rows)
        grad_ref[rows, :] = grad
        std_ref[rows, :] = standard
        return sums[0] + fold(grad), sums[1] + fold(grad * standard)

    diag = diag_ref[...]
    high = diag.astype(BF16).astype(F32)
    middle = (diag - high).astype(BF16).astype(F32)
    row = lax.broadcasted_iota(jnp.int32, (16, chip_rows), 0)
    terms = jnp.where(row == 0, high, jnp.where(row == 1, middle, jnp.where(row == 2, diag - high - middle, 0.0)))
    out_ref[n_rows:, :] = jnp.concatenate([terms, jnp.zeros((16, width - chip_rows), F32)], axis=1).astype(BF16)

    zero = jnp.zeros((8, width), F32)
    total, cross = lax.fori_loop(0, n_chip, first, (zero, zero))
    grad_mean = jnp.sum(total, axis=0, keepdims=True) / n_rows
    grad_cross = jnp.sum(cross, axis=0, keepdims=True) / n_rows

    def second(p, carry):
        rows = pl.ds(pl.multiple_of(p * chip_rows, chip_rows), chip_rows)
        out_ref[rows, :] = ((grad_ref[rows, :] - grad_mean - std_ref[rows, :] * grad_cross) * inv).astype(BF16)
        return carry

    lax.fori_loop(0, n_chip, second, 0)


def order_kernel(place_ref, rows_ref, own_ref, sent_ref, view_ref):
    n, width = rows_ref.shape
    depth = width // 32

    def blocks(view):
        for j in range(32):
            view_ref[j] = rows_ref[view * n // 2 : (view + 1) * n // 2, j * depth : (j + 1) * depth]

    @pl.when(place_ref[1] == 0)
    def _():
        blocks(0)

    @pl.when(place_ref[1] != 0)
    def _():
        blocks(1)

    def pick(core, out_ref):
        for j in range(16):
            chip = j if core == 0 else (j % 4) * 4 + j // 4
            source = (2 * chip + core) * depth
            out_ref[:, j * depth : (j + 1) * depth] = rows_ref[:, source : source + depth]

    @pl.when(place_ref[0] == 0)
    def _():
        pick(0, own_ref)
        pick(1, sent_ref)

    @pl.when(place_ref[0] != 0)
    def _():
        pick(1, own_ref)
        pick(0, sent_ref)


def project_kernel(place_ref, own_ref, other_ref, weight_ref, kept_ref, sent_ref):
    rows = jnp.concatenate([own_ref[...], other_ref[...]], axis=0)
    both = jnp.dot(rows, weight_ref[...], preferred_element_type=F32)
    n, half = both.shape[0] // 4, both.shape[1] // 2
    first = place_ref[0] == 0
    for owner in range(2):
        a = both[2 * owner * n : (2 * owner + 1) * n, :]
        b = both[(2 * owner + 1) * n : (2 * owner + 2) * n, :]
        low = jnp.concatenate([a[:, :half], b[:, :half]], axis=1)
        high = jnp.concatenate([a[:, half:], b[:, half:]], axis=1)
        kept_ref[owner * n : (owner + 1) * n, :] = jnp.where(first, low, high)
        sent_ref[owner * n : (owner + 1) * n, :] = jnp.where(first, high, low)


def half_grad(odd, one_ref, other_ref, grad_ref, store):
    rows, half = one_ref.shape[1], grad_ref.shape[1] // 2

    def product(a_ref, b_ref):
        return jnp.dot(a_ref[...], grad_ref[:rows, :half], preferred_element_type=F32) + jnp.dot(
            b_ref[...], grad_ref[:rows, half:], preferred_element_type=F32
        )

    @pl.when(odd == 0)
    def _():
        store(product(one_ref, other_ref))

    @pl.when(odd != 0)
    def _():
        store(product(other_ref, one_ref))


def own_half_kernel(place_ref, one_ref, other_ref, grad_ref, out_ref):
    def store(value):
        out_ref[...] = value

    half_grad(place_ref[1], one_ref, other_ref, grad_ref, store)


def other_half_kernel(off_factor, place_ref, one_ref, other_ref, grad_ref, mine_ref, off_ref, diag_ref, out_ref, loss_ref):
    first = place_ref[0] == 0
    rows, terms = one_ref.shape[1], diag_ref.shape[1]
    other_diag = jnp.sum(grad_ref[rows:, :terms].astype(F32), axis=0, keepdims=True)
    loss_ref[0] = jnp.sum(off_factor * off_ref[...] + diag_ref[...] + other_diag) / D_OUT
    half = mine_ref.shape[1]

    def store(value):
        mine = mine_ref[...]
        out_ref[:, :half] = jnp.where(first, mine, value)
        out_ref[:, half:] = jnp.where(first, value, mine)

    half_grad(place_ref[1], one_ref, other_ref, grad_ref, store)


def body(embeds, weight):
    n_chip = lax.axis_size(PLANE)
    n_near, n_far = lax.axis_size("z0"), lax.axis_size("z1")
    n_feat = n_near * n_far
    n_batch = 2 * n_chip
    local_rows, _, d_in = embeds.shape
    chip_rows = 2 * local_rows
    n_rows = local_rows * n_batch
    depth, width_out = weight.shape
    half = width_out // 2
    core = lax.axis_index("core")
    chip = lax.axis_index(PLANE)
    first = core == 0

    def in_core_order(own, other, axis):
        return jnp.concatenate([jnp.where(first, own, other), jnp.where(first, other, own)], axis=axis)

    def swap_core(a):
        return lax.ppermute(a, "core", [(0, 1), (1, 0)])

    odd = lax.axis_index("z0") % 2
    place = jnp.stack([core, odd]).astype(jnp.int32)
    vmem = pl.BlockSpec(memory_space=pltpu.VMEM)
    smem = pl.BlockSpec(memory_space=pltpu.SMEM)
    params = pltpu.CompilerParams(vmem_limit_bytes=32 * 1024 * 1024)

    with jax.named_scope("embeds_exchange"):
        by_view = lax.optimization_barrier(embeds.transpose(1, 0, 2).reshape(2 * local_rows, d_in))
    with jax.named_scope("embeds_order"):
        own_rows, sent_rows, one_view = pl.pallas_call(
            order_kernel,
            out_shape=[jax.ShapeDtypeStruct((2 * local_rows, n_chip * depth), BF16)] * 2
            + [jax.ShapeDtypeStruct((n_batch, local_rows, depth), BF16)],
            in_specs=[smem, vmem],
            out_specs=[vmem] * 3,
            compiler_params=params,
            name="order",
        )(place, by_view)
    with jax.named_scope("weight_gather"):
        first_groups, second_groups = ring_groups()
        row_weight = ring_gather(weight, first_groups)
        row_weight, one_view, own_rows, sent_rows = lax.optimization_barrier((row_weight, one_view, own_rows, sent_rows))
        core_weight = ring_gather(row_weight, second_groups).reshape(n_chip * depth, width_out)
        core_weight, one_view, sent_rows = lax.optimization_barrier((core_weight, one_view, sent_rows))
        one_view = exchange(one_view, BATCH).reshape(n_rows, depth)
        other_rows = swap_core(sent_rows)
    with jax.named_scope("project"):
        kept, sent = pl.pallas_call(
            project_kernel,
            out_shape=[jax.ShapeDtypeStruct((2 * local_rows, width_out), F32)] * 2,
            in_specs=[smem] + [vmem] * 3,
            out_specs=[vmem, vmem],
            compiler_params=params,
            name="project",
        )(place, own_rows, other_rows, core_weight)
        got_other, got_own = jnp.split(swap_core(sent), 2)
        own, other = jnp.split(kept, 2)
        projected = in_core_order(own + got_own, other + got_other, 0)
    with jax.named_scope("project_gather"):
        chip_mean = jnp.sum(projected, axis=0) / chip_rows
        projected, chip_mean, one_view = lax.optimization_barrier((projected, chip_mean, one_view))
        block = with_rows((projected - chip_mean).astype(BF16), pieces(chip_mean))
        block, one_view = lax.optimization_barrier((block, one_view))
        one_t = one_view.T
        other_t = lax.ppermute(one_t, "z0", [(0, 1), (1, 0), (2, 3), (3, 2)])
        got = gather(block, PLANE)
    with jax.named_scope("standardize"):
        chip_means = jnp.sum(got[:, chip_rows : chip_rows + 3].astype(F32), axis=1)
        row_mean = jnp.sum(chip_means, axis=0) / n_chip
        shift = chip_means - row_mean
        centered = got[:, :chip_rows].astype(F32) + shift[:, None, :]
        centered = centered.reshape(n_rows, width_out)
        variance = jnp.sum(centered * centered, axis=0) / n_rows
        spread = jnp.sqrt(variance + epsilon)
        inverse = 1.0 / spread
        normed = (centered * inverse).astype(BF16)
        view_a, view_b = normed[:, :half], normed[:, half:]
        float_a, float_b = view_a.astype(F32), view_b.astype(F32)
        diagonal = jnp.sum(float_a * float_b, axis=0) / n_rows
        diag_terms = (1.0 - diagonal) ** 2 - off_weight * diagonal * diagonal
        diag_local = diag_terms[:chip_rows] + diag_terms[chip_rows:]

    with jax.named_scope("gram"):
        def partial(view):
            mine = lax.dynamic_slice_in_dim(view, chip * chip_rows, chip_rows, axis=0)
            return lax.dot_general(view, mine, (((1,), (1,)), ((), ())), preferred_element_type=F32)

        sent = partial(jnp.where(first, view_b, view_a)).astype(BF16)
        kept = partial(jnp.where(first, view_a, view_b))
        weight_diag = 2.0 * ((1.0 - off_weight) * diagonal - 1.0)
        factor = loss_scale / n_rows * jnp.concatenate([weight_diag, weight_diag])
        sent, kept, diag_local, factor, inverse, one_t, other_t = lax.optimization_barrier(
            (sent, kept, diag_local, factor, inverse, one_t, other_t)
        )
    with jax.named_scope("gram_core"):
        extra = pad_rows(pieces(diag_local), chip_rows)
        parts = kept + swap_core(sent).astype(F32)
    with jax.named_scope("gram_reduce"):
        parts = parts.astype(BF16).reshape(n_near, n_rows // n_near, chip_rows)
        extra = jnp.broadcast_to(extra[None], (n_near, PAD, chip_rows))
        got_z = exchange(jnp.concatenate([parts, extra], axis=1), "z0")
        summed = jnp.sum(got_z.astype(F32), axis=0)
        extra = pad_rows(pieces(jnp.sum(summed[n_rows // n_near :], axis=0)), chip_rows)
        parts = summed[: n_rows // n_near].astype(BF16).reshape(n_far, n_rows // n_feat, chip_rows)
        extra = jnp.broadcast_to(extra[None], (n_far, PAD, chip_rows))
        got_z = exchange(jnp.concatenate([parts, extra], axis=1), "z1")
        summed = jnp.sum(got_z.astype(F32), axis=0)
        gram_block = summed[: n_rows // n_feat].astype(BF16)
        diag_terms = jnp.sum(summed[n_rows // n_feat :], axis=0)
        gram_block, diag_terms = lax.optimization_barrier((gram_block, diag_terms))
    with jax.named_scope("gram_gather"):
        gram_t = gather(gather(gram_block, "z1"), "z0").reshape(n_rows, chip_rows)
        other_gram = swap_core(gram_t)
    with jax.named_scope("back"):
        own_gram, other_gram = gram_t.astype(F32), other_gram.astype(F32)
        with_own = split_product(own_gram, jnp.where(first, view_b, view_a))
        with_other = split_product(other_gram, jnp.where(first, view_a, view_b))
        off_local = jnp.sum(own_gram * other_gram, axis=0)
        back = in_core_order(with_other, with_own, 1).astype(BF16)
        terms = jnp.concatenate([off_local, jnp.zeros((width_out - chip_rows,), F32)])
        block = with_rows(back, pieces(terms))
    with jax.named_scope("back_gather"):
        got_back = gather(block, PLANE)
    with jax.named_scope("grad"):
        scale_off = 2.0 * off_weight / (n_rows * n_rows)
        off_terms = jnp.sum(got_back[:, chip_rows:, :chip_rows].astype(F32), axis=(0, 1))[None]
        grad_proj = pl.pallas_call(
            functools.partial(grad_kernel, n_rows, chip_rows, loss_scale * scale_off),
            out_shape=jax.ShapeDtypeStruct((n_rows + 16, width_out), BF16),
            in_specs=[vmem] * 6,
            out_specs=vmem,
            scratch_shapes=[pltpu.VMEM((n_rows, width_out), F32)] * 2,
            compiler_params=params,
            cost_estimate=pl.CostEstimate(flops=20 * n_rows * width_out, bytes_accessed=8 * n_rows * width_out, transcendentals=0),
            name="grad",
        )(got_back, got, shift, inverse[None], factor[None], diag_terms[None])
    with jax.named_scope("grad_swap"):
        other_proj = swap_core(grad_proj)
    with jax.named_scope("weight_grad"):
        mine = pl.pallas_call(
            own_half_kernel,
            out_shape=jax.ShapeDtypeStruct((depth, half), F32),
            in_specs=[smem] + [vmem] * 3,
            out_specs=vmem,
            compiler_params=params,
            name="own_half",
        )(place, one_t, other_t, grad_proj)
        grad_weight, loss = pl.pallas_call(
            functools.partial(other_half_kernel, off_weight / (n_rows * n_rows)),
            out_shape=[jax.ShapeDtypeStruct((depth, width_out), F32), jax.ShapeDtypeStruct((1,), F32)],
            in_specs=[smem] + [vmem] * 6,
            out_specs=[vmem, smem],
            compiler_params=params,
            name="other_half",
        )(place, one_t, other_t, other_proj, mine, off_terms, diag_terms[None])
    return (loss[0], grad_weight)


def solution(mesh):
    n_batch, n_feat = mesh.devices.shape
    grid = Mesh(mesh.devices.reshape(4, n_batch // 8, 2, n_feat // 4, 4), BATCH + FEAT)
    return jax.shard_map(
        body,
        mesh=grid,
        in_specs=(P(BATCH, None, None), P(BATCH, FEAT)),
        out_specs=(P(), P(BATCH, FEAT)),
        check_vma=False,
    )
```

```python
import functools

import jax
import jax.numpy as jnp
from jax import lax
from jax.experimental import pallas as pl
from jax.experimental.pallas import tpu as pltpu
from jax.sharding import Mesh, PartitionSpec as P

D_OUT = 8192

off_weight = 0.0051
loss_scale = 8.0
epsilon = 1e-05

F32 = jnp.float32
BF16 = jnp.bfloat16
PLANE = ("y", "x")
BATCH = ("y", "x", "core")
FEAT = ("z1", "z0")
PAD = 8


def exchange(blocks, axes):
    return lax.all_to_all(blocks, axes, split_axis=0, concat_axis=0, tiled=True)


def gather(block, axes):
    n = lax.axis_size(axes)
    blocks = jnp.broadcast_to(block[None], (n,) + block.shape)
    return exchange(blocks, axes)


def pieces(value):
    high = lax.reduce_precision(value, 8, 7)
    rest = value - high
    middle = lax.reduce_precision(rest, 8, 7)
    low = rest - middle
    return [high.astype(BF16), middle.astype(BF16), low.astype(BF16)]


def pad_rows(rows, width):
    rows = [r.reshape(1, width) for r in rows]
    return jnp.concatenate(rows + [jnp.zeros((PAD - len(rows), width), BF16)], axis=0)


def split_product(gram_t, view):
    high = gram_t.astype(BF16)
    low = (gram_t - high.astype(F32)).astype(BF16)
    rows = (((0,), (0,)), ((), ()))
    return lax.dot_general(high, view, rows, preferred_element_type=F32) + lax.dot_general(
        low, view, rows, preferred_element_type=F32
    )


def with_rows(main, rows):
    n = main.shape[0]
    index = lax.broadcasted_iota(jnp.int32, (n + PAD, 1), 0)
    main = jnp.pad(main, ((0, PAD), (0, 0)))
    for i, row in enumerate(rows):
        main = jnp.where(index == n + i, row[None, :], main)
    return main


def ring_groups():
    index = lambda y, x, c: (y * 4 + x) * 2 + c
    along_x = lambda c: [[index(y, x, c) for x in range(4)] for y in range(4)]
    along_y = lambda c: [[index(y, x, c) for y in range(4)] for x in range(4)]
    return along_x(0) + along_y(1), along_y(0) + along_x(1)


def ring_gather(block, groups):
    blocks = jnp.broadcast_to(block[None], (4,) + block.shape)
    return lax.all_to_all(blocks, BATCH, split_axis=0, concat_axis=0, tiled=True, axis_index_groups=groups)


def grad_kernel(n_rows, chip_rows, scale, back_ref, got_ref, shift_ref, inv_ref, cross_ref, diag_ref, out_ref, grad_ref, std_ref):
    n_chip, _, width = got_ref.shape
    half = width // 2
    inv, factor = inv_ref[...], cross_ref[...]

    def fold(a):
        return jnp.sum(a.reshape(chip_rows // 8, 8, width), axis=0)

    def first(p, sums):
        centered = got_ref[p, :chip_rows].astype(F32) + shift_ref[pl.ds(p, 1), :]
        standard = centered * inv
        normed = standard.astype(BF16).astype(F32)
        crossed = jnp.concatenate([normed[:, half:], normed[:, :half]], axis=1)
        grad = scale * back_ref[p, :chip_rows].astype(F32) + factor * crossed
        rows = pl.ds(pl.multiple_of(p * chip_rows, chip_rows), chip_rows)
        grad_ref[rows, :] = grad
        std_ref[rows, :] = standard
        return sums[0] + fold(grad), sums[1] + fold(grad * standard)

    diag = diag_ref[...]
    high = diag.astype(BF16).astype(F32)
    middle = (diag - high).astype(BF16).astype(F32)
    row = lax.broadcasted_iota(jnp.int32, (16, chip_rows), 0)
    terms = jnp.where(row == 0, high, jnp.where(row == 1, middle, jnp.where(row == 2, diag - high - middle, 0.0)))
    out_ref[n_rows:, :] = jnp.concatenate([terms, jnp.zeros((16, width - chip_rows), F32)], axis=1).astype(BF16)

    zero = jnp.zeros((8, width), F32)
    total, cross = lax.fori_loop(0, n_chip, first, (zero, zero))
    grad_mean = jnp.sum(total, axis=0, keepdims=True) / n_rows
    grad_cross = jnp.sum(cross, axis=0, keepdims=True) / n_rows

    def second(p, carry):
        rows = pl.ds(pl.multiple_of(p * chip_rows, chip_rows), chip_rows)
        out_ref[rows, :] = ((grad_ref[rows, :] - grad_mean - std_ref[rows, :] * grad_cross) * inv).astype(BF16)
        return carry

    lax.fori_loop(0, n_chip, second, 0)


def order_kernel(place_ref, rows_ref, own_ref, sent_ref, view_ref):
    n, width = rows_ref.shape
    depth = width // 32

    def blocks(view):
        for j in range(32):
            view_ref[j] = rows_ref[view * n // 2 : (view + 1) * n // 2, j * depth : (j + 1) * depth]

    @pl.when(place_ref[1] == 0)
    def _():
        blocks(0)

    @pl.when(place_ref[1] != 0)
    def _():
        blocks(1)

    def pick(core, out_ref):
        for j in range(16):
            chip = j if core == 0 else (j % 4) * 4 + j // 4
            source = (2 * chip + core) * depth
            out_ref[:, j * depth : (j + 1) * depth] = rows_ref[:, source : source + depth]

    @pl.when(place_ref[0] == 0)
    def _():
        pick(0, own_ref)
        pick(1, sent_ref)

    @pl.when(place_ref[0] != 0)
    def _():
        pick(1, own_ref)
        pick(0, sent_ref)


def project_kernel(place_ref, own_ref, other_ref, weight_ref, kept_ref, sent_ref):
    rows = jnp.concatenate([own_ref[...], other_ref[...]], axis=0)
    both = jnp.dot(rows, weight_ref[...], preferred_element_type=F32)
    n, half = both.shape[0] // 4, both.shape[1] // 2
    first = place_ref[0] == 0
    for owner in range(2):
        a = both[2 * owner * n : (2 * owner + 1) * n, :]
        b = both[(2 * owner + 1) * n : (2 * owner + 2) * n, :]
        low = jnp.concatenate([a[:, :half], b[:, :half]], axis=1)
        high = jnp.concatenate([a[:, half:], b[:, half:]], axis=1)
        kept_ref[owner * n : (owner + 1) * n, :] = jnp.where(first, low, high)
        sent_ref[owner * n : (owner + 1) * n, :] = jnp.where(first, high, low)


def half_grad(odd, one_refs, other_refs, grad_ref, store):
    rows, half = one_refs[0].shape[1], grad_ref.shape[1] // 2

    def product(a_refs, b_refs):
        total = 0.0
        for i in range(2):
            part = slice(i * rows, (i + 1) * rows)
            total += jnp.dot(a_refs[i][...], grad_ref[part, :half], preferred_element_type=F32)
            total += jnp.dot(b_refs[i][...], grad_ref[part, half:], preferred_element_type=F32)
        return total

    @pl.when(odd == 0)
    def _():
        store(product(one_refs, other_refs))

    @pl.when(odd != 0)
    def _():
        store(product(other_refs, one_refs))


def own_half_kernel(place_ref, one_low, one_high, other_low, other_high, grad_ref, out_ref):
    def store(value):
        out_ref[...] = value

    half_grad(place_ref[1], (one_low, one_high), (other_low, other_high), grad_ref, store)


def other_half_kernel(
    off_factor, place_ref, one_low, one_high, other_low, other_high, grad_ref, mine_ref, off_ref, diag_ref, out_ref, loss_ref
):
    first = place_ref[0] == 0
    rows, terms = 2 * one_low.shape[1], diag_ref.shape[1]
    other_diag = jnp.sum(grad_ref[rows:, :terms].astype(F32), axis=0, keepdims=True)
    loss_ref[0] = jnp.sum(off_factor * off_ref[...] + diag_ref[...] + other_diag) / D_OUT
    half = mine_ref.shape[1]

    def store(value):
        mine = mine_ref[...]
        out_ref[:, :half] = jnp.where(first, mine, value)
        out_ref[:, half:] = jnp.where(first, value, mine)

    half_grad(place_ref[1], (one_low, one_high), (other_low, other_high), grad_ref, store)


def body(embeds, weight):
    n_chip = lax.axis_size(PLANE)
    n_near, n_far = lax.axis_size("z0"), lax.axis_size("z1")
    n_feat = n_near * n_far
    n_batch = 2 * n_chip
    local_rows, _, d_in = embeds.shape
    chip_rows = 2 * local_rows
    n_rows = local_rows * n_batch
    depth, width_out = weight.shape
    half = width_out // 2
    core = lax.axis_index("core")
    chip = lax.axis_index(PLANE)
    first = core == 0

    def in_core_order(own, other, axis):
        return jnp.concatenate([jnp.where(first, own, other), jnp.where(first, other, own)], axis=axis)

    def swap_core(a):
        return lax.ppermute(a, "core", [(0, 1), (1, 0)])

    odd = lax.axis_index("z0") % 2
    place = jnp.stack([core, odd]).astype(jnp.int32)
    vmem = pl.BlockSpec(memory_space=pltpu.VMEM)
    smem = pl.BlockSpec(memory_space=pltpu.SMEM)
    params = pltpu.CompilerParams(vmem_limit_bytes=32 * 1024 * 1024)

    with jax.named_scope("embeds_exchange"):
        by_view = lax.optimization_barrier(embeds.transpose(1, 0, 2).reshape(2 * local_rows, d_in))
    with jax.named_scope("embeds_order"):
        own_rows, sent_rows, one_view = pl.pallas_call(
            order_kernel,
            out_shape=[jax.ShapeDtypeStruct((2 * local_rows, n_chip * depth), BF16)] * 2
            + [jax.ShapeDtypeStruct((n_batch, local_rows, depth), BF16)],
            in_specs=[smem, vmem],
            out_specs=[vmem] * 3,
            compiler_params=params,
            name="order",
        )(place, by_view)
    with jax.named_scope("weight_gather"):
        first_groups, second_groups = ring_groups()
        row_weight = ring_gather(weight, first_groups)
        row_weight, one_view, own_rows, sent_rows = lax.optimization_barrier((row_weight, one_view, own_rows, sent_rows))
        core_weight = ring_gather(row_weight, second_groups).reshape(n_chip * depth, width_out)
        core_weight, one_view, sent_rows = lax.optimization_barrier((core_weight, one_view, sent_rows))
        one_view = exchange(one_view, BATCH).reshape(n_rows, depth)
        other_rows = swap_core(sent_rows)
    with jax.named_scope("project"):
        kept, sent = pl.pallas_call(
            project_kernel,
            out_shape=[jax.ShapeDtypeStruct((2 * local_rows, width_out), F32)] * 2,
            in_specs=[smem] + [vmem] * 3,
            out_specs=[vmem, vmem],
            compiler_params=params,
            name="project",
        )(place, own_rows, other_rows, core_weight)
        got_other, got_own = jnp.split(swap_core(sent), 2)
        own, other = jnp.split(kept, 2)
        projected = in_core_order(own + got_own, other + got_other, 0)
    with jax.named_scope("project_gather"):
        chip_mean = jnp.sum(projected, axis=0) / chip_rows
        projected, chip_mean, one_view = lax.optimization_barrier((projected, chip_mean, one_view))
        block = with_rows((projected - chip_mean).astype(BF16), pieces(chip_mean))
        block, one_view = lax.optimization_barrier((block, one_view))
        one_low, one_high = one_view[: n_rows // 2].T, one_view[n_rows // 2 :].T
        got = gather(block, PLANE)
    with jax.named_scope("standardize"):
        chip_means = jnp.sum(got[:, chip_rows : chip_rows + 3].astype(F32), axis=1)
        row_mean = jnp.sum(chip_means, axis=0) / n_chip
        shift = chip_means - row_mean
        centered = got[:, :chip_rows].astype(F32) + shift[:, None, :]
        centered = centered.reshape(n_rows, width_out)
        variance = jnp.sum(centered * centered, axis=0) / n_rows
        spread = jnp.sqrt(variance + epsilon)
        inverse = 1.0 / spread
        normed = (centered * inverse).astype(BF16)
        view_a, view_b = normed[:, :half], normed[:, half:]
        float_a, float_b = view_a.astype(F32), view_b.astype(F32)
        diagonal = jnp.sum(float_a * float_b, axis=0) / n_rows
        diag_terms = (1.0 - diagonal) ** 2 - off_weight * diagonal * diagonal
        diag_local = diag_terms[:chip_rows] + diag_terms[chip_rows:]

    with jax.named_scope("gram"):
        def partial(view):
            mine = lax.dynamic_slice_in_dim(view, chip * chip_rows, chip_rows, axis=0)
            return lax.dot_general(view, mine, (((1,), (1,)), ((), ())), preferred_element_type=F32)

        sent = partial(jnp.where(first, view_b, view_a)).astype(BF16)
        kept = partial(jnp.where(first, view_a, view_b))
        weight_diag = 2.0 * ((1.0 - off_weight) * diagonal - 1.0)
        factor = loss_scale / n_rows * jnp.concatenate([weight_diag, weight_diag])
        sent, kept, diag_local, factor, inverse, one_low, one_high = lax.optimization_barrier(
            (sent, kept, diag_local, factor, inverse, one_low, one_high)
        )
    with jax.named_scope("gram_core"):
        extra = pad_rows(pieces(diag_local), chip_rows)
        parts = kept + swap_core(sent).astype(F32)
    with jax.named_scope("gram_reduce"):
        parts = parts.astype(BF16).reshape(n_near, n_rows // n_near, chip_rows)
        extra = jnp.broadcast_to(extra[None], (n_near, PAD, chip_rows))
        got_z = exchange(jnp.concatenate([parts, extra], axis=1), "z0")
        summed = jnp.sum(got_z.astype(F32), axis=0)
        extra = pad_rows(pieces(jnp.sum(summed[n_rows // n_near :], axis=0)), chip_rows)
        parts = summed[: n_rows // n_near].astype(BF16).reshape(n_far, n_rows // n_feat, chip_rows)
        extra = jnp.broadcast_to(extra[None], (n_far, PAD, chip_rows))
        parts, extra, one_low = lax.optimization_barrier((parts, extra, one_low))
        other_low = lax.ppermute(one_low, "z0", [(0, 1), (1, 0), (2, 3), (3, 2)])
        got_z = exchange(jnp.concatenate([parts, extra], axis=1), "z1")
        summed = jnp.sum(got_z.astype(F32), axis=0)
        gram_block = summed[: n_rows // n_feat].astype(BF16)
        diag_terms = jnp.sum(summed[n_rows // n_feat :], axis=0)
        gram_block, diag_terms, other_low, one_high = lax.optimization_barrier(
            (gram_block, diag_terms, other_low, one_high)
        )
    with jax.named_scope("gram_gather"):
        other_high = lax.ppermute(one_high, "z0", [(0, 1), (1, 0), (2, 3), (3, 2)])
        gram_far, other_high = lax.optimization_barrier((gather(gram_block, "z1"), other_high))
        gram_t = gather(gram_far, "z0").reshape(n_rows, chip_rows)
        other_gram = swap_core(gram_t)
    with jax.named_scope("back"):
        own_gram, other_gram = gram_t.astype(F32), other_gram.astype(F32)
        with_own = split_product(own_gram, jnp.where(first, view_b, view_a))
        with_other = split_product(other_gram, jnp.where(first, view_a, view_b))
        off_local = jnp.sum(own_gram * other_gram, axis=0)
        back = in_core_order(with_other, with_own, 1).astype(BF16)
        terms = jnp.concatenate([off_local, jnp.zeros((width_out - chip_rows,), F32)])
        block = with_rows(back, pieces(terms))
    with jax.named_scope("back_gather"):
        got_back = gather(block, PLANE)
    with jax.named_scope("grad"):
        scale_off = 2.0 * off_weight / (n_rows * n_rows)
        off_terms = jnp.sum(got_back[:, chip_rows:, :chip_rows].astype(F32), axis=(0, 1))[None]
        grad_proj = pl.pallas_call(
            functools.partial(grad_kernel, n_rows, chip_rows, loss_scale * scale_off),
            out_shape=jax.ShapeDtypeStruct((n_rows + 16, width_out), BF16),
            in_specs=[vmem] * 6,
            out_specs=vmem,
            scratch_shapes=[pltpu.VMEM((n_rows, width_out), F32)] * 2,
            compiler_params=params,
            cost_estimate=pl.CostEstimate(flops=20 * n_rows * width_out, bytes_accessed=8 * n_rows * width_out, transcendentals=0),
            name="grad",
        )(got_back, got, shift, inverse[None], factor[None], diag_terms[None])
    with jax.named_scope("grad_swap"):
        other_proj = swap_core(grad_proj)
    with jax.named_scope("weight_grad"):
        mine = pl.pallas_call(
            own_half_kernel,
            out_shape=jax.ShapeDtypeStruct((depth, half), F32),
            in_specs=[smem] + [vmem] * 5,
            out_specs=vmem,
            compiler_params=params,
            name="own_half",
        )(place, one_low, one_high, other_low, other_high, grad_proj)
        grad_weight, loss = pl.pallas_call(
            functools.partial(other_half_kernel, off_weight / (n_rows * n_rows)),
            out_shape=[jax.ShapeDtypeStruct((depth, width_out), F32), jax.ShapeDtypeStruct((1,), F32)],
            in_specs=[smem] + [vmem] * 8,
            out_specs=[vmem, smem],
            compiler_params=params,
            name="other_half",
        )(place, one_low, one_high, other_low, other_high, other_proj, mine, off_terms, diag_terms[None])
    return (loss[0], grad_weight)


def solution(mesh):
    n_batch, n_feat = mesh.devices.shape
    grid = Mesh(mesh.devices.reshape(4, n_batch // 8, 2, n_feat // 4, 4), BATCH + FEAT)
    return jax.shard_map(
        body,
        mesh=grid,
        in_specs=(P(BATCH, None, None), P(BATCH, FEAT)),
        out_specs=(P(), P(BATCH, FEAT)),
        check_vma=False,
    )
```

```python
import functools

import jax
import jax.numpy as jnp
from jax import lax
from jax.experimental import pallas as pl
from jax.experimental.pallas import tpu as pltpu
from jax.sharding import Mesh, PartitionSpec as P

D_OUT = 8192

off_weight = 0.0051
loss_scale = 8.0
epsilon = 1e-05

F32 = jnp.float32
BF16 = jnp.bfloat16
PLANE = ("y", "x")
BATCH = ("y", "x", "core")
FEAT = ("z1", "z0")
PAD = 8


def exchange(blocks, axes):
    return lax.all_to_all(blocks, axes, split_axis=0, concat_axis=0, tiled=True)


def gather(block, axes):
    n = lax.axis_size(axes)
    blocks = jnp.broadcast_to(block[None], (n,) + block.shape)
    return exchange(blocks, axes)


def pieces(value):
    high = lax.reduce_precision(value, 8, 7)
    rest = value - high
    middle = lax.reduce_precision(rest, 8, 7)
    low = rest - middle
    return [high.astype(BF16), middle.astype(BF16), low.astype(BF16)]


def pad_rows(rows, width):
    rows = [r.reshape(1, width) for r in rows]
    return jnp.concatenate(rows + [jnp.zeros((PAD - len(rows), width), BF16)], axis=0)


def split_product(gram_t, view):
    high = gram_t.astype(BF16)
    low = (gram_t - high.astype(F32)).astype(BF16)
    rows = (((0,), (0,)), ((), ()))
    return lax.dot_general(high, view, rows, preferred_element_type=F32) + lax.dot_general(
        low, view, rows, preferred_element_type=F32
    )


def with_rows(main, rows):
    n = main.shape[0]
    index = lax.broadcasted_iota(jnp.int32, (n + PAD, 1), 0)
    main = jnp.pad(main, ((0, PAD), (0, 0)))
    for i, row in enumerate(rows):
        main = jnp.where(index == n + i, row[None, :], main)
    return main


def ring_groups():
    index = lambda y, x, c: (y * 4 + x) * 2 + c
    along_x = lambda c: [[index(y, x, c) for x in range(4)] for y in range(4)]
    along_y = lambda c: [[index(y, x, c) for y in range(4)] for x in range(4)]
    return along_x(0) + along_y(1), along_y(0) + along_x(1)


def ring_gather(block, groups):
    blocks = jnp.broadcast_to(block[None], (4,) + block.shape)
    return lax.all_to_all(blocks, BATCH, split_axis=0, concat_axis=0, tiled=True, axis_index_groups=groups)


def grad_kernel(n_rows, chip_rows, scale, back_ref, got_ref, shift_ref, inv_ref, cross_ref, diag_ref, out_ref, grad_ref, std_ref):
    n_chip, _, width = got_ref.shape
    half = width // 2
    inv, factor = inv_ref[...], cross_ref[...]

    def fold(a):
        return jnp.sum(a.reshape(chip_rows // 8, 8, width), axis=0)

    def first(p, sums):
        centered = got_ref[p, :chip_rows].astype(F32) + shift_ref[pl.ds(p, 1), :]
        standard = centered * inv
        normed = standard.astype(BF16).astype(F32)
        crossed = jnp.concatenate([normed[:, half:], normed[:, :half]], axis=1)
        grad = scale * back_ref[p, :chip_rows].astype(F32) + factor * crossed
        rows = pl.ds(pl.multiple_of(p * chip_rows, chip_rows), chip_rows)
        grad_ref[rows, :] = grad
        std_ref[rows, :] = standard
        return sums[0] + fold(grad), sums[1] + fold(grad * standard)

    diag = diag_ref[...]
    high = diag.astype(BF16).astype(F32)
    middle = (diag - high).astype(BF16).astype(F32)
    row = lax.broadcasted_iota(jnp.int32, (16, chip_rows), 0)
    terms = jnp.where(row == 0, high, jnp.where(row == 1, middle, jnp.where(row == 2, diag - high - middle, 0.0)))
    out_ref[n_rows:, :] = jnp.concatenate([terms, jnp.zeros((16, width - chip_rows), F32)], axis=1).astype(BF16)

    zero = jnp.zeros((8, width), F32)
    total, cross = lax.fori_loop(0, n_chip, first, (zero, zero))
    grad_mean = jnp.sum(total, axis=0, keepdims=True) / n_rows
    grad_cross = jnp.sum(cross, axis=0, keepdims=True) / n_rows

    def second(p, carry):
        rows = pl.ds(pl.multiple_of(p * chip_rows, chip_rows), chip_rows)
        out_ref[rows, :] = ((grad_ref[rows, :] - grad_mean - std_ref[rows, :] * grad_cross) * inv).astype(BF16)
        return carry

    lax.fori_loop(0, n_chip, second, 0)


def order_kernel(place_ref, rows_ref, own_ref, sent_ref, view_ref):
    n, width = rows_ref.shape
    depth = width // 32

    def blocks(view):
        for j in range(32):
            view_ref[j] = rows_ref[view * n // 2 : (view + 1) * n // 2, j * depth : (j + 1) * depth]

    @pl.when(place_ref[1] == 0)
    def _():
        blocks(0)

    @pl.when(place_ref[1] != 0)
    def _():
        blocks(1)

    def pick(core, out_ref):
        for j in range(16):
            chip = j if core == 0 else (j % 4) * 4 + j // 4
            source = (2 * chip + core) * depth
            out_ref[:, j * depth : (j + 1) * depth] = rows_ref[:, source : source + depth]

    @pl.when(place_ref[0] == 0)
    def _():
        pick(0, own_ref)
        pick(1, sent_ref)

    @pl.when(place_ref[0] != 0)
    def _():
        pick(1, own_ref)
        pick(0, sent_ref)


def project_kernel(place_ref, own_ref, other_ref, weight_ref, kept_ref, sent_ref):
    rows = jnp.concatenate([own_ref[...], other_ref[...]], axis=0)
    both = jnp.dot(rows, weight_ref[...], preferred_element_type=F32)
    n, half = both.shape[0] // 4, both.shape[1] // 2
    first = place_ref[0] == 0
    for owner in range(2):
        a = both[2 * owner * n : (2 * owner + 1) * n, :]
        b = both[(2 * owner + 1) * n : (2 * owner + 2) * n, :]
        low = jnp.concatenate([a[:, :half], b[:, :half]], axis=1)
        high = jnp.concatenate([a[:, half:], b[:, half:]], axis=1)
        kept_ref[owner * n : (owner + 1) * n, :] = jnp.where(first, low, high)
        sent_ref[owner * n : (owner + 1) * n, :] = jnp.where(first, high, low)


def half_grad(odd, one_ref, other_ref, grad_ref, store):
    rows, half = one_ref.shape[1], grad_ref.shape[1] // 2

    def product(a_ref, b_ref):
        return jnp.dot(a_ref[...], grad_ref[:rows, :half], preferred_element_type=F32) + jnp.dot(
            b_ref[...], grad_ref[:rows, half:], preferred_element_type=F32
        )

    @pl.when(odd == 0)
    def _():
        store(product(one_ref, other_ref))

    @pl.when(odd != 0)
    def _():
        store(product(other_ref, one_ref))


def own_half_kernel(place_ref, one_ref, other_ref, grad_ref, out_ref):
    def store(value):
        out_ref[...] = value

    half_grad(place_ref[1], one_ref, other_ref, grad_ref, store)


def other_half_kernel(off_factor, place_ref, one_ref, other_ref, grad_ref, mine_ref, off_ref, diag_ref, out_ref, loss_ref):
    first = place_ref[0] == 0
    rows, terms = one_ref.shape[1], diag_ref.shape[1]
    other_diag = jnp.sum(grad_ref[rows:, :terms].astype(F32), axis=0, keepdims=True)
    loss_ref[0] = jnp.sum(off_factor * off_ref[...] + diag_ref[...] + other_diag) / D_OUT
    half = mine_ref.shape[1]

    def store(value):
        mine = mine_ref[...]
        out_ref[:, :half] = jnp.where(first, mine, value)
        out_ref[:, half:] = jnp.where(first, value, mine)

    half_grad(place_ref[1], one_ref, other_ref, grad_ref, store)


def body(embeds, weight):
    n_chip = lax.axis_size(PLANE)
    n_near, n_far = lax.axis_size("z0"), lax.axis_size("z1")
    n_feat = n_near * n_far
    n_batch = 2 * n_chip
    local_rows, _, d_in = embeds.shape
    chip_rows = 2 * local_rows
    n_rows = local_rows * n_batch
    depth, width_out = weight.shape
    half = width_out // 2
    core = lax.axis_index("core")
    chip = lax.axis_index(PLANE)
    first = core == 0

    def in_core_order(own, other, axis):
        return jnp.concatenate([jnp.where(first, own, other), jnp.where(first, other, own)], axis=axis)

    def swap_core(a):
        return lax.ppermute(a, "core", [(0, 1), (1, 0)])

    odd = lax.axis_index("z0") % 2
    place = jnp.stack([core, odd]).astype(jnp.int32)
    vmem = pl.BlockSpec(memory_space=pltpu.VMEM)
    smem = pl.BlockSpec(memory_space=pltpu.SMEM)
    params = pltpu.CompilerParams(vmem_limit_bytes=32 * 1024 * 1024)

    with jax.named_scope("embeds_exchange"):
        by_view = lax.optimization_barrier(embeds.transpose(1, 0, 2).reshape(2 * local_rows, d_in))
    with jax.named_scope("embeds_order"):
        own_rows, sent_rows, one_view = pl.pallas_call(
            order_kernel,
            out_shape=[jax.ShapeDtypeStruct((2 * local_rows, n_chip * depth), BF16)] * 2
            + [jax.ShapeDtypeStruct((n_batch, local_rows, depth), BF16)],
            in_specs=[smem, vmem],
            out_specs=[vmem] * 3,
            compiler_params=params,
            name="order",
        )(place, by_view)
    with jax.named_scope("weight_gather"):
        first_groups, second_groups = ring_groups()
        row_weight = ring_gather(weight, first_groups)
        row_weight, one_view, own_rows, sent_rows = lax.optimization_barrier((row_weight, one_view, own_rows, sent_rows))
        core_weight = ring_gather(row_weight, second_groups).reshape(n_chip * depth, width_out)
        core_weight, one_view, sent_rows = lax.optimization_barrier((core_weight, one_view, sent_rows))
        one_view = exchange(one_view, BATCH).reshape(n_rows, depth)
        other_rows = swap_core(sent_rows)
    with jax.named_scope("project"):
        kept, sent = pl.pallas_call(
            project_kernel,
            out_shape=[jax.ShapeDtypeStruct((2 * local_rows, width_out), F32)] * 2,
            in_specs=[smem] + [vmem] * 3,
            out_specs=[vmem, vmem],
            compiler_params=params,
            name="project",
        )(place, own_rows, other_rows, core_weight)
        got_other, got_own = jnp.split(swap_core(sent), 2)
        own, other = jnp.split(kept, 2)
        projected = in_core_order(own + got_own, other + got_other, 0)
    with jax.named_scope("project_gather"):
        chip_mean = jnp.sum(projected, axis=0) / chip_rows
        projected, chip_mean, one_view = lax.optimization_barrier((projected, chip_mean, one_view))
        block = with_rows((projected - chip_mean).astype(BF16), pieces(chip_mean))
        block, one_view = lax.optimization_barrier((block, one_view))
        one_t = one_view.T
        other_t = lax.ppermute(one_t, "z0", [(0, 1), (1, 0), (2, 3), (3, 2)])
        got = gather(block, PLANE)
    with jax.named_scope("standardize"):
        chip_means = jnp.sum(got[:, chip_rows : chip_rows + 3].astype(F32), axis=1)
        row_mean = jnp.sum(chip_means, axis=0) / n_chip
        shift = chip_means - row_mean
        centered = got[:, :chip_rows].astype(F32) + shift[:, None, :]
        centered = centered.reshape(n_rows, width_out)
        variance = jnp.sum(centered * centered, axis=0) / n_rows
        spread = jnp.sqrt(variance + epsilon)
        inverse = 1.0 / spread
        normed = (centered * inverse).astype(BF16)
        view_a, view_b = normed[:, :half], normed[:, half:]
        float_a, float_b = view_a.astype(F32), view_b.astype(F32)
        diagonal = jnp.sum(float_a * float_b, axis=0) / n_rows
        diag_terms = (1.0 - diagonal) ** 2 - off_weight * diagonal * diagonal
        diag_local = diag_terms[:chip_rows] + diag_terms[chip_rows:]

    with jax.named_scope("gram"):
        def partial(view):
            mine = lax.dynamic_slice_in_dim(view, chip * chip_rows, chip_rows, axis=0)
            return lax.dot_general(view, mine, (((1,), (1,)), ((), ())), preferred_element_type=F32)

        sent = partial(jnp.where(first, view_b, view_a)).astype(BF16)
        kept = partial(jnp.where(first, view_a, view_b))
        weight_diag = 2.0 * ((1.0 - off_weight) * diagonal - 1.0)
        factor = loss_scale / n_rows * jnp.concatenate([weight_diag, weight_diag])
        sent, one_t, other_t = lax.optimization_barrier((sent, one_t, other_t))
    with jax.named_scope("gram_core"):
        extra = pad_rows(pieces(diag_local), chip_rows)
        parts = kept + swap_core(sent).astype(F32)
        parts, extra, factor, inverse = lax.optimization_barrier((parts.astype(BF16), extra, factor, inverse))
    with jax.named_scope("gram_reduce"):
        parts = parts.astype(BF16).reshape(n_near, n_rows // n_near, chip_rows)
        extra = jnp.broadcast_to(extra[None], (n_near, PAD, chip_rows))
        got_z = exchange(jnp.concatenate([parts, extra], axis=1), "z0")
        summed = jnp.sum(got_z.astype(F32), axis=0)
        extra = pad_rows(pieces(jnp.sum(summed[n_rows // n_near :], axis=0)), chip_rows)
        parts = summed[: n_rows // n_near].astype(BF16).reshape(n_far, n_rows // n_feat, chip_rows)
        extra = jnp.broadcast_to(extra[None], (n_far, PAD, chip_rows))
        got_z = exchange(jnp.concatenate([parts, extra], axis=1), "z1")
        summed = jnp.sum(got_z.astype(F32), axis=0)
        gram_block = summed[: n_rows // n_feat].astype(BF16)
        diag_terms = jnp.sum(summed[n_rows // n_feat :], axis=0)
        gram_block, diag_terms = lax.optimization_barrier((gram_block, diag_terms))
    with jax.named_scope("gram_gather"):
        gram_t = gather(gather(gram_block, "z1"), "z0").reshape(n_rows, chip_rows)
        other_gram = swap_core(gram_t)
    with jax.named_scope("back"):
        own_gram, other_gram = gram_t.astype(F32), other_gram.astype(F32)
        with_own = split_product(own_gram, jnp.where(first, view_b, view_a))
        with_other = split_product(other_gram, jnp.where(first, view_a, view_b))
        off_local = jnp.sum(own_gram * other_gram, axis=0)
        back = in_core_order(with_other, with_own, 1).astype(BF16)
        terms = jnp.concatenate([off_local, jnp.zeros((width_out - chip_rows,), F32)])
        block = with_rows(back, pieces(terms))
    with jax.named_scope("back_gather"):
        got_back = gather(block, PLANE)
    with jax.named_scope("grad"):
        scale_off = 2.0 * off_weight / (n_rows * n_rows)
        off_terms = jnp.sum(got_back[:, chip_rows:, :chip_rows].astype(F32), axis=(0, 1))[None]
        grad_proj = pl.pallas_call(
            functools.partial(grad_kernel, n_rows, chip_rows, loss_scale * scale_off),
            out_shape=jax.ShapeDtypeStruct((n_rows + 16, width_out), BF16),
            in_specs=[vmem] * 6,
            out_specs=vmem,
            scratch_shapes=[pltpu.VMEM((n_rows, width_out), F32)] * 2,
            compiler_params=params,
            cost_estimate=pl.CostEstimate(flops=20 * n_rows * width_out, bytes_accessed=8 * n_rows * width_out, transcendentals=0),
            name="grad",
        )(got_back, got, shift, inverse[None], factor[None], diag_terms[None])
    with jax.named_scope("grad_swap"):
        other_proj = swap_core(grad_proj)
    with jax.named_scope("weight_grad"):
        mine = pl.pallas_call(
            own_half_kernel,
            out_shape=jax.ShapeDtypeStruct((depth, half), F32),
            in_specs=[smem] + [vmem] * 3,
            out_specs=vmem,
            compiler_params=params,
            name="own_half",
        )(place, one_t, other_t, grad_proj)
        grad_weight, loss = pl.pallas_call(
            functools.partial(other_half_kernel, off_weight / (n_rows * n_rows)),
            out_shape=[jax.ShapeDtypeStruct((depth, width_out), F32), jax.ShapeDtypeStruct((1,), F32)],
            in_specs=[smem] + [vmem] * 6,
            out_specs=[vmem, smem],
            compiler_params=params,
            name="other_half",
        )(place, one_t, other_t, other_proj, mine, off_terms, diag_terms[None])
    return (loss[0], grad_weight)


def solution(mesh):
    n_batch, n_feat = mesh.devices.shape
    grid = Mesh(mesh.devices.reshape(4, n_batch // 8, 2, n_feat // 4, 4), BATCH + FEAT)
    return jax.shard_map(
        body,
        mesh=grid,
        in_specs=(P(BATCH, None, None), P(BATCH, FEAT)),
        out_specs=(P(), P(BATCH, FEAT)),
        check_vma=False,
    )
```

```python
import functools

import jax
import jax.numpy as jnp
from jax import lax
from jax.experimental import pallas as pl
from jax.experimental.pallas import tpu as pltpu
from jax.sharding import Mesh, PartitionSpec as P

D_OUT = 8192

off_weight = 0.0051
loss_scale = 8.0
epsilon = 1e-05

F32 = jnp.float32
BF16 = jnp.bfloat16
PLANE = ("y", "x")
BATCH = ("y", "x", "core")
FEAT = ("z1", "z0")
PAD = 8


def exchange(blocks, axes):
    return lax.all_to_all(blocks, axes, split_axis=0, concat_axis=0, tiled=True)


def gather(block, axes):
    n = lax.axis_size(axes)
    blocks = jnp.broadcast_to(block[None], (n,) + block.shape)
    return exchange(blocks, axes)


def pieces(value):
    high = lax.reduce_precision(value, 8, 7)
    rest = value - high
    middle = lax.reduce_precision(rest, 8, 7)
    low = rest - middle
    return [high.astype(BF16), middle.astype(BF16), low.astype(BF16)]


def pad_rows(rows, width):
    rows = [r.reshape(1, width) for r in rows]
    return jnp.concatenate(rows + [jnp.zeros((PAD - len(rows), width), BF16)], axis=0)


def split_product(gram_t, view):
    high = gram_t.astype(BF16)
    low = (gram_t - high.astype(F32)).astype(BF16)
    rows = (((0,), (0,)), ((), ()))
    return lax.dot_general(high, view, rows, preferred_element_type=F32) + lax.dot_general(
        low, view, rows, preferred_element_type=F32
    )


def with_rows(main, rows):
    n = main.shape[0]
    index = lax.broadcasted_iota(jnp.int32, (n + PAD, 1), 0)
    main = jnp.pad(main, ((0, PAD), (0, 0)))
    for i, row in enumerate(rows):
        main = jnp.where(index == n + i, row[None, :], main)
    return main


def ring_groups():
    index = lambda y, x, c: (y * 4 + x) * 2 + c
    along_x = lambda c: [[index(y, x, c) for x in range(4)] for y in range(4)]
    along_y = lambda c: [[index(y, x, c) for y in range(4)] for x in range(4)]
    return along_x(0) + along_y(1), along_y(0) + along_x(1)


def ring_gather(block, groups):
    blocks = jnp.broadcast_to(block[None], (4,) + block.shape)
    return lax.all_to_all(blocks, BATCH, split_axis=0, concat_axis=0, tiled=True, axis_index_groups=groups)


def grad_kernel(n_rows, chip_rows, scale, back_ref, got_ref, shift_ref, inv_ref, cross_ref, diag_ref, out_ref, grad_ref, std_ref):
    n_chip, _, width = got_ref.shape
    half = width // 2
    inv, factor = inv_ref[...], cross_ref[...]

    def fold(a):
        return jnp.sum(a.reshape(chip_rows // 8, 8, width), axis=0)

    def first(p, sums):
        centered = got_ref[p, :chip_rows].astype(F32) + shift_ref[pl.ds(p, 1), :]
        standard = centered * inv
        normed = standard.astype(BF16).astype(F32)
        crossed = jnp.concatenate([normed[:, half:], normed[:, :half]], axis=1)
        grad = scale * back_ref[p, :chip_rows].astype(F32) + factor * crossed
        rows = pl.ds(pl.multiple_of(p * chip_rows, chip_rows), chip_rows)
        grad_ref[rows, :] = grad
        std_ref[rows, :] = standard
        return sums[0] + fold(grad), sums[1] + fold(grad * standard)

    diag = diag_ref[...]
    high = diag.astype(BF16).astype(F32)
    middle = (diag - high).astype(BF16).astype(F32)
    row = lax.broadcasted_iota(jnp.int32, (16, chip_rows), 0)
    terms = jnp.where(row == 0, high, jnp.where(row == 1, middle, jnp.where(row == 2, diag - high - middle, 0.0)))
    out_ref[n_rows:, :] = jnp.concatenate([terms, jnp.zeros((16, width - chip_rows), F32)], axis=1).astype(BF16)

    zero = jnp.zeros((8, width), F32)
    total, cross = lax.fori_loop(0, n_chip, first, (zero, zero))
    grad_mean = jnp.sum(total, axis=0, keepdims=True) / n_rows
    grad_cross = jnp.sum(cross, axis=0, keepdims=True) / n_rows

    def second(p, carry):
        rows = pl.ds(pl.multiple_of(p * chip_rows, chip_rows), chip_rows)
        out_ref[rows, :] = ((grad_ref[rows, :] - grad_mean - std_ref[rows, :] * grad_cross) * inv).astype(BF16)
        return carry

    lax.fori_loop(0, n_chip, second, 0)


def order_kernel(place_ref, rows_ref, own_ref, sent_ref, view_ref):
    n, width = rows_ref.shape
    depth = width // 32

    for q in range(4):

        @pl.when(place_ref[2] == q)
        def _(q=q):
            for j in range(32):
                view_ref[j] = rows_ref[q * n // 4 : (q + 1) * n // 4, j * depth : (j + 1) * depth]

    def pick(core, out_ref):
        for j in range(16):
            chip = j if core == 0 else (j % 4) * 4 + j // 4
            source = (2 * chip + core) * depth
            out_ref[:, j * depth : (j + 1) * depth] = rows_ref[:, source : source + depth]

    @pl.when(place_ref[0] == 0)
    def _():
        pick(0, own_ref)
        pick(1, sent_ref)

    @pl.when(place_ref[0] != 0)
    def _():
        pick(1, own_ref)
        pick(0, sent_ref)


def project_kernel(place_ref, own_ref, other_ref, weight_ref, kept_ref, sent_ref):
    rows = jnp.concatenate([own_ref[...], other_ref[...]], axis=0)
    both = jnp.dot(rows, weight_ref[...], preferred_element_type=F32)
    n, half = both.shape[0] // 4, both.shape[1] // 2
    first = place_ref[0] == 0
    for owner in range(2):
        a = both[2 * owner * n : (2 * owner + 1) * n, :]
        b = both[(2 * owner + 1) * n : (2 * owner + 2) * n, :]
        low = jnp.concatenate([a[:, :half], b[:, :half]], axis=1)
        high = jnp.concatenate([a[:, half:], b[:, half:]], axis=1)
        kept_ref[owner * n : (owner + 1) * n, :] = jnp.where(first, low, high)
        sent_ref[owner * n : (owner + 1) * n, :] = jnp.where(first, high, low)


def half_grad(odd, one_ref, other_ref, grad_ref, store):
    rows, half = one_ref.shape[1], grad_ref.shape[1] // 2

    def product(a_ref, b_ref):
        return jnp.dot(a_ref[...], grad_ref[:rows, :half], preferred_element_type=F32) + jnp.dot(
            b_ref[...], grad_ref[:rows, half:], preferred_element_type=F32
        )

    @pl.when(odd == 0)
    def _():
        store(product(one_ref, other_ref))

    @pl.when(odd != 0)
    def _():
        store(product(other_ref, one_ref))


def own_half_kernel(place_ref, one_ref, other_ref, grad_ref, out_ref):
    def store(value):
        out_ref[...] = value

    half_grad(place_ref[1], one_ref, other_ref, grad_ref, store)


def other_half_kernel(off_factor, place_ref, one_ref, other_ref, grad_ref, mine_ref, off_ref, diag_ref, out_ref, loss_ref):
    first = place_ref[0] == 0
    rows, terms = one_ref.shape[1], diag_ref.shape[1]
    other_diag = jnp.sum(grad_ref[rows:, :terms].astype(F32), axis=0, keepdims=True)
    loss_ref[0] = jnp.sum(off_factor * off_ref[...] + diag_ref[...] + other_diag) / D_OUT
    half = mine_ref.shape[1]

    def store(value):
        mine = mine_ref[...]
        out_ref[:, :half] = jnp.where(first, mine, value)
        out_ref[:, half:] = jnp.where(first, value, mine)

    half_grad(place_ref[1], one_ref, other_ref, grad_ref, store)


def body(embeds, weight):
    n_chip = lax.axis_size(PLANE)
    n_near, n_far = lax.axis_size("z0"), lax.axis_size("z1")
    n_feat = n_near * n_far
    n_batch = 2 * n_chip
    local_rows, _, d_in = embeds.shape
    chip_rows = 2 * local_rows
    n_rows = local_rows * n_batch
    depth, width_out = weight.shape
    half = width_out // 2
    core = lax.axis_index("core")
    chip = lax.axis_index(PLANE)
    first = core == 0

    def in_core_order(own, other, axis):
        return jnp.concatenate([jnp.where(first, own, other), jnp.where(first, other, own)], axis=axis)

    def swap_core(a):
        return lax.ppermute(a, "core", [(0, 1), (1, 0)])

    near = lax.axis_index("z0")
    odd = near // 2
    place = jnp.stack([core, odd, near]).astype(jnp.int32)
    vmem = pl.BlockSpec(memory_space=pltpu.VMEM)
    smem = pl.BlockSpec(memory_space=pltpu.SMEM)
    params = pltpu.CompilerParams(vmem_limit_bytes=32 * 1024 * 1024)

    with jax.named_scope("embeds_exchange"):
        by_view = lax.optimization_barrier(embeds.transpose(1, 0, 2).reshape(2 * local_rows, d_in))
    with jax.named_scope("embeds_order"):
        own_rows, sent_rows, one_view = pl.pallas_call(
            order_kernel,
            out_shape=[jax.ShapeDtypeStruct((2 * local_rows, n_chip * depth), BF16)] * 2
            + [jax.ShapeDtypeStruct((n_batch, local_rows // 2, depth), BF16)],
            in_specs=[smem, vmem],
            out_specs=[vmem] * 3,
            compiler_params=params,
            name="order",
        )(place, by_view)
    with jax.named_scope("weight_gather"):
        first_groups, second_groups = ring_groups()
        row_weight = ring_gather(weight, first_groups)
        row_weight, one_view, own_rows, sent_rows = lax.optimization_barrier((row_weight, one_view, own_rows, sent_rows))
        core_weight = ring_gather(row_weight, second_groups).reshape(n_chip * depth, width_out)
        core_weight, one_view, sent_rows = lax.optimization_barrier((core_weight, one_view, sent_rows))
        one_view = exchange(one_view, BATCH)
        other_rows = swap_core(sent_rows)
    with jax.named_scope("project"):
        kept, sent = pl.pallas_call(
            project_kernel,
            out_shape=[jax.ShapeDtypeStruct((2 * local_rows, width_out), F32)] * 2,
            in_specs=[smem] + [vmem] * 3,
            out_specs=[vmem, vmem],
            compiler_params=params,
            name="project",
        )(place, own_rows, other_rows, core_weight)
        got_other, got_own = jnp.split(swap_core(sent), 2)
        own, other = jnp.split(kept, 2)
        projected = in_core_order(own + got_own, other + got_other, 0)
    with jax.named_scope("project_gather"):
        chip_mean = jnp.sum(projected, axis=0) / chip_rows
        projected, chip_mean, one_view = lax.optimization_barrier((projected, chip_mean, one_view))
        block = with_rows((projected - chip_mean).astype(BF16), pieces(chip_mean))
        block, one_view = lax.optimization_barrier((block, one_view))
        half_got = lax.ppermute(one_view, "z0", [(0, 1), (1, 0), (2, 3), (3, 2)])
        even = near % 2 == 0
        low, high = jnp.where(even, one_view, half_got), jnp.where(even, half_got, one_view)
        one_t = jnp.concatenate([low, high], axis=1).reshape(n_rows, depth).T
        pairs = [(z, (z + 1) % n_feat) for z in range(1, n_feat, 2)]
        other_t = lax.ppermute(one_t, FEAT, pairs + [(b, a) for a, b in pairs])
        got = gather(block, PLANE)
    with jax.named_scope("standardize"):
        chip_means = jnp.sum(got[:, chip_rows : chip_rows + 3].astype(F32), axis=1)
        row_mean = jnp.sum(chip_means, axis=0) / n_chip
        shift = chip_means - row_mean
        centered = got[:, :chip_rows].astype(F32) + shift[:, None, :]
        centered = centered.reshape(n_rows, width_out)
        variance = jnp.sum(centered * centered, axis=0) / n_rows
        spread = jnp.sqrt(variance + epsilon)
        inverse = 1.0 / spread
        normed = (centered * inverse).astype(BF16)
        view_a, view_b = normed[:, :half], normed[:, half:]
        float_a, float_b = view_a.astype(F32), view_b.astype(F32)
        diagonal = jnp.sum(float_a * float_b, axis=0) / n_rows
        diag_terms = (1.0 - diagonal) ** 2 - off_weight * diagonal * diagonal
        diag_local = diag_terms[:chip_rows] + diag_terms[chip_rows:]

    with jax.named_scope("gram"):
        def partial(view):
            mine = lax.dynamic_slice_in_dim(view, chip * chip_rows, chip_rows, axis=0)
            return lax.dot_general(view, mine, (((1,), (1,)), ((), ())), preferred_element_type=F32)

        sent = partial(jnp.where(first, view_b, view_a)).astype(BF16)
        kept = partial(jnp.where(first, view_a, view_b))
        weight_diag = 2.0 * ((1.0 - off_weight) * diagonal - 1.0)
        factor = loss_scale / n_rows * jnp.concatenate([weight_diag, weight_diag])
        sent, one_t, other_t = lax.optimization_barrier((sent, one_t, other_t))
    with jax.named_scope("gram_core"):
        extra = pad_rows(pieces(diag_local), chip_rows)
        parts = kept + swap_core(sent).astype(F32)
        parts, extra, factor, inverse = lax.optimization_barrier((parts.astype(BF16), extra, factor, inverse))
    with jax.named_scope("gram_reduce"):
        parts = parts.astype(BF16).reshape(n_near, n_rows // n_near, chip_rows)
        extra = jnp.broadcast_to(extra[None], (n_near, PAD, chip_rows))
        got_z = exchange(jnp.concatenate([parts, extra], axis=1), "z0")
        summed = jnp.sum(got_z.astype(F32), axis=0)
        extra = pad_rows(pieces(jnp.sum(summed[n_rows // n_near :], axis=0)), chip_rows)
        parts = summed[: n_rows // n_near].astype(BF16).reshape(n_far, n_rows // n_feat, chip_rows)
        extra = jnp.broadcast_to(extra[None], (n_far, PAD, chip_rows))
        got_z = exchange(jnp.concatenate([parts, extra], axis=1), "z1")
        summed = jnp.sum(got_z.astype(F32), axis=0)
        gram_block = summed[: n_rows // n_feat].astype(BF16)
        diag_terms = jnp.sum(summed[n_rows // n_feat :], axis=0)
        gram_block, diag_terms = lax.optimization_barrier((gram_block, diag_terms))
    with jax.named_scope("gram_gather"):
        gram_t = gather(gather(gram_block, "z1"), "z0").reshape(n_rows, chip_rows)
        other_gram = swap_core(gram_t)
    with jax.named_scope("back"):
        own_gram, other_gram = gram_t.astype(F32), other_gram.astype(F32)
        with_own = split_product(own_gram, jnp.where(first, view_b, view_a))
        with_other = split_product(other_gram, jnp.where(first, view_a, view_b))
        off_local = jnp.sum(own_gram * other_gram, axis=0)
        back = in_core_order(with_other, with_own, 1).astype(BF16)
        terms = jnp.concatenate([off_local, jnp.zeros((width_out - chip_rows,), F32)])
        block = with_rows(back, pieces(terms))
    with jax.named_scope("back_gather"):
        got_back = gather(block, PLANE)
    with jax.named_scope("grad"):
        scale_off = 2.0 * off_weight / (n_rows * n_rows)
        off_terms = jnp.sum(got_back[:, chip_rows:, :chip_rows].astype(F32), axis=(0, 1))[None]
        grad_proj = pl.pallas_call(
            functools.partial(grad_kernel, n_rows, chip_rows, loss_scale * scale_off),
            out_shape=jax.ShapeDtypeStruct((n_rows + 16, width_out), BF16),
            in_specs=[vmem] * 6,
            out_specs=vmem,
            scratch_shapes=[pltpu.VMEM((n_rows, width_out), F32)] * 2,
            compiler_params=params,
            cost_estimate=pl.CostEstimate(flops=20 * n_rows * width_out, bytes_accessed=8 * n_rows * width_out, transcendentals=0),
            name="grad",
        )(got_back, got, shift, inverse[None], factor[None], diag_terms[None])
    with jax.named_scope("grad_swap"):
        other_proj = swap_core(grad_proj)
    with jax.named_scope("weight_grad"):
        mine = pl.pallas_call(
            own_half_kernel,
            out_shape=jax.ShapeDtypeStruct((depth, half), F32),
            in_specs=[smem] + [vmem] * 3,
            out_specs=vmem,
            compiler_params=params,
            name="own_half",
        )(place, one_t, other_t, grad_proj)
        grad_weight, loss = pl.pallas_call(
            functools.partial(other_half_kernel, off_weight / (n_rows * n_rows)),
            out_shape=[jax.ShapeDtypeStruct((depth, width_out), F32), jax.ShapeDtypeStruct((1,), F32)],
            in_specs=[smem] + [vmem] * 6,
            out_specs=[vmem, smem],
            compiler_params=params,
            name="other_half",
        )(place, one_t, other_t, other_proj, mine, off_terms, diag_terms[None])
    return (loss[0], grad_weight)


def solution(mesh):
    n_batch, n_feat = mesh.devices.shape
    grid = Mesh(mesh.devices.reshape(4, n_batch // 8, 2, n_feat // 4, 4), BATCH + FEAT)
    return jax.shard_map(
        body,
        mesh=grid,
        in_specs=(P(BATCH, None, None), P(BATCH, FEAT)),
        out_specs=(P(), P(BATCH, FEAT)),
        check_vma=False,
    )
```
